256 devices in a mesh: lat: 8 (over z), lon: 8 (over x_hi, y), mp: 4 (over x_lo, core).
Axes of the slice: x: 4 (x_hi: 2, x_lo: 2; x = x_hi * 2 + x_lo), y: 4, z: 8, core: 2. Of those that a mesh axis runs over, the one named last changes fastest.
Arguments:
- tokens: bfloat16 [4, 48, 96, 1024], P(None, 'lat', 'lon'), may hold values from -6 to 6
- qkv_first: bfloat16 [1024, 3, 1024], P(None, None, 'mp'), may hold values from -5 to 5
- qkv_second: bfloat16 [1024, 3, 1024], P(None, None, 'mp'), may hold values from -5 to 5
- out_first: bfloat16 [1024, 1024], P('mp'), may hold values from -0.1875 to 0.1875
- out_second: bfloat16 [1024, 1024], P('mp'), may hold values from -0.1875 to 0.1875
- rel_tables: float32 [2, 16, 37], P(None, 'mp'), may hold values from -4 to 4
- up_weight: bfloat16 [1024, 4096], P(None, 'mp'), may hold values from -0.1875 to 0.1875
- down_weight: bfloat16 [4096, 1024], P('mp'), may hold values from -0.09375 to 0.09375
Outputs:
- blocks_out: bfloat16 [4, 48, 96, 1024], P(None, 'lat', 'lon')
The draws below stay inside these ranges and needn't reach their ends.
All inputs are finite; a program needn't handle non-finite values.
Results may differ from the reference program's by a relative error of at most 0.024.
Values may be sent and summed in bfloat16 or wider, within the bound.
No kernel may reach another device: no remote copies, remote signals or barrier semaphores. Data moves between devices by JAX's collectives and lax.ppermute only.
A program may use at most 64 MiB of HBM per device.

```python
import jax
import jax.numpy as jnp
from jax import lax

D = 1024
HEADS = 16
FF = 4096
LEV = 4
WL = 2
WY = 6
WX = 12
SL = 1
SY = 3
SX = 6
RELS = 37
NLAT = 48
NLON = 96


def draw_qkv_first(key, part):
    key = jax.random.fold_in(key, 11)
    base_key = jax.random.fold_in(key, 0)
    base = jnp.clip(jax.random.normal(base_key, (D, 3, D), jnp.float32), -4.0, 4.0) * D ** (-0.5)
    return base.astype(jnp.bfloat16)


def draw_qkv_second(key, part):
    key = jax.random.fold_in(key, 23)
    base_key = jax.random.fold_in(key, 0)
    base = jnp.clip(jax.random.normal(base_key, (D, 3, D), jnp.float32), -4.0, 4.0) * D ** (-0.5)
    return base.astype(jnp.bfloat16)


def level_of(stream_key, dims, cuts, least, high):
    gain = 1.0
    for position, parts in cuts:
        draws = jax.random.uniform(jax.random.fold_in(jax.random.fold_in(stream_key, 6), position), (parts,), jnp.float32, least / len(cuts), high / len(cuts))
        gain = gain * jnp.repeat(jnp.exp(draws), dims[position] // parts).reshape((-1,) + (1,) * (len(dims) - 1 - position))
    return gain


def noise(rng, shape, deviation, bound, cuts=(), held_as=jnp.bfloat16):
    gain = level_of(rng, shape, cuts, -0.22, 0.18) if cuts else 1.0
    values = jax.random.normal(rng, shape, jnp.float32) * deviation * gain
    return jnp.minimum(jnp.maximum(values, -bound), bound).astype(held_as)


def setup_inputs(seed: int = 0) -> dict:
    arg_keys = jax.random.split(jax.random.key(seed), 9)
    return {
        "tokens": noise(arg_keys[0], (LEV, NLAT, NLON, D), 1.0, 6.0, ((1, 8), (2, 8))),
        "qkv_first": draw_qkv_first(jax.random.fold_in(arg_keys[8], 71), 0),
        "qkv_second": draw_qkv_second(jax.random.fold_in(arg_keys[8], 71), 0),
        "out_first": noise(arg_keys[3], (D, D), D ** -0.5, 0.1875, ((0, 4),)),
        "out_second": noise(arg_keys[4], (D, D), D ** -0.5, 0.1875, ((0, 4),)),
        "rel_tables": noise(arg_keys[5], (2, HEADS, RELS), 1.0, 4.0, ((1, 4),), jnp.float32),
        "up_weight": noise(arg_keys[6], (D, FF), D ** -0.5, 0.1875, ((1, 4),)),
        "down_weight": noise(arg_keys[7], (FF, D), FF ** -0.5, 0.09375, ((0, 4),)),
    }


NEG = -1000000000.0
HIGH = lax.Precision.HIGHEST

def normalize(values):
    floats = values.astype(jnp.float32)
    center = floats - lax.optimization_barrier(jnp.mean(floats, axis=-1, keepdims=True))
    spread = lax.optimization_barrier(jnp.mean(center * center, axis=-1, keepdims=True))
    return (center * lax.rsqrt(spread + 1e-05)).astype(jnp.bfloat16)

def to_windows(values):
    levels, rows, cols, width = values.shape
    blocks = values.reshape(levels // WL, WL, rows // WY, WY, cols // WX, WX, width)
    return blocks.transpose(0, 2, 4, 1, 3, 5, 6).reshape(-1, WL * WY * WX, width)

def from_windows(windows, levels, rows, cols):
    width = windows.shape[-1]
    blocks = windows.reshape(levels // WL, rows // WY, cols // WX, WL, WY, WX, width)
    return blocks.transpose(0, 3, 1, 4, 2, 5, 6).reshape(levels, rows, cols, width)

def bias_matrix(table):
    index = jnp.arange(WL * WY * WX)
    level = index // (WY * WX)
    row_pos = index // WX % WY
    col_pos = index % WX
    offset = 0
    result = jnp.zeros((table.shape[0], WL * WY * WX, WL * WY * WX), jnp.float32)
    for coord, extent in ((level, WL), (row_pos, WY), (col_pos, WX)):
        span = 2 * extent - 1
        delta = coord[:, None] - coord[None, :] + extent - 1
        onehot = (delta[:, :, None] == jnp.arange(span)[None, None, :]).astype(jnp.float32)
        result = result + jnp.einsum('hk,ijk->hij', table[:, offset:offset + span], onehot, precision=HIGH)
        offset += span
    return result

def attend(packed, table, allowed):
    count, size, triple = packed.shape
    heads = table.shape[0]
    width = triple // 3
    split = packed.reshape(count, size, 3, heads, width // heads).astype(jnp.float32)
    query, key_part, value = (split[:, :, 0], split[:, :, 1], split[:, :, 2])
    scores = jnp.einsum('wihd,wjhd->whij', query, key_part)
    scores = scores * (width // heads) ** (-0.5) + bias_matrix(table)[None]
    if allowed is not None:
        scores = jnp.where(allowed[:, None], scores, NEG)
    peak = lax.optimization_barrier(jnp.max(scores, axis=-1, keepdims=True))
    expo = jnp.exp(scores - peak)
    probs = (expo / lax.optimization_barrier(jnp.sum(expo, axis=-1, keepdims=True))).astype(jnp.bfloat16)
    mixed = jnp.einsum('whij,wjhd->wihd', probs.astype(jnp.float32), value)
    return mixed.astype(jnp.bfloat16).reshape(count, size, width)

def region_allowed(levels, rows, cols, row_start, total_rows):
    lev_coord = jnp.arange(levels)
    row_coord = row_start + jnp.arange(rows)
    lev_region = (lev_coord >= levels - WL).astype(jnp.int32) + (lev_coord >= levels - SL).astype(jnp.int32)
    row_region = (row_coord >= total_rows - WY).astype(jnp.int32) + (row_coord >= total_rows - SY).astype(jnp.int32)
    ident = lev_region[:, None] * 3 + row_region[None, :]
    ident = jnp.broadcast_to(ident[:, :, None, None], (levels, rows, cols, 1))
    flat = to_windows(ident)[:, :, 0]
    return flat[:, :, None] == flat[:, None, :]

def attention(normed, weight, table, allowed):
    levels, rows, cols, width = normed.shape
    packed = jnp.dot(normed.reshape(-1, width), weight.reshape(width, -1), preferred_element_type=jnp.float32)
    packed = packed.astype(jnp.bfloat16).reshape(levels, rows, cols, -1)
    mixed = attend(to_windows(packed), table, allowed)
    return from_windows(mixed, levels, rows, cols)

def reference(tokens, qkv_first, qkv_second, out_first, out_second, rel_tables, up_weight, down_weight):
    levels, rows, cols, width = tokens.shape
    mixed = attention(normalize(tokens), qkv_first, rel_tables[0], None)
    branch = jnp.dot(mixed.reshape(-1, width), out_first, preferred_element_type=jnp.float32).astype(jnp.bfloat16)
    first = (tokens.reshape(-1, width).astype(jnp.float32) + branch.astype(jnp.float32)).astype(jnp.bfloat16)
    first = first.reshape(levels, rows, cols, width)
    rolled = jnp.roll(normalize(first), (-SL, -SY, -SX), (0, 1, 2))
    allowed = region_allowed(levels, rows, cols, 0, rows)
    mixed = attention(rolled, qkv_second, rel_tables[1], allowed)
    branch = jnp.dot(mixed.reshape(-1, width), out_second, preferred_element_type=jnp.float32).astype(jnp.bfloat16)
    branch = jnp.roll(branch.reshape(levels, rows, cols, width), (SL, SY, SX), (0, 1, 2))
    second = (first.astype(jnp.float32) + branch.astype(jnp.float32)).astype(jnp.bfloat16)
    flat = second.reshape(-1, width)
    hidden = jax.nn.gelu(jnp.dot(normalize(flat), up_weight, preferred_element_type=jnp.float32), approximate=False)
    hidden = hidden.astype(jnp.bfloat16)
    branch = jnp.dot(hidden, down_weight, preferred_element_type=jnp.float32).astype(jnp.bfloat16)
    result = (flat.astype(jnp.float32) + branch.astype(jnp.float32)).astype(jnp.bfloat16)
    return result.reshape(levels, rows, cols, width)
```

```python
import functools

import jax
import jax.numpy as jnp
import numpy as np
from jax import lax
from jax.experimental import pallas as pl
from jax.experimental.pallas import tpu as pltpu
from jax.sharding import PartitionSpec as P

WL = 2
WY = 6
WX = 12
SY = 3
SX = 6
HD = 64
NEG = -1000000000.0
AXES = ("lat", "lon", "mp")
MIB = 1024 * 1024

USED = 36
ROWS = 40
KEPT = 4 * ROWS
FEAT = 32
F_Y = 4
F_X = 10
F_PAD = 22


def quadrant_start(q):
    return (3, 0, 3, 0)[q], (6, 6, 0, 0)[q]


def build_constants():
    tokens = 4 * WY * WX
    select = np.zeros((2, KEPT, tokens), np.float32)
    for core in range(2):
        levels = (1, 2) if core == 0 else (3, 0)
        for q in range(4):
            y0, x0 = quadrant_start(q)
            row = q * ROWS
            for level in levels:
                for y in range(3):
                    for x in range(6):
                        select[core, row, (level * WY + y0 + y) * WX + x0 + x] = 1.0
                        row += 1
    flat = np.zeros((tokens, FEAT), np.float32)
    for t in range(tokens):
        flat[t, t // (WY * WX)] = 1.0
        flat[t, F_Y + t // WX % WY] = 1.0
        flat[t, F_X + t % WX] = 1.0
    rolled = np.zeros((KEPT, FEAT), np.float32)
    level_ban = np.zeros((KEPT, 128), np.float32)
    row_ban = np.zeros((KEPT, 128), np.float32)
    for q in range(4):
        for s in range(ROWS):
            i = q * ROWS + s
            if s >= USED:
                rolled[i, F_PAD] = 1.0
                continue
            level, y, x = s // 18, s // 6 % 3 + 3 * (q % 2), s % 6 + 6 * (q // 2)
            rolled[i, level] = 1.0
            rolled[i, F_Y + y] = 1.0
            rolled[i, F_X + x] = 1.0
            for half in (0, 64):
                level_ban[i, half + 1 - level] = NEG
                for other in range(WY):
                    if (other < 3) != (y < 3):
                        row_ban[i, half + F_Y + other] = NEG
    index = np.full((2, FEAT, FEAT), 37, np.int64)
    for block in range(2):
        for i in range(4):
            for j in range(4):
                near = i // 2 == j // 2
                index[block, i, j] = i - j + 1 if near else 38
            index[block, i, F_PAD] = 38
        for i in range(WY):
            for j in range(WY):
                index[block, F_Y + i, F_Y + j] = 3 + i - j + 5
        for i in range(WX):
            for j in range(WX):
                index[block, F_X + i, F_X + j] = 14 + i - j + 11
    pick = (index.reshape(2, 1, -1) == np.arange(39).reshape(1, 39, 1)).astype(np.float32)
    return {
        "select": select.astype(jnp.bfloat16),
        "place": select.transpose(0, 2, 1).astype(jnp.bfloat16),
        "flat": np.tile(flat, (1, 4)).astype(jnp.bfloat16),
        "rolled": np.tile(rolled, (1, 4)).astype(jnp.bfloat16),
        "level_ban": level_ban,
        "row_ban": row_ban,
        "pick": pick,
    }


def pairs(counts, target):
    lats, lons, mps = counts
    result = []
    for a in range(lats):
        for b in range(lons):
            for m in range(mps):
                ta, tb, tm = target(a, b, m)
                dest = ((ta % lats) * lons + tb % lons) * mps + tm
                result.append(((a * lons + b) * mps + m, dest))
    return result


def dot(left, right):
    return jnp.dot(left, right, preferred_element_type=jnp.float32)


def dot_t(left, right):
    return lax.dot_general(left, right, (((1,), (1,)), ((), ())), preferred_element_type=jnp.float32)


def normalize(floats):
    center = floats - jnp.mean(floats, axis=-1, keepdims=True)
    spread = jnp.mean(center * center, axis=-1, keepdims=True)
    return (center * lax.rsqrt(spread + 1e-05)).astype(jnp.bfloat16)


def four_heads(xq, xk, weight, extra, key_feat):
    query = (dot(xq, weight[:, :256]) * HD**-0.5).astype(jnp.bfloat16)
    rest = dot(xk, weight[:, 256:]).astype(jnp.bfloat16)
    results = []
    for pair in range(2):
        cols = slice(pair * 128, pair * 128 + 128)
        q, k, v = query[:, cols], rest[:, cols], rest[:, 256 + pair * 128 : 384 + pair * 128]
        e = extra[:, cols]
        low_q = lax.broadcasted_iota(jnp.int32, q.shape, 1) < HD
        low_k = lax.broadcasted_iota(jnp.int32, k.shape, 1) < HD
        outs = []
        for head in range(2):
            mine_q, mine_k = (low_q, low_k) if head == 0 else (~low_q, ~low_k)
            scores = dot_t(jnp.where(mine_q, q, e), jnp.where(mine_k, k, key_feat))
            expo = jnp.exp(scores - jnp.max(scores, axis=-1, keepdims=True))
            probs = (expo / jnp.sum(expo, axis=-1, keepdims=True)).astype(jnp.bfloat16)
            outs.append(dot(probs, v))
        results.append(jnp.where(low_q, outs[0], outs[1]).astype(jnp.bfloat16))
    return results


def core_index():
    return lax.rem(lax.axis_index("mp"), 2)


def first_kernel(tokens, weight, bias, select, flat, *refs):
    out = refs[-1]
    pick = select[core_index()]
    xk = normalize(tokens[...].astype(jnp.float32))
    xq = dot(pick, xk).astype(jnp.bfloat16)
    feat = dot(pick, flat[...]).astype(jnp.bfloat16)
    extra = dot(feat[:, :FEAT], bias[...]).astype(jnp.bfloat16)
    heads = four_heads(xq, xk, weight[...], extra, flat[...])
    start = 0
    if len(refs) == 2:
        out[:, :256] = refs[0][...]
        start = 256
    out[:, start : start + 128] = heads[0]
    out[:, start + 128 : start + 256] = heads[1]


def projected(mine, other, w0, w1, w2, w3):
    total = dot(mine[:, :256], w0[...]) + dot(mine[:, 256:], w1[...])
    total = total + dot(other[:, :256], w2[...]) + dot(other[:, 256:], w3[...])
    return total.astype(jnp.bfloat16).astype(jnp.float32)


def residual_kernel(mine, other, w0, w1, w2, w3, tokens, select, *outs):
    base = dot(select[core_index()], tokens[...])
    first = base + projected(mine, other, w0, w1, w2, w3)
    for q in range(4):
        outs[q][...] = first[q * ROWS : (q + 1) * ROWS].astype(jnp.bfloat16)


def joined(pieces):
    return jnp.concatenate([p[...].astype(jnp.float32) for p in pieces], axis=0)


def second_kernel(p0, p1, p2, p3, w_own, w_sib, b_own, b_sib, rolled, level_ban, row_ban, out):
    xn = normalize(joined((p0, p1, p2, p3)))
    ban_levels = (core_index() == 1).astype(jnp.float32)
    ban_rows = (lax.axis_index("lat") == lax.axis_size("lat") - 1).astype(jnp.float32)
    ban = level_ban[...] * ban_levels + row_ban[...] * ban_rows
    ban = jnp.concatenate([ban, ban], axis=1)
    key_feat = rolled[...]
    for part, (weight, bias) in enumerate(((w_own, b_own), (w_sib, b_sib))):
        extra = (dot(key_feat[:, :FEAT], bias[...]) + ban).astype(jnp.bfloat16)
        heads = four_heads(xn, xn, weight[...], extra, key_feat)
        out[:, part * 256 : part * 256 + 128] = heads[0]
        out[:, part * 256 + 128 : part * 256 + 256] = heads[1]


def gelu(x):
    return 0.5 * x * (1.0 + lax.erf(x * np.float32(np.sqrt(0.5))))


def mlp_kernel(mine, other, w0, w1, w2, w3, p0, p1, p2, p3, u0, u1, d0, d1, *outs):
    second = joined((p0, p1, p2, p3)) + projected(mine, other, w0, w1, w2, w3)
    second = second.astype(jnp.bfloat16).astype(jnp.float32)
    xn = normalize(second)
    h0 = gelu(dot(xn, u0[...])).astype(jnp.bfloat16)
    h1 = gelu(dot(xn, u1[...])).astype(jnp.bfloat16)
    total = 0.5 * second + dot(h0, d0[...]) + dot(h1, d1[...])
    for q in range(4):
        outs[q][...] = total[q * ROWS : (q + 1) * ROWS].astype(jnp.bfloat16)


def sum_kernel(*refs):
    out = refs[-1]
    parts = []
    for q in range(4):
        parts.append(refs[2 * q][...].astype(jnp.float32) + refs[2 * q + 1][...].astype(jnp.float32))
    out[...] = jnp.concatenate(parts, axis=0).astype(jnp.bfloat16)


def place_kernel(mine, other, place, out):
    core = core_index()
    out[...] = (dot(place[core], mine[...]) + dot(place[1 - core], other[...])).astype(jnp.bfloat16)


def call(kernel, outs, operands, flops, limit):
    shapes = [jax.ShapeDtypeStruct(s, jnp.bfloat16) for s in outs]
    moved = sum(o.size * o.dtype.itemsize for o in operands) + sum(2 * s.size for s in shapes)
    vmem = pl.BlockSpec(memory_space=pltpu.VMEM)
    result = pl.pallas_call(
        kernel,
        out_shape=shapes,
        in_specs=[vmem] * len(operands),
        out_specs=[vmem] * len(shapes),
        compiler_params=pltpu.CompilerParams(vmem_limit_bytes=limit * MIB),
        cost_estimate=pl.CostEstimate(flops=flops, bytes_accessed=moved, transcendentals=0),
    )(*operands)
    return result if len(result) > 1 else result[0]


def bias_rows(tables, pick):
    heads = tables.shape[1]
    fill = jnp.broadcast_to(jnp.array([0.0, NEG], jnp.float32), (2, heads, 2))
    wide = jnp.concatenate([tables, fill], axis=2)
    rows = jnp.einsum("bhk,bkn->bhn", wide, pick, precision=lax.Precision.HIGHEST)
    high = lax.reduce_precision(rows, 8, 7)
    both = jnp.stack([high, rows - high], axis=2).astype(jnp.bfloat16)
    both = both.reshape(2, heads // 2, 2, 2, FEAT, FEAT)[:, :, ::-1]
    return both.transpose(0, 4, 1, 2, 3, 5).reshape(2, FEAT, heads * 2 * FEAT)


def body(counts, tokens, qkv_first, qkv_second, out_first, out_second, rel_tables, up_weight, down_weight):
    levels, rows, cols, width = tokens.shape
    count = levels * rows * cols
    consts = {name: jnp.asarray(value) for name, value in build_constants().items()}
    select, place = consts["select"], consts["place"]

    def move(value, target):
        return lax.ppermute(value, AXES, pairs(counts, target))

    def core_swap(value):
        return move(value, lambda a, b, m: (a, b, m ^ 1))

    def chip_swap(value):
        return move(value, lambda a, b, m: (a, b, m ^ 2))

    offsets = ((0, 0), (1, 0), (0, 1), (1, 1))
    turn = counts[1] // 2

    flat_tokens = tokens.reshape(count, width)
    wide_first = qkv_first.reshape(width, -1)
    wide_second = qkv_second.reshape(width, -1)

    of2 = chip_swap(out_first)
    of1 = core_swap(out_first)
    sib_first = core_swap(wide_first)
    bias = bias_rows(rel_tables, consts["pick"])
    sib_bias = core_swap(bias)

    part = call(
        first_kernel, [(KEPT, 256)], (flat_tokens, wide_first, bias[0], select, consts["flat"]), 10**9, 24
    )
    mixed = call(
        first_kernel,
        [(KEPT, 512)],
        (flat_tokens, sib_first, sib_bias[0], select, consts["flat"], part),
        10**9,
        24,
    )
    of3 = core_swap(of2)
    other = chip_swap(mixed)
    sib_second = core_swap(wide_second)
    os2 = chip_swap(out_second)
    os1 = core_swap(out_second)
    os3 = core_swap(os2)
    sib_up = core_swap(up_weight)
    sib_down = core_swap(down_weight)

    firsts = call(
        residual_kernel,
        [(ROWS, width)] * 4,
        (mixed, other, out_first, of1, of2, of3, flat_tokens, select),
        5 * 10**8,
        24,
    )
    shifted = [firsts[0]]
    for q in (1, 2, 3):
        dy, dx = offsets[q]

        def target(a, b, m, dy=dy, dx=dx):
            return a - dy, b - dx, m ^ 2 if dx and b % turn == 0 else m

        shifted.append(move(firsts[q], target))

    mixed = call(
        second_kernel,
        [(KEPT, 512)],
        (
            *shifted,
            wide_second,
            sib_second,
            bias[1],
            sib_bias[1],
            consts["rolled"],
            consts["level_ban"],
            consts["row_ban"],
        ),
        10**9,
        24,
    )
    other = chip_swap(mixed)
    partial = call(
        mlp_kernel,
        [(ROWS, width)] * 4,
        (mixed, other, out_second, os1, os2, os3, *shifted, up_weight, sib_up, down_weight, sib_down),
        2 * 10**9,
        40,
    )
    terms = []
    for q in (3, 2, 1, 0):
        dy, dx = offsets[q]
        far = move(partial[q], lambda a, b, m, dy=dy, dx=dx: (a + dy, b + dx, m ^ 2))
        near = move(partial[q], lambda a, b, m, dy=dy, dx=dx: (a + dy, b + dx, m)) if q else partial[q]
        terms = [near, far] + terms
    done = call(sum_kernel, [(KEPT, width)], terms, 10**6, 16)
    result = call(place_kernel, [(count, width)], (done, core_swap(done), place), 2 * 10**8, 16)
    return result.reshape(levels, rows, cols, width)


def solution(mesh):
    counts = tuple(mesh.shape[name] for name in AXES)
    return jax.shard_map(
        functools.partial(body, counts),
        mesh=mesh,
        in_specs=(
            P(None, "lat", "lon", None),
            P(None, None, "mp"),
            P(None, None, "mp"),
            P("mp", None),
            P("mp", None),
            P(None, "mp", None),
            P(None, "mp"),
            P("mp", None),
        ),
        out_specs=P(None, "lat", "lon", None),
        check_vma=False,
    )
```

```python
import functools

import jax
import jax.numpy as jnp
import numpy as np
from jax import lax
from jax.experimental import pallas as pl
from jax.experimental.pallas import tpu as pltpu
from jax.sharding import PartitionSpec as P

WL = 2
WY = 6
WX = 12
SY = 3
SX = 6
HD = 64
NEG = -1000000000.0
AXES = ("lat", "lon", "mp")
MIB = 1024 * 1024

USED = 36
ROWS = 40
KEPT = 4 * ROWS
PATCH = 4 * WY * WX
WINDOW = WL * WY * WX
FEAT = 32
F_Y = 4
F_X = 10
F_PAD = 22


def pairs(counts, target):
    lats, lons, mps = counts
    result = []
    for a in range(lats):
        for b in range(lons):
            for m in range(mps):
                ta, tb, tm = target(a, b, m)
                dest = ((ta % lats) * lons + tb % lons) * mps + tm
                result.append(((a * lons + b) * mps + m, dest))
    return result


def dot(left, right):
    return jnp.dot(left, right, preferred_element_type=jnp.float32)


def dot_t(left, right):
    return lax.dot_general(left, right, (((1,), (1,)), ((), ())), preferred_element_type=jnp.float32)


def normalize(floats):
    center = floats - jnp.mean(floats, axis=-1, keepdims=True)
    spread = jnp.mean(center * center, axis=-1, keepdims=True)
    return (center * lax.rsqrt(spread + 1e-05)).astype(jnp.bfloat16)


def core_index():
    return lax.rem(lax.axis_index("mp"), 2)


def iota(shape, axis):
    return lax.broadcasted_iota(jnp.int32, shape, axis)


def one_hot(condition):
    return jnp.where(condition, 1.0, 0.0).astype(jnp.bfloat16)


def piece_place(slot):
    level = (slot * 57) >> 10
    rest = slot - level * 18
    row = (rest * 43) >> 8
    return level, row, rest - row * 6


def kept_place(index):
    q = (index * 205) >> 13
    return (q, index - q * ROWS) + piece_place(index - q * ROWS)


def real_level(level, core):
    return jnp.where(core == 0, 1 + level, 3 - 3 * level)


def patch_place(q, row, col):
    return row + 3 - 3 * (q & 1), col + 6 - 3 * (q & 2)


def bias_rows(table, block, pair):
    shape = (FEAT, 4 * FEAT)
    i, lane = iota(shape, 0), iota(shape, 1)
    j = lane & (FEAT - 1)
    kind = jnp.full(shape, 37, jnp.int32)
    kind = jnp.where((i < WL) & (j < WL), i - j + 1, kind)
    kind = jnp.where((i < WL) & (j == F_PAD), 38, kind)
    in_y = (i >= F_Y) & (i < F_Y + WY) & (j >= F_Y) & (j < F_Y + WY)
    kind = jnp.where(in_y, 3 + i - j + 5, kind)
    in_x = (i >= F_X) & (i < F_X + WX) & (j >= F_X) & (j < F_X + WX)
    kind = jnp.where(in_x, 14 + i - j + 11, kind)
    total = jnp.where(kind == 38, NEG, 0.0)
    for k in range(37):
        value = jnp.where(lane < HD, table[block, 2 * pair + 1, k], table[block, 2 * pair, k])
        total = jnp.where(kind == k, value, total)
    high = total.astype(jnp.bfloat16).astype(jnp.float32)
    return jnp.where((lane & FEAT) != 0, total - high, high).astype(jnp.bfloat16)


def features(level, row, col, used, count):
    j = iota((count, 128), 1) & (FEAT - 1)
    hit = (j == level) | (j == F_Y + row) | (j == F_X + col)
    return one_hot(jnp.where(used, jnp.where(hit, 1, 0), jnp.where(j == F_PAD, 1, 0)) == 1)


def pair_heads(query, key, value, extra, key_feat):
    low_q = iota(query.shape, 1) < HD
    low_k = iota(key.shape, 1) < HD
    outs = []
    for head in range(2):
        mine_q, mine_k = (low_q, low_k) if head == 0 else (~low_q, ~low_k)
        scores = dot_t(jnp.where(mine_q, query, extra), jnp.where(mine_k, key, key_feat))
        expo = jnp.exp(scores - jnp.max(scores, axis=-1, keepdims=True))
        probs = (expo / jnp.sum(expo, axis=-1, keepdims=True)).astype(jnp.bfloat16)
        outs.append(dot(probs, value))
    return jnp.where(low_q, outs[0], outs[1]).astype(jnp.bfloat16)


def first_kernel(tokens, weight, table, keep, give, base):
    core = core_index()
    floats = tokens[...].astype(jnp.float32).reshape(PATCH, -1)
    xn = normalize(floats)
    q = (dot(xn, weight[0]) * HD**-0.5).astype(jnp.bfloat16)
    k = dot(xn, weight[1]).astype(jnp.bfloat16)
    v = dot(xn, weight[2]).astype(jnp.bfloat16)
    index = iota((PATCH, 1), 0)
    level = (index * 911) >> 16
    order = one_hot(iota((PATCH, PATCH), 1) == (index - 72 * level) * 4 + level)
    q, k, v = (dot(order, part).astype(jnp.bfloat16) for part in (q, k, v))
    index = iota((WINDOW, 1), 0)
    level = (index * 911) >> 16
    rest = index - 72 * level
    row = (rest * 171) >> 11
    feat = features(level, row, rest - 12 * row, index >= 0, WINDOW)
    parts = []
    for pair in range(2):
        cols = slice(pair * 128, pair * 128 + 128)
        extra = dot(feat[:, :FEAT], bias_rows(table, 0, pair)).astype(jnp.bfloat16)
        halves = []
        for w in range(2):
            rows = slice(w * WINDOW, (w + 1) * WINDOW)
            halves.append(pair_heads(q[rows, cols], k[rows, cols], v[rows, cols], extra, feat))
        parts.append(jnp.concatenate(halves, axis=0))
    mixed = jnp.concatenate(parts, axis=1)
    quad, slot, level, row, col = kept_place(iota((KEPT, 1), 0))
    row, col = patch_place(quad, row, col)
    lanes = iota((KEPT, PATCH), 1)
    for out, chosen in ((keep, core), (give, 1 - core)):
        place = real_level(level, chosen) * 72 + row * 12 + col
        place = jnp.where(slot < USED, place, -1)
        out[...] = dot(one_hot(lanes == place), mixed).astype(jnp.bfloat16)
    place = (row * 12 + col) * 4 + real_level(level, core)
    place = jnp.where(slot < USED, place, -1)
    base[...] = dot(one_hot(lanes == place), floats.astype(jnp.bfloat16)).astype(jnp.bfloat16)


def residual_kernel(o0, o1, o2, o3, w0, w1, w2a, w2b, w3a, w3b, base, *outs):
    total = dot(o0[...], w0[...]) + dot(o1[...], w1[...])
    total = total + dot(o2[:, :128], w2a[...]) + dot(o2[:, 128:], w2b[...])
    total = total + dot(o3[:, :128], w3a[...]) + dot(o3[:, 128:], w3b[...])
    first = base[...].astype(jnp.float32) + total.astype(jnp.bfloat16).astype(jnp.float32)
    for q in range(4):
        outs[q][...] = first[q * ROWS : (q + 1) * ROWS].astype(jnp.bfloat16)


def joined(pieces):
    return jnp.concatenate([p[...].astype(jnp.float32) for p in pieces], axis=0)


def second_kernel(p0, p1, p2, p3, w_own, w_sib, t_own, t_sib, out):
    xn = normalize(joined((p0, p1, p2, p3)))
    quad, slot, level, row, col = kept_place(iota((KEPT, 1), 0))
    row, col = row + 3 * (quad & 1), col + 3 * (quad & 2)
    feat = features(level, row, col, slot < USED, KEPT)
    lane = iota((KEPT, 128), 1)
    j = lane & (FEAT - 1)
    split_levels = core_index() == 1
    split_rows = lax.axis_index("lat") == lax.axis_size("lat") - 1
    ban_level = (j < WL) & (j != level)
    ban_row = (j >= F_Y) & (j < F_Y + WY) & ((j >= F_Y + SY) != (row >= SY))
    ban = jnp.where(ban_level, split_levels.astype(jnp.int32), jnp.where(ban_row, split_rows.astype(jnp.int32), 0))
    ban = jnp.where((lane & FEAT) == 0, ban, 0) == 1
    for part, (weight, table) in enumerate(((w_own, t_own), (w_sib, t_sib))):
        q = (dot(xn, weight[0]) * HD**-0.5).astype(jnp.bfloat16)
        k = dot(xn, weight[1]).astype(jnp.bfloat16)
        v = dot(xn, weight[2]).astype(jnp.bfloat16)
        for pair in range(2):
            cols = slice(pair * 128, pair * 128 + 128)
            extra = dot(feat[:, :FEAT], bias_rows(table, 1, pair))
            extra = jnp.where(ban, NEG, extra).astype(jnp.bfloat16)
            start = part * 256 + pair * 128
            out[:, start : start + 128] = pair_heads(q[:, cols], k[:, cols], v[:, cols], extra, feat)


def gelu(x):
    return 0.5 * x * (1.0 + lax.erf(x * np.float32(np.sqrt(0.5))))


def owned(member):
    return jnp.where(member == 0, 0, jnp.where(member == 1, 3, member - 1))


def mlp_kernel(mine, other, w0, w1, w2, w3, p0, p1, p2, p3, u0, u1, d0, d1, *refs):
    outs, held = refs[:4], refs[4]
    total = dot(mine[:, :256], w0[...]) + dot(mine[:, 256:], w1[...])
    total = total + dot(other[:, :256], w2[...]) + dot(other[:, 256:], w3[...])
    second = joined((p0, p1, p2, p3)) + total.astype(jnp.bfloat16).astype(jnp.float32)
    second = second.astype(jnp.bfloat16).astype(jnp.float32)
    xn = normalize(second)
    h0 = gelu(dot(xn, u0[...])).astype(jnp.bfloat16)
    h1 = gelu(dot(xn, u1[...])).astype(jnp.bfloat16)
    held[...] = 0.5 * second + dot(h0, d0[...]) + dot(h1, d1[...])
    member = lax.axis_index("mp")
    for step in range(4):
        start = pl.multiple_of(owned(member ^ step) * ROWS, 8)
        outs[step][...] = held[pl.ds(start, ROWS), :].astype(jnp.bfloat16)


def sum_kernel(own, far, near_sib, far_sib, out):
    mine = own[...].astype(jnp.float32) + far[...].astype(jnp.float32)
    sib = near_sib[...].astype(jnp.float32) + far_sib[...].astype(jnp.float32)
    first = core_index() == 0
    out[...] = jnp.concatenate([jnp.where(first, mine, sib), jnp.where(first, sib, mine)], axis=0).astype(
        jnp.bfloat16
    )


def place_kernel(r0, r1, r2, r3, out):
    member = lax.axis_index("mp")
    index = iota((1, 2 * ROWS), 1)
    core = jnp.where(index >= ROWS, 1, 0)
    slot = index - core * ROWS
    level, row, col = piece_place(slot)
    total = None
    for step, part in enumerate((r0, r1, r2, r3)):
        prow, pcol = patch_place(owned(member ^ step), row, col)
        place = (prow * 12 + pcol) * 4 + real_level(level, core)
        place = jnp.where(slot < USED, place, -1)
        term = dot(one_hot(iota((PATCH, 2 * ROWS), 0) == place), part[...])
        total = term if total is None else total + term
    out[...] = total.reshape(out.shape).astype(jnp.bfloat16)


def call(kernel, outs, operands, flops, limit, tables=(), scratch=()):
    shapes = [jax.ShapeDtypeStruct(s, jnp.bfloat16) for s in outs]
    moved = sum(o.size * o.dtype.itemsize for o in operands) + sum(2 * s.size for s in shapes)
    vmem = pl.BlockSpec(memory_space=pltpu.VMEM)
    smem = pl.BlockSpec(memory_space=pltpu.SMEM)
    result = pl.pallas_call(
        kernel,
        out_shape=shapes,
        in_specs=[vmem] * len(operands) + [smem] * len(tables),
        out_specs=[vmem] * len(shapes),
        scratch_shapes=scratch,
        compiler_params=pltpu.CompilerParams(vmem_limit_bytes=limit * MIB),
        cost_estimate=pl.CostEstimate(flops=flops, bytes_accessed=moved, transcendentals=0),
    )(*operands, *tables)
    return result if len(result) > 1 else result[0]


def tied(values, after):
    return lax.optimization_barrier((tuple(values), tuple(after)))[0]


def body(counts, tokens, qkv_first, qkv_second, out_first, out_second, rel_tables, up_weight, down_weight):
    levels, rows, cols, width = tokens.shape
    half = out_first.shape[0] // 2
    turn = counts[1] // 2

    def move(value, target):
        return lax.ppermute(value, AXES, pairs(counts, target))

    def core_swap(value):
        return move(value, lambda a, b, m: (a, b, m ^ 1))

    def chip_swap(value):
        return move(value, lambda a, b, m: (a, b, m ^ 2))

    def far_swap(value):
        return move(value, lambda a, b, m: (a, b, m ^ 3))

    def side_swap(value):
        return move(value, lambda a, b, m: (a, b + turn, m ^ 2))

    offsets = ((0, 0), (1, 0), (0, 1), (1, 1))
    pieces = [(ROWS, width)] * 4
    halves = [(KEPT, 256)] * 2

    tok = tokens.transpose(1, 2, 0, 3).reshape(rows * cols, levels, width)
    w_first = qkv_first.transpose(1, 0, 2)
    w_second = qkv_second.transpose(1, 0, 2)

    f2a = chip_swap(out_first[:half])
    f2b = side_swap(out_first[half:])
    f1 = core_swap(out_first)
    keep, give, base = call(
        first_kernel, halves + [(KEPT, width)], (tok, w_first), 10**9, 24, tables=(rel_tables,)
    )
    from_far = far_swap(give)
    from_chip = chip_swap(keep)
    from_core = core_swap(give)
    f3a = core_swap(f2a)
    f3b = core_swap(f2b)
    s_table = core_swap(rel_tables)
    w_sib = core_swap(w_second)

    firsts = call(
        residual_kernel,
        pieces,
        (keep, from_core, from_chip, from_far, out_first, f1, f2a, f2b, f3a, f3b, base),
        5 * 10**8,
        24,
    )
    *firsts, w_sib, s_table = tied((*firsts, w_sib, s_table), ())
    shifted = {0: firsts[0]}
    for q in (3, 2, 1):
        dy, dx = offsets[q]

        def target(a, b, m, dy=dy, dx=dx):
            return a - dy, b - dx, m ^ 2 if dx and b % turn == 0 else m

        shifted[q] = move(firsts[q], target)
    shifted = [shifted[q] for q in range(4)]
    out_second, up_weight, down_weight = tied((out_second, up_weight, down_weight), (w_sib,))
    s2 = chip_swap(out_second)
    s1 = core_swap(out_second)
    u1 = core_swap(up_weight)
    d1 = core_swap(down_weight)

    mixed = call(
        second_kernel,
        [(KEPT, 512)],
        (*shifted, w_second, w_sib),
        10**9,
        24,
        tables=(rel_tables, s_table),
    )
    other = chip_swap(mixed)
    s3 = core_swap(s2)
    own, to_core, to_chip, to_far = call(
        mlp_kernel,
        pieces,
        (mixed, other, out_second, s1, s2, s3, *shifted, up_weight, u1, down_weight, d1),
        2 * 10**9,
        40,
        scratch=[pltpu.VMEM((KEPT, width), jnp.float32)],
    )
    at_far = far_swap(to_far)
    at_chip = chip_swap(to_chip)
    at_core = core_swap(to_core)
    done = call(sum_kernel, [(2 * ROWS, width)], (own, at_chip, at_core, at_far), 10**6, 16)

    def home(flip):
        def target(a, b, m):
            dy, dx = offsets[(0, 3, 1, 2)[m]]
            return a + dy, b + dx, m ^ flip

        return target

    here = move(done, home(0))
    there = move(done, home(2))
    result = call(
        place_kernel,
        [(rows * cols, levels, width)],
        (here, core_swap(here), there, core_swap(there)),
        2 * 10**8,
        16,
    )
    return result.reshape(rows, cols, levels, width).transpose(2, 0, 1, 3)


def solution(mesh):
    counts = tuple(mesh.shape[name] for name in AXES)
    return jax.shard_map(
        functools.partial(body, counts),
        mesh=mesh,
        in_specs=(
            P(None, "lat", "lon", None),
            P(None, None, "mp"),
            P(None, None, "mp"),
            P("mp", None),
            P("mp", None),
            P(None, "mp", None),
            P(None, "mp"),
            P("mp", None),
        ),
        out_specs=P(None, "lat", "lon", None),
        check_vma=False,
    )
```

```python
import functools

import jax
import jax.numpy as jnp
import numpy as np
from jax import lax
from jax.experimental import pallas as pl
from jax.experimental.pallas import tpu as pltpu
from jax.sharding import PartitionSpec as P

WL = 2
WY = 6
WX = 12
SY = 3
SX = 6
HD = 64
NEG = -1000000000.0
AXES = ("lat", "lon", "mp")
MIB = 1024 * 1024

USED = 36
ROWS = 40
KEPT = 4 * ROWS
PATCH = 4 * WY * WX
WINDOW = WL * WY * WX
FEAT = 32
F_Y = 4
F_X = 10
F_PAD = 22


def pairs(counts, target):
    lats, lons, mps = counts
    result = []
    for a in range(lats):
        for b in range(lons):
            for m in range(mps):
                ta, tb, tm = target(a, b, m)
                dest = ((ta % lats) * lons + tb % lons) * mps + tm
                result.append(((a * lons + b) * mps + m, dest))
    return result


def dot(left, right):
    return jnp.dot(left, right, preferred_element_type=jnp.float32)


def dot_t(left, right):
    return lax.dot_general(left, right, (((1,), (1,)), ((), ())), preferred_element_type=jnp.float32)


def normalize(floats):
    center = floats - jnp.mean(floats, axis=-1, keepdims=True)
    spread = jnp.mean(center * center, axis=-1, keepdims=True)
    return (center * lax.rsqrt(spread + 1e-05)).astype(jnp.bfloat16)


def core_index():
    return lax.rem(lax.axis_index("mp"), 2)


def iota(shape, axis):
    return lax.broadcasted_iota(jnp.int32, shape, axis)


def one_hot(condition):
    return jnp.where(condition, 1.0, 0.0).astype(jnp.bfloat16)


def piece_place(slot):
    level = (slot * 57) >> 10
    rest = slot - level * 18
    row = (rest * 43) >> 8
    return level, row, rest - row * 6


def kept_place(index):
    q = (index * 205) >> 13
    return (q, index - q * ROWS) + piece_place(index - q * ROWS)


def real_level(level, core):
    return jnp.where(core == 0, 1 + level, 3 - 3 * level)


def patch_place(q, row, col):
    return row + 3 - 3 * (q & 1), col + 6 - 3 * (q & 2)


def bias_rows(table, block, pair):
    shape = (FEAT, 4 * FEAT)
    i, lane = iota(shape, 0), iota(shape, 1)
    j = lane & (FEAT - 1)
    kind = jnp.full(shape, 37, jnp.int32)
    kind = jnp.where((i < WL) & (j < WL), i - j + 1, kind)
    kind = jnp.where((i < WL) & (j == F_PAD), 38, kind)
    in_y = (i >= F_Y) & (i < F_Y + WY) & (j >= F_Y) & (j < F_Y + WY)
    kind = jnp.where(in_y, 3 + i - j + 5, kind)
    in_x = (i >= F_X) & (i < F_X + WX) & (j >= F_X) & (j < F_X + WX)
    kind = jnp.where(in_x, 14 + i - j + 11, kind)
    total = jnp.where(kind == 38, NEG, 0.0)
    for k in range(37):
        value = jnp.where(lane < HD, table[block, 2 * pair + 1, k], table[block, 2 * pair, k])
        total = jnp.where(kind == k, value, total)
    high = total.astype(jnp.bfloat16).astype(jnp.float32)
    return jnp.where((lane & FEAT) != 0, total - high, high).astype(jnp.bfloat16)


def features(level, row, col, used, count):
    j = iota((count, 128), 1) & (FEAT - 1)
    hit = (j == level) | (j == F_Y + row) | (j == F_X + col)
    return one_hot(jnp.where(used, jnp.where(hit, 1, 0), jnp.where(j == F_PAD, 1, 0)) == 1)


def pair_heads(query, key, value, extra, key_feat):
    low_q = iota(query.shape, 1) < HD
    low_k = iota(key.shape, 1) < HD
    outs = []
    for head in range(2):
        mine_q, mine_k = (low_q, low_k) if head == 0 else (~low_q, ~low_k)
        scores = dot_t(jnp.where(mine_q, query, extra), jnp.where(mine_k, key, key_feat))
        expo = jnp.exp(scores - jnp.max(scores, axis=-1, keepdims=True))
        probs = (expo / jnp.sum(expo, axis=-1, keepdims=True)).astype(jnp.bfloat16)
        outs.append(dot(probs, value))
    return jnp.where(low_q, outs[0], outs[1]).astype(jnp.bfloat16)


def fetch(source, held, sems):
    copies = [pltpu.make_async_copy(source.at[p], held.at[p], sems.at[p]) for p in range(3)]
    for copy in copies:
        copy.start()
    return copies


def first_kernel(tokens_ref, weight_ref, table_ref, keep, give, base, weight, sems, tokens, table, more):
    core = core_index()
    load = pltpu.make_async_copy(tokens_ref, tokens, more.at[0])
    load.start()
    copies = fetch(weight_ref, weight, sems)
    copies.append(pltpu.make_async_copy(table_ref, table, more.at[1]))
    copies[-1].start()
    load.wait()
    floats = tokens[...].astype(jnp.float32).reshape(PATCH, -1)
    xn = normalize(floats)
    for copy in copies:
        copy.wait()
    q = (dot(xn, weight[0]) * HD**-0.5).astype(jnp.bfloat16)
    k = dot(xn, weight[1]).astype(jnp.bfloat16)
    v = dot(xn, weight[2]).astype(jnp.bfloat16)
    index = iota((PATCH, 1), 0)
    level = (index * 911) >> 16
    order = one_hot(iota((PATCH, PATCH), 1) == (index - 72 * level) * 4 + level)
    q, k, v = (dot(order, part).astype(jnp.bfloat16) for part in (q, k, v))
    index = iota((WINDOW, 1), 0)
    level = (index * 911) >> 16
    rest = index - 72 * level
    row = (rest * 171) >> 11
    feat = features(level, row, rest - 12 * row, index >= 0, WINDOW)
    parts = []
    for pair in range(2):
        cols = slice(pair * 128, pair * 128 + 128)
        extra = dot(feat[:, :FEAT], bias_rows(table, 0, pair)).astype(jnp.bfloat16)
        halves = []
        for w in range(2):
            rows = slice(w * WINDOW, (w + 1) * WINDOW)
            halves.append(pair_heads(q[rows, cols], k[rows, cols], v[rows, cols], extra, feat))
        parts.append(jnp.concatenate(halves, axis=0))
    mixed = jnp.concatenate(parts, axis=1)
    quad, slot, level, row, col = kept_place(iota((KEPT, 1), 0))
    row, col = patch_place(quad, row, col)
    lanes = iota((KEPT, PATCH), 1)
    for out, chosen in ((keep, core), (give, 1 - core)):
        place = real_level(level, chosen) * 72 + row * 12 + col
        place = jnp.where(slot < USED, place, -1)
        out[...] = dot(one_hot(lanes == place), mixed).astype(jnp.bfloat16)
    place = (row * 12 + col) * 4 + real_level(level, core)
    place = jnp.where(slot < USED, place, -1)
    base[...] = dot(one_hot(lanes == place), floats.astype(jnp.bfloat16)).astype(jnp.bfloat16)


def partial_kernel(o1, w0, w1, o0_ref, base_ref, out, base_out, o0, base, sems):
    loads = [pltpu.make_async_copy(o0_ref, o0, sems.at[0]), pltpu.make_async_copy(base_ref, base, sems.at[1])]
    for load in loads:
        load.start()
    total = dot(o1[...], w1[...])
    loads[0].wait()
    out[...] = (total + dot(o0[...], w0[...])).astype(jnp.bfloat16)
    loads[1].wait()
    base_out[...] = base[...]


def branch_sum(mine, other):
    total = mine[...].astype(jnp.float32) + other[...].astype(jnp.float32)
    return total.astype(jnp.bfloat16).astype(jnp.float32)


def residual_kernel(mine, other, base, *outs):
    first = base[...].astype(jnp.float32) + branch_sum(mine, other)
    for q in range(4):
        outs[q][...] = first[q * ROWS : (q + 1) * ROWS].astype(jnp.bfloat16)


def joined(pieces):
    return jnp.concatenate([p[...].astype(jnp.float32) for p in pieces], axis=0)


def second_kernel(p0, p1, p2, p3, w_sib, o0, o1, w_ref, t_own_ref, t_sib_ref, out, w_own, sems, t_own, t_sib, more):
    copies = fetch(w_ref, w_own, sems)
    loads = [
        pltpu.make_async_copy(t_own_ref, t_own, more.at[0]),
        pltpu.make_async_copy(t_sib_ref, t_sib, more.at[1]),
    ]
    for load in loads:
        load.start()
    xn = normalize(joined((p0, p1, p2, p3)))
    quad, slot, level, row, col = kept_place(iota((KEPT, 1), 0))
    row, col = row + 3 * (quad & 1), col + 3 * (quad & 2)
    feat = features(level, row, col, slot < USED, KEPT)
    lane = iota((KEPT, 128), 1)
    j = lane & (FEAT - 1)
    split_levels = core_index() == 1
    split_rows = lax.axis_index("lat") == lax.axis_size("lat") - 1
    ban_level = (j < WL) & (j != level)
    ban_row = (j >= F_Y) & (j < F_Y + WY) & ((j >= F_Y + SY) != (row >= SY))
    ban = jnp.where(ban_level, split_levels.astype(jnp.int32), jnp.where(ban_row, split_rows.astype(jnp.int32), 0))
    ban = jnp.where((lane & FEAT) == 0, ban, 0) == 1
    for load in loads:
        load.wait()
    total = None
    for weight, table, project in ((w_sib, t_sib, o1), (w_own, t_own, o0)):
        if weight is w_own:
            for copy in copies:
                copy.wait()
        q = (dot(xn, weight[0]) * HD**-0.5).astype(jnp.bfloat16)
        k = dot(xn, weight[1]).astype(jnp.bfloat16)
        v = dot(xn, weight[2]).astype(jnp.bfloat16)
        for pair in range(2):
            cols = slice(pair * 128, pair * 128 + 128)
            extra = dot(feat[:, :FEAT], bias_rows(table, 1, pair))
            extra = jnp.where(ban, NEG, extra).astype(jnp.bfloat16)
            mixed = pair_heads(q[:, cols], k[:, cols], v[:, cols], extra, feat)
            term = dot(mixed, project[cols, :])
            total = term if total is None else total + term
    out[...] = total.astype(jnp.bfloat16)


def gelu(x):
    return 0.5 * x * (1.0 + lax.erf(x * np.float32(np.sqrt(0.5))))


def owned(member):
    return jnp.where(member == 0, 0, jnp.where(member == 1, 3, member - 1))


def mlp_kernel(mine, other, p0, p1, p2, p3, u0, u1, d0, d1, *refs):
    outs, held = refs[:4], refs[4]
    second = joined((p0, p1, p2, p3)) + branch_sum(mine, other)
    second = second.astype(jnp.bfloat16).astype(jnp.float32)
    xn = normalize(second)
    h0 = gelu(dot(xn, u0[...])).astype(jnp.bfloat16)
    h1 = gelu(dot(xn, u1[...])).astype(jnp.bfloat16)
    held[...] = 0.5 * second + dot(h0, d0[...]) + dot(h1, d1[...])
    member = lax.axis_index("mp")
    for step in range(4):
        start = pl.multiple_of(owned(member ^ step) * ROWS, 8)
        outs[step][...] = held[pl.ds(start, ROWS), :].astype(jnp.bfloat16)


def sum_kernel(own, far, near_sib, far_sib, out):
    mine = own[...].astype(jnp.float32) + far[...].astype(jnp.float32)
    sib = near_sib[...].astype(jnp.float32) + far_sib[...].astype(jnp.float32)
    first = core_index() == 0
    out[...] = jnp.concatenate([jnp.where(first, mine, sib), jnp.where(first, sib, mine)], axis=0).astype(
        jnp.bfloat16
    )


def place_kernel(r0, r1, r2, r3, out):
    member = lax.axis_index("mp")
    index = iota((1, 2 * ROWS), 1)
    core = jnp.where(index >= ROWS, 1, 0)
    slot = index - core * ROWS
    level, row, col = piece_place(slot)
    total = None
    for step, part in enumerate((r0, r1, r2, r3)):
        prow, pcol = patch_place(owned(member ^ step), row, col)
        place = (prow * 12 + pcol) * 4 + real_level(level, core)
        place = jnp.where(slot < USED, place, -1)
        term = dot(one_hot(iota((PATCH, 2 * ROWS), 0) == place), part[...])
        total = term if total is None else total + term
    out[...] = total.reshape(out.shape).astype(jnp.bfloat16)


def call(kernel, outs, operands, flops, limit, large=(), scratch=()):
    shapes = [jax.ShapeDtypeStruct(s, jnp.bfloat16) for s in outs]
    operands = (*operands, *large)
    moved = sum(o.size * o.dtype.itemsize for o in operands) + sum(2 * s.size for s in shapes)
    vmem = pl.BlockSpec(memory_space=pltpu.VMEM)
    plain = len(operands) - len(large)
    result = pl.pallas_call(
        kernel,
        out_shape=shapes,
        in_specs=[vmem] * plain + [pl.BlockSpec(memory_space=pltpu.HBM)] * len(large),
        out_specs=[vmem] * len(shapes),
        scratch_shapes=scratch,
        compiler_params=pltpu.CompilerParams(vmem_limit_bytes=limit * MIB),
        cost_estimate=pl.CostEstimate(flops=flops, bytes_accessed=moved, transcendentals=0),
    )(*operands)
    return result if len(result) > 1 else result[0]


def tied(*values):
    return lax.optimization_barrier(values)


def body(counts, tokens, qkv_first, qkv_second, out_first, out_second, rel_tables, up_weight, down_weight):
    levels, rows, cols, width = tokens.shape
    turn = counts[1] // 2

    def move(value, target):
        return lax.ppermute(value, AXES, pairs(counts, target))

    def core_swap(value):
        return move(value, lambda a, b, m: (a, b, m ^ 1))

    def chip_swap(value):
        return move(value, lambda a, b, m: (a, b, m ^ 2))

    def far_swap(value):
        return move(value, lambda a, b, m: (a, b, m ^ 3))

    offsets = ((0, 0), (1, 0), (0, 1), (1, 1))
    pieces = [(ROWS, width)] * 4
    halves = [(KEPT, 256)] * 2
    own_qkv = [pltpu.VMEM((3, width, 256), jnp.bfloat16), pltpu.SemaphoreType.DMA((3,))]
    table = pltpu.SMEM(rel_tables.shape, jnp.float32)
    two = pltpu.SemaphoreType.DMA((2,))

    tok = tokens.transpose(1, 2, 0, 3).reshape(rows * cols, levels, width)
    w_first = qkv_first.transpose(1, 0, 2)
    w_second = qkv_second.transpose(1, 0, 2)

    f1 = core_swap(out_first)
    s1 = core_swap(out_second)
    w_sib = core_swap(w_second)
    s_table = core_swap(rel_tables)
    keep, give, base = call(
        first_kernel,
        halves + [(KEPT, width)],
        (),
        10**9,
        57,
        large=(tok, w_first, rel_tables),
        scratch=own_qkv + [pltpu.VMEM(tok.shape, jnp.bfloat16), table, two],
    )
    keep, give, f1, s1, w_sib, s_table = tied(keep, give, f1, s1, w_sib, s_table)
    part, base = call(
        partial_kernel,
        [(KEPT, width)] * 2,
        (core_swap(give), out_first, f1),
        2 * 10**8,
        8,
        large=(keep, base),
        scratch=[pltpu.VMEM((KEPT, 256), jnp.bfloat16), pltpu.VMEM((KEPT, width), jnp.bfloat16), two],
    )
    firsts = call(residual_kernel, pieces, (part, chip_swap(part), base), 10**6, 8)
    shifted = {0: firsts[0]}
    for q in (3, 2, 1):
        dy, dx = offsets[q]

        def target(a, b, m, dy=dy, dx=dx):
            return a - dy, b - dx, m ^ 2 if dx and b % turn == 0 else m

        shifted[q] = move(firsts[q], target)
    shifted = [shifted[q] for q in range(4)]

    part = call(
        second_kernel,
        [(KEPT, width)],
        (*shifted, w_sib, out_second, s1),
        10**9,
        16,
        large=(w_second, rel_tables, s_table),
        scratch=own_qkv + [table, table, two],
    )
    part, up_weight, down_weight = tied(part, up_weight, down_weight)
    u1 = core_swap(up_weight)
    d1 = core_swap(down_weight)
    own, to_core, to_chip, to_far = call(
        mlp_kernel,
        pieces,
        (part, chip_swap(part), *shifted, up_weight, u1, down_weight, d1),
        2 * 10**9,
        24,
        scratch=[pltpu.VMEM((KEPT, width), jnp.float32)],
    )
    at_far = far_swap(to_far)
    at_chip = chip_swap(to_chip)
    at_core = core_swap(to_core)
    done = call(sum_kernel, [(2 * ROWS, width)], (own, at_chip, at_core, at_far), 10**6, 8)

    def home(flip):
        def target(a, b, m):
            dy, dx = offsets[(0, 3, 1, 2)[m]]
            return a + dy, b + dx, m ^ flip

        return target

    here = move(done, home(0))
    there = move(done, home(2))
    result = call(
        place_kernel,
        [(rows * cols, levels, width)],
        (here, core_swap(here), there, core_swap(there)),
        2 * 10**8,
        12,
    )
    return result.reshape(rows, cols, levels, width).transpose(2, 0, 1, 3)


def solution(mesh):
    counts = tuple(mesh.shape[name] for name in AXES)
    return jax.shard_map(
        functools.partial(body, counts),
        mesh=mesh,
        in_specs=(
            P(None, "lat", "lon", None),
            P(None, None, "mp"),
            P(None, None, "mp"),
            P("mp", None),
            P("mp", None),
            P(None, "mp", None),
            P(None, "mp"),
            P("mp", None),
        ),
        out_specs=P(None, "lat", "lon", None),
        check_vma=False,
    )
```

```python
import functools

import jax
import jax.numpy as jnp
import numpy as np
from jax import lax
from jax.experimental import pallas as pl
from jax.experimental.pallas import tpu as pltpu
from jax.sharding import PartitionSpec as P

WL = 2
WY = 6
WX = 12
SY = 3
SX = 6
HD = 64
NEG = -1000000000.0
AXES = ("lat", "lon", "mp")
MIB = 1024 * 1024

USED = 36
ROWS = 40
KEPT = 4 * ROWS
HALF = 2 * ROWS
PATCH = 4 * WY * WX
WINDOW = WL * WY * WX
FEAT = 32
F_Y = 4
F_X = 10
F_PAD = 22


def pairs(counts, target):
    lats, lons, mps = counts
    result = []
    for a in range(lats):
        for b in range(lons):
            for m in range(mps):
                ta, tb, tm = target(a, b, m)
                dest = ((ta % lats) * lons + tb % lons) * mps + tm
                result.append(((a * lons + b) * mps + m, dest))
    return result


def dot(left, right):
    return jnp.dot(left, right, preferred_element_type=jnp.float32)


def dot_t(left, right):
    return lax.dot_general(left, right, (((1,), (1,)), ((), ())), preferred_element_type=jnp.float32)


def normalize(floats):
    center = floats - jnp.mean(floats, axis=-1, keepdims=True)
    spread = jnp.mean(center * center, axis=-1, keepdims=True)
    return (center * lax.rsqrt(spread + 1e-05)).astype(jnp.bfloat16)


def core_index():
    return lax.rem(lax.axis_index("mp"), 2)


def iota(shape, axis):
    return lax.broadcasted_iota(jnp.int32, shape, axis)


def one_hot(condition):
    return jnp.where(condition, 1.0, 0.0).astype(jnp.bfloat16)


def piece_place(slot):
    level = (slot * 57) >> 10
    rest = slot - level * 18
    row = (rest * 43) >> 8
    return level, row, rest - row * 6


def kept_place(index):
    piece = (index * 205) >> 13
    slot = index - piece * ROWS
    return ((piece + 2) & 3, slot) + piece_place(slot)


def real_level(level, core):
    return jnp.where(core == 0, 1 + level, 3 - 3 * level)


def patch_place(q, row, col):
    return row + 3 - 3 * (q & 1), col + 6 - 3 * (q & 2)


def bias_rows(table, block, pair):
    shape = (FEAT, 4 * FEAT)
    i, lane = iota(shape, 0), iota(shape, 1)
    j = lane & (FEAT - 1)
    kind = jnp.full(shape, 37, jnp.int32)
    kind = jnp.where((i < WL) & (j < WL), i - j + 1, kind)
    kind = jnp.where((i < WL) & (j == F_PAD), 38, kind)
    in_y = (i >= F_Y) & (i < F_Y + WY) & (j >= F_Y) & (j < F_Y + WY)
    kind = jnp.where(in_y, 3 + i - j + 5, kind)
    in_x = (i >= F_X) & (i < F_X + WX) & (j >= F_X) & (j < F_X + WX)
    kind = jnp.where(in_x, 14 + i - j + 11, kind)
    total = jnp.where(kind == 38, NEG, 0.0)
    for k in range(37):
        value = jnp.where(lane < HD, table[block, 2 * pair + 1, k], table[block, 2 * pair, k])
        total = jnp.where(kind == k, value, total)
    high = total.astype(jnp.bfloat16).astype(jnp.float32)
    return jnp.where((lane & FEAT) != 0, total - high, high).astype(jnp.bfloat16)


def bias_kernel(table, first, second):
    for block, out in enumerate((first, second)):
        for pair in range(2):
            out[:, pair * 128 : pair * 128 + 128] = bias_rows(table, block, pair)


def features(level, row, col, used, count):
    j = iota((count, 128), 1) & (FEAT - 1)
    hit = (j == level) | (j == F_Y + row) | (j == F_X + col)
    return one_hot(jnp.where(used, jnp.where(hit, 1, 0), jnp.where(j == F_PAD, 1, 0)) == 1)


def pair_heads(query, key, value, extra, key_feat):
    low_q = iota(query.shape, 1) < HD
    low_k = iota(key.shape, 1) < HD
    outs = []
    for head in range(2):
        mine_q, mine_k = (low_q, low_k) if head == 0 else (~low_q, ~low_k)
        scores = dot_t(jnp.where(mine_q, query, extra), jnp.where(mine_k, key, key_feat))
        expo = jnp.exp(scores - jnp.max(scores, axis=-1, keepdims=True))
        probs = (expo / jnp.sum(expo, axis=-1, keepdims=True)).astype(jnp.bfloat16)
        outs.append(dot(probs, value))
    return jnp.where(low_q, outs[0], outs[1]).astype(jnp.bfloat16)


def first_kernel(tokens, weight, bias, keep, give, *bases):
    core = core_index()
    floats = tokens[...].astype(jnp.float32).reshape(PATCH, -1)
    xn = normalize(floats)
    q = (dot(xn, weight[0]) * HD**-0.5).astype(jnp.bfloat16)
    k = dot(xn, weight[1]).astype(jnp.bfloat16)
    v = dot(xn, weight[2]).astype(jnp.bfloat16)
    index = iota((PATCH, 1), 0)
    level = (index * 911) >> 16
    order = one_hot(iota((PATCH, PATCH), 1) == (index - 72 * level) * 4 + level)
    q, k, v = (dot(order, part).astype(jnp.bfloat16) for part in (q, k, v))
    index = iota((WINDOW, 1), 0)
    level = (index * 911) >> 16
    rest = index - 72 * level
    row = (rest * 171) >> 11
    feat = features(level, row, rest - 12 * row, index >= 0, WINDOW)
    parts = []
    for pair in range(2):
        cols = slice(pair * 128, pair * 128 + 128)
        extra = dot(feat[:, :FEAT], bias[:, cols]).astype(jnp.bfloat16)
        halves = []
        for w in range(2):
            rows = slice(w * WINDOW, (w + 1) * WINDOW)
            halves.append(pair_heads(q[rows, cols], k[rows, cols], v[rows, cols], extra, feat))
        parts.append(jnp.concatenate(halves, axis=0))
    mixed = jnp.concatenate(parts, axis=1)
    quad, slot, level, row, col = kept_place(iota((KEPT, 1), 0))
    row, col = patch_place(quad, row, col)
    lanes = iota((KEPT, PATCH), 1)
    for out, chosen in ((keep, core), (give, 1 - core)):
        place = real_level(level, chosen) * 72 + row * 12 + col
        place = jnp.where(slot < USED, place, -1)
        out[...] = dot(one_hot(lanes == place), mixed).astype(jnp.bfloat16)
    place = (row * 12 + col) * 4 + real_level(level, core)
    place = jnp.where(slot < USED, place, -1)
    base = dot(one_hot(lanes == place), floats.astype(jnp.bfloat16)).astype(jnp.bfloat16)
    for h in range(2):
        bases[h][...] = base[h * HALF : (h + 1) * HALF]


def store_halves(total, outs):
    for h in range(2):
        outs[h][...] = total[h * HALF : (h + 1) * HALF].astype(jnp.bfloat16)


def partial_kernel(o0, o1, w0, w1, *outs):
    store_halves(dot(o0[...], w0[...]) + dot(o1[...], w1[...]), outs)


def branch_sum(mine, other):
    total = mine[...].astype(jnp.float32) + other[...].astype(jnp.float32)
    return total.astype(jnp.bfloat16).astype(jnp.float32)


def residual_kernel(mine, other, base, *outs):
    first = base[...].astype(jnp.float32) + branch_sum(mine, other)
    for p in range(2):
        outs[p][...] = first[p * ROWS : (p + 1) * ROWS].astype(jnp.bfloat16)


def joined(pieces):
    return jnp.concatenate([p[...].astype(jnp.float32) for p in pieces], axis=0)


def norm_kernel(p0, p1, out):
    out[...] = normalize(joined((p0, p1)))


def second_kernel(xn_a, p2, p3, w_own, w_sib, o_own, o_sib, b_own, b_sib, *outs):
    xn_b = normalize(joined((p2, p3))).astype(jnp.float32)
    xn = jnp.concatenate([xn_a[...].astype(jnp.float32), xn_b], axis=0).astype(jnp.bfloat16)
    quad, slot, level, row, col = kept_place(iota((KEPT, 1), 0))
    row, col = row + 3 * (quad & 1), col + 3 * (quad & 2)
    feat = features(level, row, col, slot < USED, KEPT)
    lane = iota((KEPT, 128), 1)
    j = lane & (FEAT - 1)
    split_levels = core_index() == 1
    split_rows = lax.axis_index("lat") == lax.axis_size("lat") - 1
    ban_level = (j < WL) & (j != level)
    ban_row = (j >= F_Y) & (j < F_Y + WY) & ((j >= F_Y + SY) != (row >= SY))
    ban = jnp.where(ban_level, split_levels.astype(jnp.int32), jnp.where(ban_row, split_rows.astype(jnp.int32), 0))
    ban = jnp.where((lane & FEAT) == 0, ban, 0) == 1
    total = None
    for weight, bias, project in ((w_own, b_own, o_own), (w_sib, b_sib, o_sib)):
        q = (dot(xn, weight[0]) * HD**-0.5).astype(jnp.bfloat16)
        k = dot(xn, weight[1]).astype(jnp.bfloat16)
        v = dot(xn, weight[2]).astype(jnp.bfloat16)
        for pair in range(2):
            cols = slice(pair * 128, pair * 128 + 128)
            extra = dot(feat[:, :FEAT], bias[:, cols])
            extra = jnp.where(ban, NEG, extra).astype(jnp.bfloat16)
            mixed = pair_heads(q[:, cols], k[:, cols], v[:, cols], extra, feat)
            term = dot(mixed, project[cols, :])
            total = term if total is None else total + term
    store_halves(total, outs)


def gelu(x):
    return 0.5 * x * (1.0 + lax.erf(x * np.float32(np.sqrt(0.5))))


def mlp_kernel(mine, other, p0, p1, u0, u1, d0, d1, out):
    second = joined((p0, p1)) + branch_sum(mine, other)
    second = second.astype(jnp.bfloat16).astype(jnp.float32)
    xn = normalize(second)
    h0 = gelu(dot(xn, u0[...])).astype(jnp.bfloat16)
    h1 = gelu(dot(xn, u1[...])).astype(jnp.bfloat16)
    out[...] = (0.5 * second + dot(h0, d0[...]) + dot(h1, d1[...])).astype(jnp.bfloat16)


def sum_kernel(mine, other, *outs):
    total = mine[...].astype(jnp.float32) + other[...].astype(jnp.float32)
    for p in range(2):
        outs[p][...] = total[p * ROWS : (p + 1) * ROWS].astype(jnp.bfloat16)


def place_kernel(half, m0, m1, s0, s1, *refs):
    out, held, sems = refs[-3:]
    core = core_index()
    index = iota((1, HALF), 1)
    slot = jnp.where(index >= ROWS, index - ROWS, index)
    level, row, col = piece_place(slot)
    row = jnp.where(index >= ROWS, row, row + SY)
    total = None
    for chosen, pieces in ((core, (m0, m1)), (1 - core, (s0, s1))):
        place = (row * SX + col) * 4 + real_level(level, chosen)
        place = jnp.where(slot < USED, place, -1)
        term = dot(one_hot(iota((PATCH // 2, HALF), 0) == place), joined(pieces).astype(jnp.bfloat16))
        total = term if total is None else total + term
    held[...] = total.reshape(held.shape).astype(jnp.bfloat16)
    copies = []
    for y in range(WY):
        target = out.at[pl.ds(y * WX + half * SX, SX)]
        copies.append(pltpu.make_async_copy(held.at[pl.ds(y * SX, SX)], target, sems.at[y]))
        copies[-1].start()
    for copy in copies:
        copy.wait()


def place(half, pieces, shape, held):
    vmem, large = pl.BlockSpec(memory_space=pltpu.VMEM), pl.BlockSpec(memory_space=pl.ANY)
    return pl.pallas_call(
        functools.partial(place_kernel, half),
        out_shape=jax.ShapeDtypeStruct(shape, jnp.bfloat16),
        in_specs=[vmem] * 4 + [large] * len(held),
        out_specs=large,
        scratch_shapes=[
            pltpu.VMEM((shape[0] // 2,) + shape[1:], jnp.bfloat16),
            pltpu.SemaphoreType.DMA((WY,)),
        ],
        input_output_aliases={4: 0} if held else {},
        compiler_params=pltpu.CompilerParams(vmem_limit_bytes=12 * MIB),
        cost_estimate=pl.CostEstimate(flops=10**10, bytes_accessed=10**6, transcendentals=0),
    )(*pieces, *held)


def call(kernel, outs, operands, flops, limit, table=False):
    shapes = [jax.ShapeDtypeStruct(s, jnp.bfloat16) for s in outs]
    moved = sum(o.size * o.dtype.itemsize for o in operands) + sum(2 * s.size for s in shapes)
    result = pl.pallas_call(
        kernel,
        out_shape=shapes,
        in_specs=[pl.BlockSpec(memory_space=pltpu.SMEM if table else pltpu.VMEM)] * len(operands),
        out_specs=[pl.BlockSpec(memory_space=pltpu.VMEM)] * len(shapes),
        compiler_params=pltpu.CompilerParams(vmem_limit_bytes=limit * MIB),
        cost_estimate=pl.CostEstimate(flops=flops, bytes_accessed=moved, transcendentals=0),
    )(*operands)
    return result if len(result) > 1 else result[0]


def tied(*values):
    return lax.optimization_barrier(values)


def body(counts, tokens, qkv_first, qkv_second, out_first, out_second, rel_tables, up_weight, down_weight):
    levels, rows, cols, width = tokens.shape
    turn = counts[1] // 2

    def move(value, target):
        return lax.ppermute(value, AXES, pairs(counts, target))

    def core_swap(value):
        return move(value, lambda a, b, m: (a, b, m ^ 1))

    def chip_swap(value):
        return move(value, lambda a, b, m: (a, b, m ^ 2))

    def out_to(value, dy, dx):
        return move(value, lambda a, b, m: (a - dy, b - dx, m ^ 2 if dx and b % turn == 0 else m))

    def home(value, dy, dx):
        return move(value, lambda a, b, m: (a + dy, b + dx, m ^ 2 if dx and (b + 1) % turn == 0 else m))

    full, half, piece = [(KEPT, width)], [(HALF, width)], [(ROWS, width)]
    heads, features = [(KEPT, 256)], [(FEAT, 256)]

    tok = tokens.transpose(1, 2, 0, 3).reshape(rows * cols, levels, width)
    w_first = qkv_first.transpose(1, 0, 2)
    w_second = qkv_second.transpose(1, 0, 2)

    f1 = core_swap(out_first)
    s1 = core_swap(out_second)
    w_sib = core_swap(w_second)
    bias1, bias2 = call(bias_kernel, features * 2, (rel_tables,), 5 * 10**9, 4, table=True)
    bias2_sib = core_swap(bias2)
    keep, give, base_a, base_b = call(first_kernel, heads * 2 + half * 2, (tok, w_first, bias1), 10**9, 16)
    keep, give, f1, s1, w_sib, bias2_sib = tied(keep, give, f1, s1, w_sib, bias2_sib)
    given, up_late, down_late = tied(core_swap(give), up_weight, down_weight)
    u1 = core_swap(up_late)
    d1 = core_swap(down_late)
    part_a, part_b = call(partial_kernel, half * 2, (keep, given, out_first, f1), 2 * 10**8, 8)
    other_a = chip_swap(part_a)
    other_b = chip_swap(part_b)
    lon, diag = call(residual_kernel, piece * 2, (part_a, other_a, base_a), 10**6, 8)
    lon, diag, part_b = tied(lon, diag, part_b)
    own, lat = call(residual_kernel, piece * 2, (part_b, other_b, base_b), 10**10, 8)
    lon = out_to(lon, 0, 1)
    diag = out_to(diag, 1, 1)
    lat = out_to(lat, 1, 0)

    xn_a = call(norm_kernel, half, (lon, diag), 10**10, 8)
    part_a, part_b = call(
        second_kernel,
        half * 2,
        (xn_a, own, lat, w_second, w_sib, out_second, s1, bias2, bias2_sib),
        10**9,
        16,
    )
    other_a = chip_swap(part_a)
    other_b = chip_swap(part_b)
    mlp = (up_weight, u1, down_weight, d1)
    part_a = call(mlp_kernel, half, (part_a, other_a, lon, diag, *mlp), 10**9, 20)
    part_a, part_b = tied(part_a, part_b)
    other_a = chip_swap(part_a)
    part_b = call(mlp_kernel, half, (part_b, other_b, own, lat, *mlp), 10**9, 20)
    other_b = chip_swap(part_b)
    lon, diag = call(sum_kernel, piece * 2, (part_a, other_a), 10**6, 8)
    lon, diag, part_b = tied(lon, diag, part_b)
    lon = home(lon, 0, 1)
    diag = home(diag, 1, 1)
    own, lat = call(sum_kernel, piece * 2, (part_b, other_b), 10**10, 8)
    lat = home(lat, 1, 0)
    shape = (rows * cols, levels, width)
    result = place(0, (lon, diag, core_swap(lon), core_swap(diag)), shape, ())
    result = place(1, (own, lat, core_swap(own), core_swap(lat)), shape, (result,))
    return result.reshape(rows, cols, levels, width).transpose(2, 0, 1, 3)


def solution(mesh):
    counts = tuple(mesh.shape[name] for name in AXES)
    return jax.shard_map(
        functools.partial(body, counts),
        mesh=mesh,
        in_specs=(
            P(None, "lat", "lon", None),
            P(None, None, "mp"),
            P(None, None, "mp"),
            P("mp", None),
            P("mp", None),
            P(None, "mp", None),
            P(None, "mp"),
            P("mp", None),
        ),
        out_specs=P(None, "lat", "lon", None),
        check_vma=False,
    )
```

```python
import functools

import jax
import jax.numpy as jnp
import numpy as np
from jax import lax
from jax.experimental import pallas as pl
from jax.experimental.pallas import tpu as pltpu
from jax.sharding import PartitionSpec as P

WL = 2
WY = 6
WX = 12
SY = 3
SX = 6
HD = 64
NEG = -1000000000.0
AXES = ("lat", "lon", "mp")
MIB = 1024 * 1024

USED = 36
ROWS = 40
KEPT = 4 * ROWS
HALF = 2 * ROWS
PATCH = 4 * WY * WX
WINDOW = WL * WY * WX
FEAT = 32
F_Y = 4
F_X = 10
F_PAD = 22


def pairs(counts, target):
    lats, lons, mps = counts
    result = []
    for a in range(lats):
        for b in range(lons):
            for m in range(mps):
                ta, tb, tm = target(a, b, m)
                dest = ((ta % lats) * lons + tb % lons) * mps + tm
                result.append(((a * lons + b) * mps + m, dest))
    return result


def dot(left, right):
    return jnp.dot(left, right, preferred_element_type=jnp.float32)


def dot_t(left, right):
    return lax.dot_general(left, right, (((1,), (1,)), ((), ())), preferred_element_type=jnp.float32)


def normalize(floats):
    center = floats - jnp.mean(floats, axis=-1, keepdims=True)
    spread = jnp.mean(center * center, axis=-1, keepdims=True)
    return (center * lax.rsqrt(spread + 1e-05)).astype(jnp.bfloat16)


def core_index():
    return lax.rem(lax.axis_index("mp"), 2)


def iota(shape, axis):
    return lax.broadcasted_iota(jnp.int32, shape, axis)


def one_hot(condition):
    return jnp.where(condition, 1.0, 0.0).astype(jnp.bfloat16)


def piece_place(slot):
    level = (slot * 57) >> 10
    rest = slot - level * 18
    row = (rest * 43) >> 8
    return level, row, rest - row * 6


def kept_place(index):
    quad = (index * 205) >> 13
    slot = index - quad * ROWS
    return (quad, slot) + piece_place(slot)


def real_level(level, core):
    return jnp.where(core == 0, 1 + level, 3 - 3 * level)


def patch_place(q, row, col):
    return row + 3 - 3 * (q & 1), col + 6 - 3 * (q & 2)


def bias_rows(table, block, pair):
    shape = (FEAT, 4 * FEAT)
    i, lane = iota(shape, 0), iota(shape, 1)
    j = lane & (FEAT - 1)
    kind = jnp.full(shape, 37, jnp.int32)
    kind = jnp.where((i < WL) & (j < WL), i - j + 1, kind)
    kind = jnp.where((i < WL) & (j == F_PAD), 38, kind)
    in_y = (i >= F_Y) & (i < F_Y + WY) & (j >= F_Y) & (j < F_Y + WY)
    kind = jnp.where(in_y, 3 + i - j + 5, kind)
    in_x = (i >= F_X) & (i < F_X + WX) & (j >= F_X) & (j < F_X + WX)
    kind = jnp.where(in_x, 14 + i - j + 11, kind)
    total = jnp.where(kind == 38, NEG, 0.0)
    for k in range(37):
        value = jnp.where(lane < HD, table[block, 2 * pair + 1, k], table[block, 2 * pair, k])
        total = jnp.where(kind == k, value, total)
    high = total.astype(jnp.bfloat16).astype(jnp.float32)
    return jnp.where((lane & FEAT) != 0, total - high, high).astype(jnp.bfloat16)


def bias_kernel(table, first, second):
    for block, out in enumerate((first, second)):
        for pair in range(2):
            out[:, pair * 128 : pair * 128 + 128] = bias_rows(table, block, pair)


def features(level, row, col, used, count):
    j = iota((count, 128), 1) & (FEAT - 1)
    hit = (j == level) | (j == F_Y + row) | (j == F_X + col)
    return one_hot(jnp.where(used, jnp.where(hit, 1, 0), jnp.where(j == F_PAD, 1, 0)) == 1)


def pair_heads(query, key, value, extra, key_feat):
    low_q = iota(query.shape, 1) < HD
    low_k = iota(key.shape, 1) < HD
    outs = []
    for head in range(2):
        mine_q, mine_k = (low_q, low_k) if head == 0 else (~low_q, ~low_k)
        scores = dot_t(jnp.where(mine_q, query, extra), jnp.where(mine_k, key, key_feat))
        expo = jnp.exp(scores - jnp.max(scores, axis=-1, keepdims=True))
        probs = (expo / jnp.sum(expo, axis=-1, keepdims=True)).astype(jnp.bfloat16)
        outs.append(dot(probs, value))
    return jnp.where(low_q, outs[0], outs[1]).astype(jnp.bfloat16)


def first_kernel(tokens, weight, bias, keep, give, *bases):
    core = core_index()
    floats = tokens[...].astype(jnp.float32).reshape(PATCH, -1)
    xn = normalize(floats)
    q = (dot(xn, weight[0]) * HD**-0.5).astype(jnp.bfloat16)
    k = dot(xn, weight[1]).astype(jnp.bfloat16)
    v = dot(xn, weight[2]).astype(jnp.bfloat16)
    index = iota((PATCH, 1), 0)
    level = (index * 911) >> 16
    order = one_hot(iota((PATCH, PATCH), 1) == (index - 72 * level) * 4 + level)
    q, k, v = (dot(order, part).astype(jnp.bfloat16) for part in (q, k, v))
    index = iota((WINDOW, 1), 0)
    level = (index * 911) >> 16
    rest = index - 72 * level
    row = (rest * 171) >> 11
    feat = features(level, row, rest - 12 * row, index >= 0, WINDOW)
    parts = []
    for pair in range(2):
        cols = slice(pair * 128, pair * 128 + 128)
        extra = dot(feat[:, :FEAT], bias[:, cols]).astype(jnp.bfloat16)
        halves = []
        for w in range(2):
            rows = slice(w * WINDOW, (w + 1) * WINDOW)
            halves.append(pair_heads(q[rows, cols], k[rows, cols], v[rows, cols], extra, feat))
        parts.append(jnp.concatenate(halves, axis=0))
    mixed = jnp.concatenate(parts, axis=1)
    quad, slot, level, row, col = kept_place(iota((KEPT, 1), 0))
    row, col = patch_place(quad, row, col)
    lanes = iota((KEPT, PATCH), 1)
    for out, chosen in ((keep, core), (give, 1 - core)):
        place = real_level(level, chosen) * 72 + row * 12 + col
        place = jnp.where(slot < USED, place, -1)
        out[...] = dot(one_hot(lanes == place), mixed).astype(jnp.bfloat16)
    place = (row * 12 + col) * 4 + real_level(level, core)
    place = jnp.where(slot < USED, place, -1)
    base = dot(one_hot(lanes == place), floats.astype(jnp.bfloat16)).astype(jnp.bfloat16)
    for h in range(2):
        bases[h][...] = base[h * HALF : (h + 1) * HALF]


def store_halves(total, outs):
    for h in range(2):
        outs[h][...] = total[h * HALF : (h + 1) * HALF].astype(jnp.bfloat16)


def partial_kernel(o0, o1, w0, w1, *outs):
    store_halves(dot(o0[...], w0[...]) + dot(o1[...], w1[...]), outs)


def branch_sum(mine, other):
    total = mine[...].astype(jnp.float32) + other[...].astype(jnp.float32)
    return total.astype(jnp.bfloat16).astype(jnp.float32)


def residual_kernel(mine, other, base, *outs):
    first = base[...].astype(jnp.float32) + branch_sum(mine, other)
    for p in range(2):
        outs[p][...] = first[p * ROWS : (p + 1) * ROWS].astype(jnp.bfloat16)


def joined(pieces):
    return jnp.concatenate([p[...].astype(jnp.float32) for p in pieces], axis=0)


def norm_kernel(p0, p1, out):
    out[...] = normalize(joined((p0, p1)))


def second_kernel(xn_a, p2, p3, w_own, w_sib, o_own, o_sib, b_own, b_sib, *outs):
    xn_b = normalize(joined((p2, p3))).astype(jnp.float32)
    xn = jnp.concatenate([xn_a[...].astype(jnp.float32), xn_b], axis=0).astype(jnp.bfloat16)
    quad, slot, level, row, col = kept_place(iota((KEPT, 1), 0))
    row, col = row + 3 * (quad & 1), col + 3 * (quad & 2)
    feat = features(level, row, col, slot < USED, KEPT)
    lane = iota((KEPT, 128), 1)
    j = lane & (FEAT - 1)
    split_levels = core_index() == 1
    split_rows = lax.axis_index("lat") == 0
    ban_level = (j < WL) & (j != level)
    ban_row = (j >= F_Y) & (j < F_Y + WY) & ((j >= F_Y + SY) != (row >= SY))
    ban = jnp.where(ban_level, split_levels.astype(jnp.int32), jnp.where(ban_row, split_rows.astype(jnp.int32), 0))
    ban = jnp.where((lane & FEAT) == 0, ban, 0) == 1
    total = None
    for weight, bias, project in ((w_own, b_own, o_own), (w_sib, b_sib, o_sib)):
        q = (dot(xn, weight[0]) * HD**-0.5).astype(jnp.bfloat16)
        k = dot(xn, weight[1]).astype(jnp.bfloat16)
        v = dot(xn, weight[2]).astype(jnp.bfloat16)
        for pair in range(2):
            cols = slice(pair * 128, pair * 128 + 128)
            extra = dot(feat[:, :FEAT], bias[:, cols])
            extra = jnp.where(ban, NEG, extra).astype(jnp.bfloat16)
            mixed = pair_heads(q[:, cols], k[:, cols], v[:, cols], extra, feat)
            term = dot(mixed, project[cols, :])
            total = term if total is None else total + term
    store_halves(total, outs)


def gelu(x):
    return 0.5 * x * (1.0 + lax.erf(x * np.float32(np.sqrt(0.5))))


def mlp_kernel(mine, other, p0, p1, u0, u1, d0, d1, out):
    second = joined((p0, p1)) + branch_sum(mine, other)
    second = second.astype(jnp.bfloat16).astype(jnp.float32)
    xn = normalize(second)
    h0 = gelu(dot(xn, u0[...])).astype(jnp.bfloat16)
    h1 = gelu(dot(xn, u1[...])).astype(jnp.bfloat16)
    out[...] = (0.5 * second + dot(h0, d0[...]) + dot(h1, d1[...])).astype(jnp.bfloat16)


def sum_kernel(mine, other, *outs):
    total = mine[...].astype(jnp.float32) + other[...].astype(jnp.float32)
    for p in range(2):
        outs[p][...] = total[p * ROWS : (p + 1) * ROWS].astype(jnp.bfloat16)


def place_kernel(half, m0, m1, s0, s1, *refs):
    out, held, sems = refs[-3:]
    core = core_index()
    index = iota((1, HALF), 1)
    slot = jnp.where(index >= ROWS, index - ROWS, index)
    level, row, col = piece_place(slot)
    row = jnp.where(index >= ROWS, row, row + SY)
    total = None
    for chosen, pieces in ((core, (m0, m1)), (1 - core, (s0, s1))):
        place = (row * SX + col) * 4 + real_level(level, chosen)
        place = jnp.where(slot < USED, place, -1)
        term = dot(one_hot(iota((PATCH // 2, HALF), 0) == place), joined(pieces).astype(jnp.bfloat16))
        total = term if total is None else total + term
    held[...] = total.reshape(held.shape).astype(jnp.bfloat16)
    copies = []
    for y in range(WY):
        target = out.at[pl.ds(y * WX + half * SX, SX)]
        copies.append(pltpu.make_async_copy(held.at[pl.ds(y * SX, SX)], target, sems.at[y]))
        copies[-1].start()
    for copy in copies:
        copy.wait()


def place(half, pieces, shape, held):
    vmem, large = pl.BlockSpec(memory_space=pltpu.VMEM), pl.BlockSpec(memory_space=pl.ANY)
    return pl.pallas_call(
        functools.partial(place_kernel, half),
        out_shape=jax.ShapeDtypeStruct(shape, jnp.bfloat16),
        in_specs=[vmem] * 4 + [large] * len(held),
        out_specs=large,
        scratch_shapes=[
            pltpu.VMEM((shape[0] // 2,) + shape[1:], jnp.bfloat16),
            pltpu.SemaphoreType.DMA((WY,)),
        ],
        input_output_aliases={4: 0} if held else {},
        compiler_params=pltpu.CompilerParams(vmem_limit_bytes=12 * MIB),
        cost_estimate=pl.CostEstimate(flops=10**10, bytes_accessed=10**6, transcendentals=0),
    )(*pieces, *held)


def call(kernel, outs, operands, flops, limit, table=False):
    shapes = [jax.ShapeDtypeStruct(s, jnp.bfloat16) for s in outs]
    moved = sum(o.size * o.dtype.itemsize for o in operands) + sum(2 * s.size for s in shapes)
    result = pl.pallas_call(
        kernel,
        out_shape=shapes,
        in_specs=[pl.BlockSpec(memory_space=pltpu.SMEM if table else pltpu.VMEM)] * len(operands),
        out_specs=[pl.BlockSpec(memory_space=pltpu.VMEM)] * len(shapes),
        compiler_params=pltpu.CompilerParams(vmem_limit_bytes=limit * MIB),
        cost_estimate=pl.CostEstimate(flops=flops, bytes_accessed=moved, transcendentals=0),
    )(*operands)
    return result if len(result) > 1 else result[0]


def tied(*values):
    return lax.optimization_barrier(values)


def body(counts, tokens, qkv_first, qkv_second, out_first, out_second, rel_tables, up_weight, down_weight):
    levels, rows, cols, width = tokens.shape
    turn = counts[1] // 2

    def move(value, target):
        return lax.ppermute(value, AXES, pairs(counts, target))

    def core_swap(value):
        return move(value, lambda a, b, m: (a, b, m ^ 1))

    def chip_swap(value):
        return move(value, lambda a, b, m: (a, b, m ^ 2))

    def out_to(value, dy, dx):
        return move(value, lambda a, b, m: (a + dy, b + dx, m ^ 2 if dx and (b + 1) % turn == 0 else m))

    def home(value, dy, dx):
        return move(value, lambda a, b, m: (a - dy, b - dx, m ^ 2 if dx and b % turn == 0 else m))

    half, piece = [(HALF, width)], [(ROWS, width)]
    heads, features = [(KEPT, 256)], [(FEAT, 256)]

    tok = tokens.transpose(1, 2, 0, 3).reshape(rows * cols, levels, width)
    w_first = qkv_first.transpose(1, 0, 2)
    w_second = qkv_second.transpose(1, 0, 2)

    f1 = core_swap(out_first)
    s1 = core_swap(out_second)
    w_sib = core_swap(w_second)
    bias1, bias2 = call(bias_kernel, features * 2, (rel_tables,), 5 * 10**9, 4, table=True)
    bias2_sib = core_swap(bias2)
    keep, give, base_a, base_b = call(first_kernel, heads * 2 + half * 2, (tok, w_first, bias1), 10**9, 16)
    keep, give, f1, s1, w_sib, bias2_sib = tied(keep, give, f1, s1, w_sib, bias2_sib)
    given, up_late, down_late = tied(core_swap(give), up_weight, down_weight)
    u1 = core_swap(up_late)
    d1 = core_swap(down_late)
    part_a, part_b = call(partial_kernel, half * 2, (keep, given, out_first, f1), 2 * 10**8, 8)
    other_a = chip_swap(part_a)
    other_b = chip_swap(part_b)
    diag, lon = call(residual_kernel, piece * 2, (part_a, other_a, base_a), 10**6, 8)
    diag, lon, part_b = tied(diag, lon, part_b)
    lat, own = call(residual_kernel, piece * 2, (part_b, other_b, base_b), 10**10, 8)
    diag = out_to(diag, 1, 1)
    lon = out_to(lon, 0, 1)
    lat = out_to(lat, 1, 0)

    xn_a = call(norm_kernel, half, (diag, lon), 10**10, 8)
    part_a, part_b = call(
        second_kernel,
        half * 2,
        (xn_a, lat, own, w_second, w_sib, out_second, s1, bias2, bias2_sib),
        10**9,
        16,
    )
    other_a = chip_swap(part_a)
    other_b = chip_swap(part_b)
    mlp = (up_weight, u1, down_weight, d1)
    part_a = call(mlp_kernel, half, (part_a, other_a, diag, lon, *mlp), 10**9, 20)
    part_a, part_b = tied(part_a, part_b)
    other_a = chip_swap(part_a)
    part_b = call(mlp_kernel, half, (part_b, other_b, lat, own, *mlp), 10**9, 20)
    other_b = chip_swap(part_b)
    diag, lon = call(sum_kernel, piece * 2, (part_a, other_a), 10**6, 8)
    diag, lon, part_b = tied(diag, lon, part_b)
    diag = home(diag, 1, 1)
    lon = home(lon, 0, 1)
    lat, own = call(sum_kernel, piece * 2, (part_b, other_b), 10**10, 8)
    lat = home(lat, 1, 0)
    shape = (rows * cols, levels, width)
    result = place(1, (diag, lon, core_swap(diag), core_swap(lon)), shape, ())
    result = place(0, (lat, own, core_swap(lat), core_swap(own)), shape, (result,))
    return result.reshape(rows, cols, levels, width).transpose(2, 0, 1, 3)


def solution(mesh):
    counts = tuple(mesh.shape[name] for name in AXES)
    return jax.shard_map(
        functools.partial(body, counts),
        mesh=mesh,
        in_specs=(
            P(None, "lat", "lon", None),
            P(None, None, "mp"),
            P(None, None, "mp"),
            P("mp", None),
            P("mp", None),
            P(None, "mp", None),
            P(None, "mp"),
            P("mp", None),
        ),
        out_specs=P(None, "lat", "lon", None),
        check_vma=False,
    )
```

```python
import functools

import jax
import jax.numpy as jnp
import numpy as np
from jax import lax
from jax.experimental import pallas as pl
from jax.experimental.pallas import tpu as pltpu
from jax.sharding import PartitionSpec as P

WL = 2
WY = 6
WX = 12
SY = 3
SX = 6
HD = 64
NEG = -1000000000.0
AXES = ("lat", "lon", "mp")
MIB = 1024 * 1024

USED = 36
ROWS = 40
KEPT = 4 * ROWS
HALF = 2 * ROWS
PATCH = 4 * WY * WX
WINDOW = WL * WY * WX
FEAT = 32
F_Y = 4
F_X = 10
F_PAD = 22


def pairs(counts, target):
    lats, lons, mps = counts
    result = []
    for a in range(lats):
        for b in range(lons):
            for m in range(mps):
                ta, tb, tm = target(a, b, m)
                dest = ((ta % lats) * lons + tb % lons) * mps + tm
                result.append(((a * lons + b) * mps + m, dest))
    return result


def dot(left, right):
    return jnp.dot(left, right, preferred_element_type=jnp.float32)


def dot_t(left, right):
    return lax.dot_general(left, right, (((1,), (1,)), ((), ())), preferred_element_type=jnp.float32)


def normalize(floats):
    center = floats - jnp.mean(floats, axis=-1, keepdims=True)
    spread = jnp.mean(center * center, axis=-1, keepdims=True)
    return (center * lax.rsqrt(spread + 1e-05)).astype(jnp.bfloat16)


def core_index():
    return lax.rem(lax.axis_index("mp"), 2)


def iota(shape, axis):
    return lax.broadcasted_iota(jnp.int32, shape, axis)


def one_hot(condition):
    return jnp.where(condition, 1.0, 0.0).astype(jnp.bfloat16)


def piece_place(slot):
    level = (slot * 57) >> 10
    rest = slot - level * 18
    row = (rest * 43) >> 8
    return level, row, rest - row * 6


def kept_place(index):
    quad = (index * 205) >> 13
    slot = index - quad * ROWS
    return (quad, slot) + piece_place(slot)


def real_level(level, core):
    return jnp.where(core == 0, 1 + level, 3 - 3 * level)


def patch_place(q, row, col):
    return row + 3 - 3 * (q & 1), col + 6 - 3 * (q & 2)


def bias_rows(table, block, pair):
    shape = (FEAT, 4 * FEAT)
    i, lane = iota(shape, 0), iota(shape, 1)
    j = lane & (FEAT - 1)
    kind = jnp.full(shape, 37, jnp.int32)
    kind = jnp.where((i < WL) & (j < WL), i - j + 1, kind)
    kind = jnp.where((i < WL) & (j == F_PAD), 38, kind)
    in_y = (i >= F_Y) & (i < F_Y + WY) & (j >= F_Y) & (j < F_Y + WY)
    kind = jnp.where(in_y, 3 + i - j + 5, kind)
    in_x = (i >= F_X) & (i < F_X + WX) & (j >= F_X) & (j < F_X + WX)
    kind = jnp.where(in_x, 14 + i - j + 11, kind)
    total = jnp.where(kind == 38, NEG, 0.0)
    for k in range(37):
        value = jnp.where(lane < HD, table[block, 2 * pair + 1, k], table[block, 2 * pair, k])
        total = jnp.where(kind == k, value, total)
    high = total.astype(jnp.bfloat16).astype(jnp.float32)
    return jnp.where((lane & FEAT) != 0, total - high, high).astype(jnp.bfloat16)


def bias_kernel(table, first, second):
    for block, out in enumerate((first, second)):
        for pair in range(2):
            out[:, pair * 128 : pair * 128 + 128] = bias_rows(table, block, pair)


def features(level, row, col, used, count):
    j = iota((count, 128), 1) & (FEAT - 1)
    hit = (j == level) | (j == F_Y + row) | (j == F_X + col)
    return one_hot(jnp.where(used, jnp.where(hit, 1, 0), jnp.where(j == F_PAD, 1, 0)) == 1)


def pair_heads(query, key, value, extra, key_feat):
    count = query.shape[0]
    low = iota(query.shape, 1) < HD
    none = jnp.zeros_like(query)
    upper = jnp.concatenate([jnp.where(low, query, none), jnp.where(low, none, extra)], axis=1)
    lower = jnp.concatenate([jnp.where(low, none, query), jnp.where(low, extra, none)], axis=1)
    scores = dot_t(jnp.concatenate([upper, lower], axis=0), jnp.concatenate([key, key_feat], axis=1))
    expo = jnp.exp(scores - jnp.max(scores, axis=-1, keepdims=True))
    scale = 1.0 / jnp.sum(expo, axis=-1, keepdims=True)
    mixed = dot(expo.astype(jnp.bfloat16), value) * scale
    return jnp.where(low, mixed[:count], mixed[count:]).astype(jnp.bfloat16)


def first_kernel(tokens, weight, bias, keep, give, *bases):
    core = core_index()
    floats = tokens[...].astype(jnp.float32).reshape(PATCH, -1)
    xn = normalize(floats)
    q = (dot(xn, weight[0]) * HD**-0.5).astype(jnp.bfloat16)
    k = dot(xn, weight[1]).astype(jnp.bfloat16)
    v = dot(xn, weight[2]).astype(jnp.bfloat16)
    index = iota((PATCH, 1), 0)
    level = (index * 911) >> 16
    order = one_hot(iota((PATCH, PATCH), 1) == (index - 72 * level) * 4 + level)
    q, k, v = (dot(order, part).astype(jnp.bfloat16) for part in (q, k, v))
    index = iota((WINDOW, 1), 0)
    level = (index * 911) >> 16
    rest = index - 72 * level
    row = (rest * 171) >> 11
    feat = features(level, row, rest - 12 * row, index >= 0, WINDOW)
    parts = []
    for pair in range(2):
        cols = slice(pair * 128, pair * 128 + 128)
        extra = dot(feat[:, :FEAT], bias[:, cols]).astype(jnp.bfloat16)
        halves = []
        for w in range(2):
            rows = slice(w * WINDOW, (w + 1) * WINDOW)
            halves.append(pair_heads(q[rows, cols], k[rows, cols], v[rows, cols], extra, feat))
        parts.append(jnp.concatenate(halves, axis=0))
    mixed = jnp.concatenate(parts, axis=1)
    quad, slot, level, row, col = kept_place(iota((KEPT, 1), 0))
    row, col = patch_place(quad, row, col)
    lanes = iota((KEPT, PATCH), 1)
    for out, chosen in ((keep, core), (give, 1 - core)):
        place = real_level(level, chosen) * 72 + row * 12 + col
        place = jnp.where(slot < USED, place, -1)
        out[...] = dot(one_hot(lanes == place), mixed).astype(jnp.bfloat16)
    place = (row * 12 + col) * 4 + real_level(level, core)
    place = jnp.where(slot < USED, place, -1)
    base = dot(one_hot(lanes == place), floats.astype(jnp.bfloat16)).astype(jnp.bfloat16)
    for h in range(2):
        bases[h][...] = base[h * HALF : (h + 1) * HALF]


def store_halves(total, outs):
    for h in range(2):
        outs[h][...] = total[h * HALF : (h + 1) * HALF].astype(jnp.bfloat16)


def partial_kernel(o0, o1, w0, w1, *outs):
    store_halves(dot(o0[...], w0[...]) + dot(o1[...], w1[...]), outs)


def branch_sum(mine, other):
    total = mine[...].astype(jnp.float32) + other[...].astype(jnp.float32)
    return total.astype(jnp.bfloat16).astype(jnp.float32)


def residual_kernel(mine, other, base, *outs):
    first = base[...].astype(jnp.float32) + branch_sum(mine, other)
    for p in range(2):
        outs[p][...] = first[p * ROWS : (p + 1) * ROWS].astype(jnp.bfloat16)


def joined(pieces):
    return jnp.concatenate([p[...].astype(jnp.float32) for p in pieces], axis=0)


def norm_kernel(p0, p1, out):
    out[...] = normalize(joined((p0, p1)))


def second_kernel(xn_a, p2, p3, w_own, w_sib, o_own, o_sib, b_own, b_sib, *outs):
    xn_b = normalize(joined((p2, p3))).astype(jnp.float32)
    xn = jnp.concatenate([xn_a[...].astype(jnp.float32), xn_b], axis=0).astype(jnp.bfloat16)
    quad, slot, level, row, col = kept_place(iota((KEPT, 1), 0))
    row, col = row + 3 * (quad & 1), col + 3 * (quad & 2)
    feat = features(level, row, col, slot < USED, KEPT)
    lane = iota((KEPT, 128), 1)
    j = lane & (FEAT - 1)
    split_levels = core_index() == 1
    split_rows = lax.axis_index("lat") == 0
    ban_level = (j < WL) & (j != level)
    ban_row = (j >= F_Y) & (j < F_Y + WY) & ((j >= F_Y + SY) != (row >= SY))
    ban = jnp.where(ban_level, split_levels.astype(jnp.int32), jnp.where(ban_row, split_rows.astype(jnp.int32), 0))
    ban = jnp.where((lane & FEAT) == 0, ban, 0) == 1
    total = None
    for weight, bias, project in ((w_own, b_own, o_own), (w_sib, b_sib, o_sib)):
        q = (dot(xn, weight[0]) * HD**-0.5).astype(jnp.bfloat16)
        k = dot(xn, weight[1]).astype(jnp.bfloat16)
        v = dot(xn, weight[2]).astype(jnp.bfloat16)
        for pair in range(2):
            cols = slice(pair * 128, pair * 128 + 128)
            extra = dot(feat[:, :FEAT], bias[:, cols])
            extra = jnp.where(ban, NEG, extra).astype(jnp.bfloat16)
            mixed = pair_heads(q[:, cols], k[:, cols], v[:, cols], extra, feat)
            term = dot(mixed, project[cols, :])
            total = term if total is None else total + term
    store_halves(total, outs)


def gelu(x):
    return 0.5 * x * (1.0 + lax.erf(x * np.float32(np.sqrt(0.5))))


def mlp_kernel(mine, other, p0, p1, u0, u1, d0, d1, out):
    second = joined((p0, p1)) + branch_sum(mine, other)
    second = second.astype(jnp.bfloat16).astype(jnp.float32)
    xn = normalize(second)
    h0 = gelu(dot(xn, u0[...])).astype(jnp.bfloat16)
    h1 = gelu(dot(xn, u1[...])).astype(jnp.bfloat16)
    out[...] = (0.5 * second + dot(h0, d0[...]) + dot(h1, d1[...])).astype(jnp.bfloat16)


def sum_kernel(mine, other, *outs):
    total = mine[...].astype(jnp.float32) + other[...].astype(jnp.float32)
    for p in range(2):
        outs[p][...] = total[p * ROWS : (p + 1) * ROWS].astype(jnp.bfloat16)


def join_kernel(p0, p1, out):
    out[...] = joined((p0, p1)).astype(jnp.bfloat16)


def place_kernel(m0, m1, s0, s1, out):
    core = core_index()
    quad, slot, level, row, col = kept_place(iota((1, KEPT), 1))
    row, col = patch_place(quad, row, col)
    total = None
    for chosen, parts in ((core, (m0, m1)), (1 - core, (s0, s1))):
        place = (row * 12 + col) * 4 + real_level(level, chosen)
        place = jnp.where(slot < USED, place, -1)
        source = jnp.concatenate([part[...] for part in parts], axis=0)
        term = dot(one_hot(iota((PATCH, KEPT), 0) == place), source)
        total = term if total is None else total + term
    out[...] = total.reshape(out.shape).astype(jnp.bfloat16)


def call(kernel, outs, operands, flops, limit, table=False):
    shapes = [jax.ShapeDtypeStruct(s, jnp.bfloat16) for s in outs]
    moved = sum(o.size * o.dtype.itemsize for o in operands) + sum(2 * s.size for s in shapes)
    result = pl.pallas_call(
        kernel,
        out_shape=shapes,
        in_specs=[pl.BlockSpec(memory_space=pltpu.SMEM if table else pltpu.VMEM)] * len(operands),
        out_specs=[pl.BlockSpec(memory_space=pltpu.VMEM)] * len(shapes),
        compiler_params=pltpu.CompilerParams(vmem_limit_bytes=limit * MIB),
        cost_estimate=pl.CostEstimate(flops=flops, bytes_accessed=moved, transcendentals=0),
    )(*operands)
    return result if len(result) > 1 else result[0]


def tied(*values):
    return lax.optimization_barrier(values)


def body(counts, tokens, qkv_first, qkv_second, out_first, out_second, rel_tables, up_weight, down_weight):
    levels, rows, cols, width = tokens.shape
    turn = counts[1] // 2

    def move(value, target):
        return lax.ppermute(value, AXES, pairs(counts, target))

    def core_swap(value):
        return move(value, lambda a, b, m: (a, b, m ^ 1))

    def chip_swap(value):
        return move(value, lambda a, b, m: (a, b, m ^ 2))

    def out_to(value, dy, dx):
        return move(value, lambda a, b, m: (a + dy, b + dx, m ^ 2 if dx and (b + 1) % turn == 0 else m))

    def home(value, dy, dx):
        return move(value, lambda a, b, m: (a - dy, b - dx, m ^ 2 if dx and b % turn == 0 else m))

    half, piece = [(HALF, width)], [(ROWS, width)]
    heads, features = [(KEPT, 256)], [(FEAT, 256)]

    tok = tokens.transpose(1, 2, 0, 3).reshape(rows * cols, levels, width)
    w_first = qkv_first.transpose(1, 0, 2)
    w_second = qkv_second.transpose(1, 0, 2)

    f1 = core_swap(out_first)
    s1 = core_swap(out_second)
    w_sib = core_swap(w_second)
    bias1, bias2 = call(bias_kernel, features * 2, (rel_tables,), 5 * 10**9, 4, table=True)
    bias2_sib = core_swap(bias2)
    keep, give, base_a, base_b = call(first_kernel, heads * 2 + half * 2, (tok, w_first, bias1), 10**9, 16)
    keep, give, f1, s1, w_sib, bias2_sib = tied(keep, give, f1, s1, w_sib, bias2_sib)
    given, up_late, down_late = tied(core_swap(give), up_weight, down_weight)
    u1 = core_swap(up_late)
    d1 = core_swap(down_late)
    part_a, part_b = call(partial_kernel, half * 2, (keep, given, out_first, f1), 2 * 10**8, 8)
    other_a = chip_swap(part_a)
    other_b = chip_swap(part_b)
    diag, lon = call(residual_kernel, piece * 2, (part_a, other_a, base_a), 10**6, 8)
    diag, lon, part_b = tied(diag, lon, part_b)
    lat, own = call(residual_kernel, piece * 2, (part_b, other_b, base_b), 10**10, 8)
    diag = out_to(diag, 1, 1)
    lon = out_to(lon, 0, 1)
    lat = out_to(lat, 1, 0)

    xn_a = call(norm_kernel, half, (diag, lon), 10**10, 8)
    part_a, part_b = call(
        second_kernel,
        half * 2,
        (xn_a, lat, own, w_second, w_sib, out_second, s1, bias2, bias2_sib),
        10**9,
        16,
    )
    other_a = chip_swap(part_a)
    other_b = chip_swap(part_b)
    mlp = (up_weight, u1, down_weight, d1)
    part_a = call(mlp_kernel, half, (part_a, other_a, diag, lon, *mlp), 10**9, 20)
    part_a, part_b = tied(part_a, part_b)
    other_a = chip_swap(part_a)
    part_b = call(mlp_kernel, half, (part_b, other_b, lat, own, *mlp), 10**9, 20)
    other_b = chip_swap(part_b)
    diag, lon = call(sum_kernel, piece * 2, (part_a, other_a), 10**6, 8)
    diag, lon, part_b = tied(diag, lon, part_b)
    diag = home(diag, 1, 1)
    lon = home(lon, 0, 1)
    lat, own = call(sum_kernel, piece * 2, (part_b, other_b), 10**10, 8)
    lat = home(lat, 1, 0)
    mine_a = call(join_kernel, half, (diag, lon), 10**10, 8)
    mine_b = call(join_kernel, half, (lat, own), 10**6, 8)
    result = call(
        place_kernel,
        [(rows * cols, levels, width)],
        (mine_a, mine_b, core_swap(mine_a), core_swap(mine_b)),
        2 * 10**8,
        12,
    )
    return result.reshape(rows, cols, levels, width).transpose(2, 0, 1, 3)


def solution(mesh):
    counts = tuple(mesh.shape[name] for name in AXES)
    return jax.shard_map(
        functools.partial(body, counts),
        mesh=mesh,
        in_specs=(
            P(None, "lat", "lon", None),
            P(None, None, "mp"),
            P(None, None, "mp"),
            P("mp", None),
            P("mp", None),
            P(None, "mp", None),
            P(None, "mp"),
            P("mp", None),
        ),
        out_specs=P(None, "lat", "lon", None),
        check_vma=False,
    )
```

```python
import functools

import jax
import jax.numpy as jnp
import numpy as np
from jax import lax
from jax.experimental import pallas as pl
from jax.experimental.pallas import tpu as pltpu
from jax.sharding import PartitionSpec as P

WL = 2
WY = 6
WX = 12
SY = 3
SX = 6
HD = 64
NEG = -1000000000.0
AXES = ("lat", "lon", "mp")
MIB = 1024 * 1024

USED = 36
ROWS = 40
KEPT = 4 * ROWS
HALF = 2 * ROWS
PATCH = 4 * WY * WX
WINDOW = WL * WY * WX
FEAT = 32
F_Y = 4
F_X = 10
F_PAD = 22


def pairs(counts, target):
    lats, lons, mps = counts
    result = []
    for a in range(lats):
        for b in range(lons):
            for m in range(mps):
                ta, tb, tm = target(a, b, m)
                dest = ((ta % lats) * lons + tb % lons) * mps + tm
                result.append(((a * lons + b) * mps + m, dest))
    return result


def dot(left, right):
    return jnp.dot(left, right, preferred_element_type=jnp.float32)


def dot_t(left, right):
    return lax.dot_general(left, right, (((1,), (1,)), ((), ())), preferred_element_type=jnp.float32)


def normalize(floats):
    center = floats - jnp.mean(floats, axis=-1, keepdims=True)
    spread = jnp.mean(center * center, axis=-1, keepdims=True)
    return (center * lax.rsqrt(spread + 1e-05)).astype(jnp.bfloat16)


def core_index():
    return lax.rem(lax.axis_index("mp"), 2)


def iota(shape, axis):
    return lax.broadcasted_iota(jnp.int32, shape, axis)


def one_hot(condition):
    return jnp.where(condition, 1.0, 0.0).astype(jnp.bfloat16)


def piece_place(slot):
    level = (slot * 57) >> 10
    rest = slot - level * 18
    row = (rest * 43) >> 8
    return level, row, rest - row * 6


def kept_place(index):
    quad = (index * 205) >> 13
    slot = index - quad * ROWS
    return (quad, slot) + piece_place(slot)


def real_level(level, core):
    return jnp.where(core == 0, 1 + level, 3 - 3 * level)


def patch_place(q, row, col):
    return row + 3 - 3 * (q & 1), col + 6 - 3 * (q & 2)


def bias_rows(table, block, pair):
    shape = (FEAT, 4 * FEAT)
    i, lane = iota(shape, 0), iota(shape, 1)
    j = lane & (FEAT - 1)
    kind = jnp.full(shape, 37, jnp.int32)
    kind = jnp.where((i < WL) & (j < WL), i - j + 1, kind)
    kind = jnp.where((i < WL) & (j == F_PAD), 38, kind)
    in_y = (i >= F_Y) & (i < F_Y + WY) & (j >= F_Y) & (j < F_Y + WY)
    kind = jnp.where(in_y, 3 + i - j + 5, kind)
    in_x = (i >= F_X) & (i < F_X + WX) & (j >= F_X) & (j < F_X + WX)
    kind = jnp.where(in_x, 14 + i - j + 11, kind)
    total = jnp.where(kind == 38, NEG, 0.0)
    for k in range(37):
        value = jnp.where(lane < HD, table[block, 2 * pair + 1, k], table[block, 2 * pair, k])
        total = jnp.where(kind == k, value, total)
    high = total.astype(jnp.bfloat16).astype(jnp.float32)
    return jnp.where((lane & FEAT) != 0, total - high, high).astype(jnp.bfloat16)


def bias_kernel(table, first, second):
    for block, out in enumerate((first, second)):
        for pair in range(2):
            out[:, pair * 128 : pair * 128 + 128] = bias_rows(table, block, pair)


def features(level, row, col, used, count):
    j = iota((count, 128), 1) & (FEAT - 1)
    hit = (j == level) | (j == F_Y + row) | (j == F_X + col)
    return one_hot(jnp.where(used, jnp.where(hit, 1, 0), jnp.where(j == F_PAD, 1, 0)) == 1)


def pair_heads(query, key, value, extra, key_feat):
    count = query.shape[0]
    low = iota(query.shape, 1) < HD
    none = jnp.zeros_like(query)
    upper = jnp.concatenate([jnp.where(low, query, none), jnp.where(low, none, extra)], axis=1)
    lower = jnp.concatenate([jnp.where(low, none, query), jnp.where(low, extra, none)], axis=1)
    scores = dot_t(jnp.concatenate([upper, lower], axis=0), jnp.concatenate([key, key_feat], axis=1))
    expo = jnp.exp(scores - jnp.max(scores, axis=-1, keepdims=True))
    scale = 1.0 / jnp.sum(expo, axis=-1, keepdims=True)
    mixed = dot(expo.astype(jnp.bfloat16), value) * scale
    return jnp.where(low, mixed[:count], mixed[count:]).astype(jnp.bfloat16)


def first_kernel(tokens, weight, bias, keep, give, *bases):
    core = core_index()
    floats = tokens[...].astype(jnp.float32).reshape(PATCH, -1)
    xn = normalize(floats)
    q = (dot(xn, weight[0]) * HD**-0.5).astype(jnp.bfloat16)
    k = dot(xn, weight[1]).astype(jnp.bfloat16)
    v = dot(xn, weight[2]).astype(jnp.bfloat16)
    index = iota((PATCH, 1), 0)
    level = (index * 911) >> 16
    order = one_hot(iota((PATCH, PATCH), 1) == (index - 72 * level) * 4 + level)
    q, k, v = (dot(order, part).astype(jnp.bfloat16) for part in (q, k, v))
    index = iota((WINDOW, 1), 0)
    level = (index * 911) >> 16
    rest = index - 72 * level
    row = (rest * 171) >> 11
    feat = features(level, row, rest - 12 * row, index >= 0, WINDOW)
    parts = []
    for pair in range(2):
        cols = slice(pair * 128, pair * 128 + 128)
        extra = dot(feat[:, :FEAT], bias[:, cols]).astype(jnp.bfloat16)
        halves = []
        for w in range(2):
            rows = slice(w * WINDOW, (w + 1) * WINDOW)
            halves.append(pair_heads(q[rows, cols], k[rows, cols], v[rows, cols], extra, feat))
        parts.append(jnp.concatenate(halves, axis=0))
    mixed = jnp.concatenate(parts, axis=1)
    quad, slot, level, row, col = kept_place(iota((KEPT, 1), 0))
    row, col = patch_place(quad, row, col)
    lanes = iota((KEPT, PATCH), 1)
    for out, chosen in ((keep, core), (give, 1 - core)):
        place = real_level(level, chosen) * 72 + row * 12 + col
        place = jnp.where(slot < USED, place, -1)
        out[...] = dot(one_hot(lanes == place), mixed).astype(jnp.bfloat16)
    place = (row * 12 + col) * 4 + real_level(level, core)
    place = jnp.where(slot < USED, place, -1)
    base = dot(one_hot(lanes == place), floats.astype(jnp.bfloat16)).astype(jnp.bfloat16)
    for h in range(2):
        bases[h][...] = base[h * HALF : (h + 1) * HALF]


def store_halves(total, outs):
    for h in range(2):
        outs[h][...] = total[h * HALF : (h + 1) * HALF].astype(jnp.bfloat16)


def partial_kernel(o0, o1, w0, w1, *outs):
    store_halves(dot(o0[...], w0[...]) + dot(o1[...], w1[...]), outs)


def branch_sum(mine, other):
    total = mine[...].astype(jnp.float32) + other[...].astype(jnp.float32)
    return total.astype(jnp.bfloat16).astype(jnp.float32)


def residual_kernel(mine, other, base, *outs):
    first = base[...].astype(jnp.float32) + branch_sum(mine, other)
    for p in range(2):
        outs[p][...] = first[p * ROWS : (p + 1) * ROWS].astype(jnp.bfloat16)


def joined(pieces):
    return jnp.concatenate([p[...].astype(jnp.float32) for p in pieces], axis=0)


def norm_kernel(p0, p1, out):
    out[...] = normalize(joined((p0, p1)))


def second_kernel(xn_a, p2, p3, w_own, w_sib, o_own, o_sib, b_own, b_sib, *outs):
    xn_b = normalize(joined((p2, p3))).astype(jnp.float32)
    xn = jnp.concatenate([xn_a[...].astype(jnp.float32), xn_b], axis=0).astype(jnp.bfloat16)
    quad, slot, level, row, col = kept_place(iota((KEPT, 1), 0))
    row, col = row + 3 * (quad & 1), col + 3 * (quad & 2)
    feat = features(level, row, col, slot < USED, KEPT)
    lane = iota((KEPT, 128), 1)
    j = lane & (FEAT - 1)
    split_levels = core_index() == 1
    split_rows = lax.axis_index("lat") == 0
    ban_level = (j < WL) & (j != level)
    ban_row = (j >= F_Y) & (j < F_Y + WY) & ((j >= F_Y + SY) != (row >= SY))
    ban = jnp.where(ban_level, split_levels.astype(jnp.int32), jnp.where(ban_row, split_rows.astype(jnp.int32), 0))
    ban = jnp.where((lane & FEAT) == 0, ban, 0) == 1
    total = None
    for weight, bias, project in ((w_own, b_own, o_own), (w_sib, b_sib, o_sib)):
        q = (dot(xn, weight[0]) * HD**-0.5).astype(jnp.bfloat16)
        k = dot(xn, weight[1]).astype(jnp.bfloat16)
        v = dot(xn, weight[2]).astype(jnp.bfloat16)
        for pair in range(2):
            cols = slice(pair * 128, pair * 128 + 128)
            extra = dot(feat[:, :FEAT], bias[:, cols])
            extra = jnp.where(ban, NEG, extra).astype(jnp.bfloat16)
            mixed = pair_heads(q[:, cols], k[:, cols], v[:, cols], extra, feat)
            term = dot(mixed, project[cols, :])
            total = term if total is None else total + term
    store_halves(total, outs)


def gelu(x):
    return 0.5 * x * (1.0 + lax.erf(x * np.float32(np.sqrt(0.5))))


def mlp_kernel(mine, other, p0, p1, u0, u1, d0, d1, out):
    second = joined((p0, p1)) + branch_sum(mine, other)
    second = second.astype(jnp.bfloat16).astype(jnp.float32)
    xn = normalize(second)
    h0 = gelu(dot(xn, u0[...])).astype(jnp.bfloat16)
    h1 = gelu(dot(xn, u1[...])).astype(jnp.bfloat16)
    out[...] = (0.5 * second + dot(h0, d0[...]) + dot(h1, d1[...])).astype(jnp.bfloat16)


def sum_kernel(mine, other, *outs):
    total = mine[...].astype(jnp.float32) + other[...].astype(jnp.float32)
    for p in range(2):
        outs[p][...] = total[p * ROWS : (p + 1) * ROWS].astype(jnp.bfloat16)


def join_kernel(p0, p1, out):
    out[...] = joined((p0, p1)).astype(jnp.bfloat16)


def place_kernel(m0, m1, s0, s1, out):
    core = core_index()
    quad, slot, level, row, col = kept_place(iota((1, KEPT), 1))
    row, col = patch_place(quad, row, col)
    total = None
    for chosen, parts in ((core, (m0, m1)), (1 - core, (s0, s1))):
        place = (row * 12 + col) * 4 + real_level(level, chosen)
        place = jnp.where(slot < USED, place, -1)
        source = jnp.concatenate([part[...] for part in parts], axis=0)
        term = dot(one_hot(iota((PATCH, KEPT), 0) == place), source)
        total = term if total is None else total + term
    out[...] = total.reshape(out.shape).astype(jnp.bfloat16)


def call(kernel, outs, operands, flops, limit, table=False):
    shapes = [jax.ShapeDtypeStruct(s, jnp.bfloat16) for s in outs]
    moved = sum(o.size * o.dtype.itemsize for o in operands) + sum(2 * s.size for s in shapes)
    result = pl.pallas_call(
        kernel,
        out_shape=shapes,
        in_specs=[pl.BlockSpec(memory_space=pltpu.SMEM if table else pltpu.VMEM)] * len(operands),
        out_specs=[pl.BlockSpec(memory_space=pltpu.VMEM)] * len(shapes),
        compiler_params=pltpu.CompilerParams(vmem_limit_bytes=limit * MIB),
        cost_estimate=pl.CostEstimate(flops=flops, bytes_accessed=moved, transcendentals=0),
    )(*operands)
    return result if len(result) > 1 else result[0]


def tied(*values):
    return lax.optimization_barrier(values)


def body(counts, tokens, qkv_first, qkv_second, out_first, out_second, rel_tables, up_weight, down_weight):
    levels, rows, cols, width = tokens.shape
    turn = counts[1] // 2

    def move(value, target):
        return lax.ppermute(value, AXES, pairs(counts, target))

    def core_swap(value):
        return move(value, lambda a, b, m: (a, b, m ^ 1))

    def chip_swap(value):
        return move(value, lambda a, b, m: (a, b, m ^ 2))

    def out_to(value, dy, dx):
        return move(value, lambda a, b, m: (a + dy, b + dx, m ^ 2 if dx and (b + 1) % turn == 0 else m))

    def home(value, dy, dx):
        return move(value, lambda a, b, m: (a - dy, b - dx, m ^ 2 if dx and b % turn == 0 else m))

    half, piece = [(HALF, width)], [(ROWS, width)]
    heads, features = [(KEPT, 256)], [(FEAT, 256)]

    tok = tokens.transpose(1, 2, 0, 3).reshape(rows * cols, levels, width)
    w_first = qkv_first.transpose(1, 0, 2)
    w_second = qkv_second.transpose(1, 0, 2)

    f1 = core_swap(out_first)
    s1 = core_swap(out_second)
    w_sib = core_swap(w_second)
    bias1, bias2 = call(bias_kernel, features * 2, (rel_tables,), 5 * 10**9, 4, table=True)
    bias2_sib = core_swap(bias2)
    keep, give, base_a, base_b = call(first_kernel, heads * 2 + half * 2, (tok, w_first, bias1), 10**9, 16)
    keep, give, f1, s1, w_sib, bias2_sib = tied(keep, give, f1, s1, w_sib, bias2_sib)
    given, up_late, down_late = tied(core_swap(give), up_weight, down_weight)
    u1 = core_swap(up_late)
    d1 = core_swap(down_late)
    part_a, part_b = call(partial_kernel, half * 2, (keep, given, out_first, f1), 2 * 10**8, 8)
    other_a = chip_swap(part_a)
    other_b = chip_swap(part_b)
    diag, lon = call(residual_kernel, piece * 2, (part_a, other_a, base_a), 10**6, 8)
    diag, lon, part_b = tied(diag, lon, part_b)
    lat, own = call(residual_kernel, piece * 2, (part_b, other_b, base_b), 10**10, 8)
    diag = out_to(diag, 1, 1)
    lon = out_to(lon, 0, 1)
    lat = out_to(lat, 1, 0)

    xn_a = call(norm_kernel, half, (diag, lon), 10**10, 8)
    part_a, part_b = call(
        second_kernel,
        half * 2,
        (xn_a, lat, own, w_second, w_sib, out_second, s1, bias2, bias2_sib),
        10**9,
        16,
    )
    other_a = chip_swap(part_a)
    other_b = chip_swap(part_b)
    mlp = (up_weight, u1, down_weight, d1)
    part_a = call(mlp_kernel, half, (part_a, other_a, diag, lon, *mlp), 10**9, 20)
    part_a, part_b = tied(part_a, part_b)
    other_a = chip_swap(part_a)
    part_b = call(mlp_kernel, half, (part_b, other_b, lat, own, *mlp), 10**9, 20)
    other_b = chip_swap(part_b)
    diag, lon = call(sum_kernel, piece * 2, (part_a, other_a), 10**6, 8)
    diag, lon, part_b = tied(diag, lon, part_b)
    diag = home(diag, 1, 1)
    lon = home(lon, 0, 1)
    lat, own = call(sum_kernel, piece * 2, (part_b, other_b), 10**10, 8)
    lat = home(lat, 1, 0)
    mine_a = call(join_kernel, half, (diag, lon), 10**10, 8)
    mine_a, lat, own = tied(mine_a, lat, own)
    mine_b = call(join_kernel, half, (lat, own), 10**6, 8)
    result = call(
        place_kernel,
        [(rows * cols, levels, width)],
        (mine_a, mine_b, core_swap(mine_a), core_swap(mine_b)),
        2 * 10**8,
        12,
    )
    return result.reshape(rows, cols, levels, width).transpose(2, 0, 1, 3)


def solution(mesh):
    counts = tuple(mesh.shape[name] for name in AXES)
    return jax.shard_map(
        functools.partial(body, counts),
        mesh=mesh,
        in_specs=(
            P(None, "lat", "lon", None),
            P(None, None, "mp"),
            P(None, None, "mp"),
            P("mp", None),
            P("mp", None),
            P(None, "mp", None),
            P(None, "mp"),
            P("mp", None),
        ),
        out_specs=P(None, "lat", "lon", None),
        check_vma=False,
    )
```

```python
import functools

import jax
import jax.numpy as jnp
import numpy as np
from jax import lax
from jax.experimental import pallas as pl
from jax.experimental.pallas import tpu as pltpu
from jax.sharding import PartitionSpec as P

WL = 2
WY = 6
WX = 12
SY = 3
SX = 6
HD = 64
NEG = -1000000000.0
AXES = ("lat", "lon", "mp")
MIB = 1024 * 1024

USED = 36
ROWS = 40
KEPT = 4 * ROWS
HALF = 2 * ROWS
PATCH = 4 * WY * WX
WINDOW = WL * WY * WX
FEAT = 32
F_Y = 4
F_X = 10
F_PAD = 22


def pairs(counts, target):
    lats, lons, mps = counts
    result = []
    for a in range(lats):
        for b in range(lons):
            for m in range(mps):
                ta, tb, tm = target(a, b, m)
                dest = ((ta % lats) * lons + tb % lons) * mps + tm
                result.append(((a * lons + b) * mps + m, dest))
    return result


def dot(left, right):
    return jnp.dot(left, right, preferred_element_type=jnp.float32)


def dot_t(left, right):
    return lax.dot_general(left, right, (((1,), (1,)), ((), ())), preferred_element_type=jnp.float32)


def normalize(floats):
    center = floats - jnp.mean(floats, axis=-1, keepdims=True)
    spread = jnp.mean(center * center, axis=-1, keepdims=True)
    return (center * lax.rsqrt(spread + 1e-05)).astype(jnp.bfloat16)


def core_index():
    return lax.rem(lax.axis_index("mp"), 2)


def iota(shape, axis):
    return lax.broadcasted_iota(jnp.int32, shape, axis)


def one_hot(condition):
    return jnp.where(condition, 1.0, 0.0).astype(jnp.bfloat16)


def piece_place(slot):
    level = (slot * 57) >> 10
    rest = slot - level * 18
    row = (rest * 43) >> 8
    return level, row, rest - row * 6


def kept_place(index, core):
    piece = (index * 205) >> 13
    slot = index - piece * ROWS
    return (jnp.where(core == 0, piece, 3 - piece), slot) + piece_place(slot)


def real_level(level, core):
    return jnp.where(core == 0, 1 + level, 3 - 3 * level)


def patch_place(q, row, col):
    return row + 3 - 3 * (q & 1), col + 6 - 3 * (q & 2)


def bias_rows(table, block, pair):
    shape = (FEAT, 4 * FEAT)
    i, lane = iota(shape, 0), iota(shape, 1)
    j = lane & (FEAT - 1)
    kind = jnp.full(shape, 37, jnp.int32)
    kind = jnp.where((i < WL) & (j < WL), i - j + 1, kind)
    kind = jnp.where((i < WL) & (j == F_PAD), 38, kind)
    in_y = (i >= F_Y) & (i < F_Y + WY) & (j >= F_Y) & (j < F_Y + WY)
    kind = jnp.where(in_y, 3 + i - j + 5, kind)
    in_x = (i >= F_X) & (i < F_X + WX) & (j >= F_X) & (j < F_X + WX)
    kind = jnp.where(in_x, 14 + i - j + 11, kind)
    total = jnp.where(kind == 38, NEG, 0.0)
    for k in range(37):
        value = jnp.where(lane < HD, table[block, 2 * pair + 1, k], table[block, 2 * pair, k])
        total = jnp.where(kind == k, value, total)
    high = total.astype(jnp.bfloat16).astype(jnp.float32)
    return jnp.where((lane & FEAT) != 0, total - high, high).astype(jnp.bfloat16)


def bias_kernel(table, first, second):
    for block, out in enumerate((first, second)):
        for pair in range(2):
            out[:, pair * 128 : pair * 128 + 128] = bias_rows(table, block, pair)


def features(level, row, col, used, count):
    j = iota((count, 128), 1) & (FEAT - 1)
    hit = (j == level) | (j == F_Y + row) | (j == F_X + col)
    return one_hot(jnp.where(used, jnp.where(hit, 1, 0), jnp.where(j == F_PAD, 1, 0)) == 1)


def pair_heads(query, key, value, extra, key_feat):
    count = query.shape[0]
    low = iota(query.shape, 1) < HD
    none = jnp.zeros_like(query)
    upper = jnp.concatenate([jnp.where(low, query, none), jnp.where(low, none, extra)], axis=1)
    lower = jnp.concatenate([jnp.where(low, none, query), jnp.where(low, extra, none)], axis=1)
    scores = dot_t(jnp.concatenate([upper, lower], axis=0), jnp.concatenate([key, key_feat], axis=1))
    expo = jnp.exp(scores - jnp.max(scores, axis=-1, keepdims=True))
    scale = 1.0 / jnp.sum(expo, axis=-1, keepdims=True)
    mixed = dot(expo.astype(jnp.bfloat16), value) * scale
    return jnp.where(low, mixed[:count], mixed[count:]).astype(jnp.bfloat16)


def first_kernel(tokens, weight, bias, keep, give, *bases):
    core = core_index()
    floats = tokens[...].astype(jnp.float32).reshape(PATCH, -1)
    xn = normalize(floats)
    q = (dot(xn, weight[0]) * HD**-0.5).astype(jnp.bfloat16)
    k = dot(xn, weight[1]).astype(jnp.bfloat16)
    v = dot(xn, weight[2]).astype(jnp.bfloat16)
    index = iota((PATCH, 1), 0)
    level = (index * 911) >> 16
    order = one_hot(iota((PATCH, PATCH), 1) == (index - 72 * level) * 4 + level)
    q, k, v = (dot(order, part).astype(jnp.bfloat16) for part in (q, k, v))
    index = iota((WINDOW, 1), 0)
    level = (index * 911) >> 16
    rest = index - 72 * level
    row = (rest * 171) >> 11
    feat = features(level, row, rest - 12 * row, index >= 0, WINDOW)
    parts = []
    for pair in range(2):
        cols = slice(pair * 128, pair * 128 + 128)
        extra = dot(feat[:, :FEAT], bias[:, cols]).astype(jnp.bfloat16)
        halves = []
        for w in range(2):
            rows = slice(w * WINDOW, (w + 1) * WINDOW)
            halves.append(pair_heads(q[rows, cols], k[rows, cols], v[rows, cols], extra, feat))
        parts.append(jnp.concatenate(halves, axis=0))
    mixed = jnp.concatenate(parts, axis=1)
    lanes = iota((KEPT, PATCH), 1)
    for out, chosen in ((give, 1 - core), (keep, core)):
        quad, slot, level, row, col = kept_place(iota((KEPT, 1), 0), chosen)
        row, col = patch_place(quad, row, col)
        level = real_level(level, chosen)
        place = jnp.where(slot < USED, level * 72 + row * 12 + col, -1)
        out[...] = dot(one_hot(lanes == place), mixed).astype(jnp.bfloat16)
    place = jnp.where(slot < USED, (row * 12 + col) * 4 + level, -1)
    base = dot(one_hot(lanes == place), floats.astype(jnp.bfloat16)).astype(jnp.bfloat16)
    for h in range(2):
        bases[h][...] = base[h * HALF : (h + 1) * HALF]


def store_halves(total, outs):
    for h in range(2):
        outs[h][...] = total[h * HALF : (h + 1) * HALF].astype(jnp.bfloat16)


def partial_kernel(o0, o1, w0, w1, *outs):
    store_halves(dot(o0[...], w0[...]) + dot(o1[...], w1[...]), outs)


def branch_sum(mine, other):
    total = mine[...].astype(jnp.float32) + other[...].astype(jnp.float32)
    return total.astype(jnp.bfloat16).astype(jnp.float32)


def residual_kernel(mine, other, base, *outs):
    first = base[...].astype(jnp.float32) + branch_sum(mine, other)
    for p in range(2):
        outs[p][...] = first[p * ROWS : (p + 1) * ROWS].astype(jnp.bfloat16)


def joined(pieces):
    return jnp.concatenate([p[...].astype(jnp.float32) for p in pieces], axis=0)


def norm_kernel(p0, p1, out):
    out[...] = normalize(joined((p0, p1)))


def second_kernel(xn_a, p2, p3, w_own, w_sib, o_own, o_sib, b_own, b_sib, *outs):
    xn_b = normalize(joined((p2, p3))).astype(jnp.float32)
    xn = jnp.concatenate([xn_a[...].astype(jnp.float32), xn_b], axis=0).astype(jnp.bfloat16)
    core = core_index()
    quad, slot, level, row, col = kept_place(iota((KEPT, 1), 0), core)
    row, col = row + 3 * (quad & 1), col + 3 * (quad & 2)
    feat = features(level, row, col, slot < USED, KEPT)
    lane = iota((KEPT, 128), 1)
    j = lane & (FEAT - 1)
    split_levels = core == 1
    split_rows = lax.axis_index("lat") == jnp.where(core == 0, 0, lax.axis_size("lat") - 1)
    ban_level = (j < WL) & (j != level)
    ban_row = (j >= F_Y) & (j < F_Y + WY) & ((j >= F_Y + SY) != (row >= SY))
    ban = jnp.where(ban_level, split_levels.astype(jnp.int32), jnp.where(ban_row, split_rows.astype(jnp.int32), 0))
    ban = jnp.where((lane & FEAT) == 0, ban, 0) == 1
    total = None
    for weight, bias, project in ((w_own, b_own, o_own), (w_sib, b_sib, o_sib)):
        q = (dot(xn, weight[0]) * HD**-0.5).astype(jnp.bfloat16)
        k = dot(xn, weight[1]).astype(jnp.bfloat16)
        v = dot(xn, weight[2]).astype(jnp.bfloat16)
        for pair in range(2):
            cols = slice(pair * 128, pair * 128 + 128)
            extra = dot(feat[:, :FEAT], bias[:, cols])
            extra = jnp.where(ban, NEG, extra).astype(jnp.bfloat16)
            mixed = pair_heads(q[:, cols], k[:, cols], v[:, cols], extra, feat)
            term = dot(mixed, project[cols, :])
            total = term if total is None else total + term
    store_halves(total, outs)


def gelu(x):
    return 0.5 * x * (1.0 + lax.erf(x * np.float32(np.sqrt(0.5))))


def mlp_kernel(mine, other, p0, p1, u0, u1, d0, d1, out):
    second = joined((p0, p1)) + branch_sum(mine, other)
    second = second.astype(jnp.bfloat16).astype(jnp.float32)
    xn = normalize(second)
    h0 = gelu(dot(xn, u0[...])).astype(jnp.bfloat16)
    h1 = gelu(dot(xn, u1[...])).astype(jnp.bfloat16)
    out[...] = (0.5 * second + dot(h0, d0[...]) + dot(h1, d1[...])).astype(jnp.bfloat16)


def sum_kernel(mine, other, *outs):
    total = mine[...].astype(jnp.float32) + other[...].astype(jnp.float32)
    for p in range(2):
        outs[p][...] = total[p * ROWS : (p + 1) * ROWS].astype(jnp.bfloat16)


def join_kernel(p0, p1, out):
    out[...] = joined((p0, p1)).astype(jnp.bfloat16)


def place_kernel(m0, m1, s0, s1, out):
    core = core_index()
    total = None
    for chosen, parts in ((core, (m0, m1)), (1 - core, (s0, s1))):
        quad, slot, level, row, col = kept_place(iota((1, KEPT), 1), chosen)
        row, col = patch_place(quad, row, col)
        place = (row * 12 + col) * 4 + real_level(level, chosen)
        place = jnp.where(slot < USED, place, -1)
        source = jnp.concatenate([part[...] for part in parts], axis=0)
        term = dot(one_hot(iota((PATCH, KEPT), 0) == place), source)
        total = term if total is None else total + term
    out[...] = total.reshape(out.shape).astype(jnp.bfloat16)


def call(kernel, outs, operands, flops, limit, table=False):
    shapes = [jax.ShapeDtypeStruct(s, jnp.bfloat16) for s in outs]
    moved = sum(o.size * o.dtype.itemsize for o in operands) + sum(2 * s.size for s in shapes)
    result = pl.pallas_call(
        kernel,
        out_shape=shapes,
        in_specs=[pl.BlockSpec(memory_space=pltpu.SMEM if table else pltpu.VMEM)] * len(operands),
        out_specs=[pl.BlockSpec(memory_space=pltpu.VMEM)] * len(shapes),
        compiler_params=pltpu.CompilerParams(vmem_limit_bytes=limit * MIB),
        cost_estimate=pl.CostEstimate(flops=flops, bytes_accessed=moved, transcendentals=0),
    )(*operands)
    return result if len(result) > 1 else result[0]


def tied(*values):
    return lax.optimization_barrier(values)


def body(counts, tokens, qkv_first, qkv_second, out_first, out_second, rel_tables, up_weight, down_weight):
    levels, rows, cols, width = tokens.shape
    turn = counts[1] // 2

    def move(value, target):
        return lax.ppermute(value, AXES, pairs(counts, target))

    def core_swap(value):
        return move(value, lambda a, b, m: (a, b, m ^ 1))

    def chip_swap(value):
        return move(value, lambda a, b, m: (a, b, m ^ 2))

    def shift(value, dy, dx):
        def target(a, b, m):
            way = 1 - 2 * (m % 2)
            seam = dx and (b if way * dx < 0 else b + 1) % turn == 0
            return a + way * dy, b + way * dx, m ^ 2 if seam else m

        return move(value, target)

    def out_to(value, dy, dx):
        return shift(value, dy, dx)

    def home(value, dy, dx):
        return shift(value, -dy, -dx)

    half, piece = [(HALF, width)], [(ROWS, width)]
    heads, features = [(KEPT, 256)], [(FEAT, 256)]

    tok = tokens.transpose(1, 2, 0, 3).reshape(rows * cols, levels, width)
    w_first = qkv_first.transpose(1, 0, 2)
    w_second = qkv_second.transpose(1, 0, 2)

    f1 = core_swap(out_first)
    s1 = core_swap(out_second)
    w_sib = core_swap(w_second)
    bias1, bias2 = call(bias_kernel, features * 2, (rel_tables,), 5 * 10**9, 4, table=True)
    bias2_sib = core_swap(bias2)
    keep, give, base_a, base_b = call(first_kernel, heads * 2 + half * 2, (tok, w_first, bias1), 10**9, 16)
    keep, give, f1, s1, w_sib, bias2_sib = tied(keep, give, f1, s1, w_sib, bias2_sib)
    given, up_late, down_late = tied(core_swap(give), up_weight, down_weight)
    u1 = core_swap(up_late)
    d1 = core_swap(down_late)
    part_a, part_b = call(partial_kernel, half * 2, (keep, given, out_first, f1), 2 * 10**8, 8)
    other_a = chip_swap(part_a)
    other_b = chip_swap(part_b)
    diag, lon = call(residual_kernel, piece * 2, (part_a, other_a, base_a), 10**6, 8)
    diag, lon, part_b = tied(diag, lon, part_b)
    lat, own = call(residual_kernel, piece * 2, (part_b, other_b, base_b), 10**10, 8)
    diag = out_to(diag, 1, 1)
    lon = out_to(lon, 0, 1)
    lat = out_to(lat, 1, 0)

    xn_a = call(norm_kernel, half, (diag, lon), 10**10, 8)
    part_a, part_b = call(
        second_kernel,
        half * 2,
        (xn_a, lat, own, w_second, w_sib, out_second, s1, bias2, bias2_sib),
        10**9,
        16,
    )
    other_a = chip_swap(part_a)
    other_b = chip_swap(part_b)
    mlp = (up_weight, u1, down_weight, d1)
    part_a = call(mlp_kernel, half, (part_a, other_a, diag, lon, *mlp), 10**9, 20)
    part_a, part_b = tied(part_a, part_b)
    other_a = chip_swap(part_a)
    part_b = call(mlp_kernel, half, (part_b, other_b, lat, own, *mlp), 10**9, 20)
    other_b = chip_swap(part_b)
    diag, lon = call(sum_kernel, piece * 2, (part_a, other_a), 10**6, 8)
    diag, lon, part_b = tied(diag, lon, part_b)
    diag = home(diag, 1, 1)
    lon = home(lon, 0, 1)
    lat, own = call(sum_kernel, piece * 2, (part_b, other_b), 10**10, 8)
    lat = home(lat, 1, 0)
    mine_a = call(join_kernel, half, (diag, lon), 10**10, 8)
    mine_a, lat, own = tied(mine_a, lat, own)
    mine_b = call(join_kernel, half, (lat, own), 10**6, 8)
    result = call(
        place_kernel,
        [(rows * cols, levels, width)],
        (mine_a, mine_b, core_swap(mine_a), core_swap(mine_b)),
        2 * 10**8,
        12,
    )
    return result.reshape(rows, cols, levels, width).transpose(2, 0, 1, 3)


def solution(mesh):
    counts = tuple(mesh.shape[name] for name in AXES)
    return jax.shard_map(
        functools.partial(body, counts),
        mesh=mesh,
        in_specs=(
            P(None, "lat", "lon", None),
            P(None, None, "mp"),
            P(None, None, "mp"),
            P("mp", None),
            P("mp", None),
            P(None, "mp", None),
            P(None, "mp"),
            P("mp", None),
        ),
        out_specs=P(None, "lat", "lon", None),
        check_vma=False,
    )
```

```python
import functools

import jax
import jax.numpy as jnp
import numpy as np
from jax import lax
from jax.experimental import pallas as pl
from jax.experimental.pallas import tpu as pltpu
from jax.sharding import PartitionSpec as P

WL = 2
WY = 6
WX = 12
SY = 3
SX = 6
HD = 64
NEG = -1000000000.0
AXES = ("lat", "lon", "mp")
MIB = 1024 * 1024

USED = 36
ROWS = 40
KEPT = 4 * ROWS
HALF = 2 * ROWS
PATCH = 4 * WY * WX
WINDOW = WL * WY * WX
FEAT = 32
F_Y = 4
F_X = 10
F_PAD = 22


def pairs(counts, target):
    lats, lons, mps = counts
    result = []
    for a in range(lats):
        for b in range(lons):
            for m in range(mps):
                ta, tb, tm = target(a, b, m)
                dest = ((ta % lats) * lons + tb % lons) * mps + tm
                result.append(((a * lons + b) * mps + m, dest))
    return result


def dot(left, right):
    return jnp.dot(left, right, preferred_element_type=jnp.float32)


def dot_t(left, right):
    return lax.dot_general(left, right, (((1,), (1,)), ((), ())), preferred_element_type=jnp.float32)


def normalize(floats):
    center = floats - jnp.mean(floats, axis=-1, keepdims=True)
    spread = jnp.mean(center * center, axis=-1, keepdims=True)
    return (center * lax.rsqrt(spread + 1e-05)).astype(jnp.bfloat16)


def core_index():
    return lax.rem(lax.axis_index("mp"), 2)


def iota(shape, axis):
    return lax.broadcasted_iota(jnp.int32, shape, axis)


def one_hot(condition):
    return jnp.where(condition, 1.0, 0.0).astype(jnp.bfloat16)


def piece_place(slot):
    level = (slot * 57) >> 10
    rest = slot - level * 18
    row = (rest * 43) >> 8
    return level, row, rest - row * 6


def kept_place(index):
    quad = (index * 205) >> 13
    slot = index - quad * ROWS
    return (quad, slot) + piece_place(slot)


def real_level(level, core):
    return jnp.where(core == 0, 1 + level, 3 - 3 * level)


def patch_place(q, row, col):
    return row + 3 - 3 * (q & 1), col + 6 - 3 * (q & 2)


def bias_rows(table, block, pair):
    shape = (FEAT, 4 * FEAT)
    i, lane = iota(shape, 0), iota(shape, 1)
    j = lane & (FEAT - 1)
    kind = jnp.full(shape, 37, jnp.int32)
    kind = jnp.where((i < WL) & (j < WL), i - j + 1, kind)
    kind = jnp.where((i < WL) & (j == F_PAD), 38, kind)
    in_y = (i >= F_Y) & (i < F_Y + WY) & (j >= F_Y) & (j < F_Y + WY)
    kind = jnp.where(in_y, 3 + i - j + 5, kind)
    in_x = (i >= F_X) & (i < F_X + WX) & (j >= F_X) & (j < F_X + WX)
    kind = jnp.where(in_x, 14 + i - j + 11, kind)
    total = jnp.where(kind == 38, NEG, 0.0)
    for k in range(37):
        value = jnp.where(lane < HD, table[block, 2 * pair + 1, k], table[block, 2 * pair, k])
        total = jnp.where(kind == k, value, total)
    high = total.astype(jnp.bfloat16).astype(jnp.float32)
    return jnp.where((lane & FEAT) != 0, total - high, high).astype(jnp.bfloat16)


def bias_kernel(table, first, second):
    for block, out in enumerate((first, second)):
        for pair in range(2):
            out[:, pair * 128 : pair * 128 + 128] = bias_rows(table, block, pair)


def features(level, row, col, used, count):
    j = iota((count, 128), 1) & (FEAT - 1)
    hit = (j == level) | (j == F_Y + row) | (j == F_X + col)
    return one_hot(jnp.where(used, jnp.where(hit, 1, 0), jnp.where(j == F_PAD, 1, 0)) == 1)


def pair_heads(query, key, value, extra, key_feat):
    count = query.shape[0]
    low = iota(query.shape, 1) < HD
    none = jnp.zeros_like(query)
    upper = jnp.concatenate([jnp.where(low, query, none), jnp.where(low, none, extra)], axis=1)
    lower = jnp.concatenate([jnp.where(low, none, query), jnp.where(low, extra, none)], axis=1)
    scores = dot_t(jnp.concatenate([upper, lower], axis=0), jnp.concatenate([key, key_feat], axis=1))
    expo = jnp.exp(scores - jnp.max(scores, axis=-1, keepdims=True))
    scale = 1.0 / jnp.sum(expo, axis=-1, keepdims=True)
    mixed = dot(expo.astype(jnp.bfloat16), value) * scale
    return jnp.where(low, mixed[:count], mixed[count:]).astype(jnp.bfloat16)


def first_kernel(tokens, weight, bias, keep, give, *bases):
    core = core_index()
    floats = tokens[...].astype(jnp.float32).reshape(PATCH, -1)
    xn = normalize(floats)
    q = (dot(xn, weight[0]) * HD**-0.5).astype(jnp.bfloat16)
    k = dot(xn, weight[1]).astype(jnp.bfloat16)
    v = dot(xn, weight[2]).astype(jnp.bfloat16)
    index = iota((PATCH, 1), 0)
    level = (index * 911) >> 16
    order = one_hot(iota((PATCH, PATCH), 1) == (index - 72 * level) * 4 + level)
    q, k, v = (dot(order, part).astype(jnp.bfloat16) for part in (q, k, v))
    index = iota((WINDOW, 1), 0)
    level = (index * 911) >> 16
    rest = index - 72 * level
    row = (rest * 171) >> 11
    feat = features(level, row, rest - 12 * row, index >= 0, WINDOW)
    parts = []
    for pair in range(2):
        cols = slice(pair * 128, pair * 128 + 128)
        extra = dot(feat[:, :FEAT], bias[:, cols]).astype(jnp.bfloat16)
        halves = []
        for w in range(2):
            rows = slice(w * WINDOW, (w + 1) * WINDOW)
            halves.append(pair_heads(q[rows, cols], k[rows, cols], v[rows, cols], extra, feat))
        parts.append(jnp.concatenate(halves, axis=0))
    mixed = jnp.concatenate(parts, axis=1)
    quad, slot, level, row, col = kept_place(iota((KEPT, 1), 0))
    row, col = patch_place(quad, row, col)
    lanes = iota((KEPT, PATCH), 1)
    for out, chosen in ((keep, core), (give, 1 - core)):
        place = real_level(level, chosen) * 72 + row * 12 + col
        place = jnp.where(slot < USED, place, -1)
        out[...] = dot(one_hot(lanes == place), mixed).astype(jnp.bfloat16)
    place = (row * 12 + col) * 4 + real_level(level, core)
    place = jnp.where(slot < USED, place, -1)
    base = dot(one_hot(lanes == place), floats.astype(jnp.bfloat16)).astype(jnp.bfloat16)
    for h in range(2):
        bases[h][...] = base[h * HALF : (h + 1) * HALF]


def store_halves(total, outs):
    for h in range(2):
        outs[h][...] = total[h * HALF : (h + 1) * HALF].astype(jnp.bfloat16)


def partial_kernel(o0, o1, w0, w1, *outs):
    store_halves(dot(o0[...], w0[...]) + dot(o1[...], w1[...]), outs)


def branch_sum(mine, other):
    total = mine[...].astype(jnp.float32) + other[...].astype(jnp.float32)
    return total.astype(jnp.bfloat16).astype(jnp.float32)


def residual_kernel(mine, other, base, *outs):
    first = base[...].astype(jnp.float32) + branch_sum(mine, other)
    for p in range(2):
        outs[p][...] = first[p * ROWS : (p + 1) * ROWS].astype(jnp.bfloat16)


def joined(pieces):
    return jnp.concatenate([p[...].astype(jnp.float32) for p in pieces], axis=0)


def norm_kernel(p0, p1, out):
    out[...] = normalize(joined((p0, p1)))


def shifted_features(half):
    quad, slot, level, row, col = kept_place(iota((KEPT, 1), 0))
    row, col = row + 3 * (quad & 1), col + 3 * (quad & 2)
    feat = features(level, row, col, slot < USED, KEPT)
    rows = slice(half * HALF, (half + 1) * HALF)
    level, row = level[rows], row[rows]
    lane = iota((HALF, 128), 1)
    j = lane & (FEAT - 1)
    split_levels = core_index() == 1
    split_rows = lax.axis_index("lat") == 0
    ban_level = (j < WL) & (j != level)
    ban_row = (j >= F_Y) & (j < F_Y + WY) & ((j >= F_Y + SY) != (row >= SY))
    ban = jnp.where(ban_level, split_levels.astype(jnp.int32), jnp.where(ban_row, split_rows.astype(jnp.int32), 0))
    return feat, feat[rows], jnp.where((lane & FEAT) == 0, ban, 0) == 1


def half_attention(half, xn, keys, values, weights, projections, biases):
    feat, mine, ban = shifted_features(half)
    total = None
    for part in range(2):
        q = (dot(xn, weights[part][0]) * HD**-0.5).astype(jnp.bfloat16)
        for pair in range(2):
            cols = slice(pair * 128, pair * 128 + 128)
            extra = dot(mine[:, :FEAT], biases[part][:, cols])
            extra = jnp.where(ban, NEG, extra).astype(jnp.bfloat16)
            mixed = pair_heads(q[:, cols], keys[part][:, cols], values[part][:, cols], extra, feat)
            term = dot(mixed, projections[part][cols, :])
            total = term if total is None else total + term
    return total.astype(jnp.bfloat16)


def second_kernel(xn_a, p2, p3, w_own, w_sib, o_own, o_sib, b_own, b_sib, out, xn_out, k_out, v_out):
    xn_b = normalize(joined((p2, p3)))
    xn_out[...] = xn_b
    xn = jnp.concatenate([xn_a[...], xn_b], axis=0)
    keys, values = [], []
    for part, weight in enumerate((w_own, w_sib)):
        keys.append(dot(xn, weight[1]).astype(jnp.bfloat16))
        values.append(dot(xn, weight[2]).astype(jnp.bfloat16))
        k_out[part] = keys[part]
        v_out[part] = values[part]
    out[...] = half_attention(0, xn_a[...], keys, values, (w_own, w_sib), (o_own, o_sib), (b_own, b_sib))


def rest_kernel(xn_b, keys, values, w_own, w_sib, o_own, o_sib, b_own, b_sib, out):
    out[...] = half_attention(1, xn_b[...], keys, values, (w_own, w_sib), (o_own, o_sib), (b_own, b_sib))


def gelu(x):
    return 0.5 * x * (1.0 + lax.erf(x * np.float32(np.sqrt(0.5))))


def mlp_kernel(mine, other, p0, p1, u0, u1, d0, d1, out):
    second = joined((p0, p1)) + branch_sum(mine, other)
    second = second.astype(jnp.bfloat16).astype(jnp.float32)
    xn = normalize(second)
    h0 = gelu(dot(xn, u0[...])).astype(jnp.bfloat16)
    h1 = gelu(dot(xn, u1[...])).astype(jnp.bfloat16)
    out[...] = (0.5 * second + dot(h0, d0[...]) + dot(h1, d1[...])).astype(jnp.bfloat16)


def sum_kernel(mine, other, *outs):
    total = mine[...].astype(jnp.float32) + other[...].astype(jnp.float32)
    for p in range(2):
        outs[p][...] = total[p * ROWS : (p + 1) * ROWS].astype(jnp.bfloat16)


def join_kernel(p0, p1, out):
    out[...] = joined((p0, p1)).astype(jnp.bfloat16)


def place_kernel(m0, m1, s0, s1, out):
    core = core_index()
    quad, slot, level, row, col = kept_place(iota((1, KEPT), 1))
    row, col = patch_place(quad, row, col)
    total = None
    for chosen, parts in ((core, (m0, m1)), (1 - core, (s0, s1))):
        place = (row * 12 + col) * 4 + real_level(level, chosen)
        place = jnp.where(slot < USED, place, -1)
        source = jnp.concatenate([part[...] for part in parts], axis=0)
        term = dot(one_hot(iota((PATCH, KEPT), 0) == place), source)
        total = term if total is None else total + term
    out[...] = total.reshape(out.shape).astype(jnp.bfloat16)


def call(kernel, outs, operands, flops, limit, table=False):
    shapes = [jax.ShapeDtypeStruct(s, jnp.bfloat16) for s in outs]
    moved = sum(o.size * o.dtype.itemsize for o in operands) + sum(2 * s.size for s in shapes)
    result = pl.pallas_call(
        kernel,
        out_shape=shapes,
        in_specs=[pl.BlockSpec(memory_space=pltpu.SMEM if table else pltpu.VMEM)] * len(operands),
        out_specs=[pl.BlockSpec(memory_space=pltpu.VMEM)] * len(shapes),
        compiler_params=pltpu.CompilerParams(vmem_limit_bytes=limit * MIB),
        cost_estimate=pl.CostEstimate(flops=flops, bytes_accessed=moved, transcendentals=0),
    )(*operands)
    return result if len(result) > 1 else result[0]


def tied(*values):
    return lax.optimization_barrier(values)


def body(counts, tokens, qkv_first, qkv_second, out_first, out_second, rel_tables, up_weight, down_weight):
    levels, rows, cols, width = tokens.shape
    turn = counts[1] // 2

    def move(value, target):
        return lax.ppermute(value, AXES, pairs(counts, target))

    def core_swap(value):
        return move(value, lambda a, b, m: (a, b, m ^ 1))

    def chip_swap(value):
        return move(value, lambda a, b, m: (a, b, m ^ 2))

    def out_to(value, dy, dx):
        return move(value, lambda a, b, m: (a + dy, b + dx, m ^ 2 if dx and (b + 1) % turn == 0 else m))

    def home(value, dy, dx):
        return move(value, lambda a, b, m: (a - dy, b - dx, m ^ 2 if dx and b % turn == 0 else m))

    half, piece = [(HALF, width)], [(ROWS, width)]
    heads, features = [(KEPT, 256)], [(FEAT, 256)]

    tok = tokens.transpose(1, 2, 0, 3).reshape(rows * cols, levels, width)
    w_first = qkv_first.transpose(1, 0, 2)
    w_second = qkv_second.transpose(1, 0, 2)

    f1 = core_swap(out_first)
    s1 = core_swap(out_second)
    w_sib = core_swap(w_second)
    bias1, bias2 = call(bias_kernel, features * 2, (rel_tables,), 5 * 10**9, 4, table=True)
    bias2_sib = core_swap(bias2)
    keep, give, base_a, base_b = call(first_kernel, heads * 2 + half * 2, (tok, w_first, bias1), 10**9, 16)
    keep, give, f1, s1, w_sib, bias2_sib = tied(keep, give, f1, s1, w_sib, bias2_sib)
    given, up_late, down_late = tied(core_swap(give), up_weight, down_weight)
    u1 = core_swap(up_late)
    d1 = core_swap(down_late)
    part_a, part_b = call(partial_kernel, half * 2, (keep, given, out_first, f1), 2 * 10**8, 8)
    other_a = chip_swap(part_a)
    other_b = chip_swap(part_b)
    diag, lon = call(residual_kernel, piece * 2, (part_a, other_a, base_a), 10**6, 8)
    diag, lon, part_b = tied(diag, lon, part_b)
    lat, own = call(residual_kernel, piece * 2, (part_b, other_b, base_b), 10**10, 8)
    diag = out_to(diag, 1, 1)
    lon = out_to(lon, 0, 1)
    lat = out_to(lat, 1, 0)

    xn_a = call(norm_kernel, half, (diag, lon), 10**10, 8)
    own_sib = (w_second, w_sib, out_second, s1, bias2, bias2_sib)
    part_a, xn_b, keys, values = call(
        second_kernel, half * 2 + [(2, KEPT, 256)] * 2, (xn_a, lat, own, *own_sib), 10**9, 16
    )
    other_a = chip_swap(part_a)
    part_b = call(rest_kernel, half, (xn_b, keys, values, *own_sib), 10**10, 16)
    other_b = chip_swap(part_b)
    mlp = (up_weight, u1, down_weight, d1)
    part_a = call(mlp_kernel, half, (part_a, other_a, diag, lon, *mlp), 10**9, 20)
    part_a, part_b = tied(part_a, part_b)
    other_a = chip_swap(part_a)
    part_b = call(mlp_kernel, half, (part_b, other_b, lat, own, *mlp), 10**9, 20)
    other_b = chip_swap(part_b)
    diag, lon = call(sum_kernel, piece * 2, (part_a, other_a), 10**6, 8)
    diag, lon, part_b = tied(diag, lon, part_b)
    diag = home(diag, 1, 1)
    lon = home(lon, 0, 1)
    lat, own = call(sum_kernel, piece * 2, (part_b, other_b), 10**10, 8)
    lat = home(lat, 1, 0)
    mine_a = call(join_kernel, half, (diag, lon), 10**10, 8)
    mine_a, lat, own = tied(mine_a, lat, own)
    mine_b = call(join_kernel, half, (lat, own), 10**6, 8)
    result = call(
        place_kernel,
        [(rows * cols, levels, width)],
        (mine_a, mine_b, core_swap(mine_a), core_swap(mine_b)),
        2 * 10**8,
        12,
    )
    return result.reshape(rows, cols, levels, width).transpose(2, 0, 1, 3)


def solution(mesh):
    counts = tuple(mesh.shape[name] for name in AXES)
    return jax.shard_map(
        functools.partial(body, counts),
        mesh=mesh,
        in_specs=(
            P(None, "lat", "lon", None),
            P(None, None, "mp"),
            P(None, None, "mp"),
            P("mp", None),
            P("mp", None),
            P(None, "mp", None),
            P(None, "mp"),
            P("mp", None),
        ),
        out_specs=P(None, "lat", "lon", None),
        check_vma=False,
    )
```

```python
import functools

import jax
import jax.numpy as jnp
import numpy as np
from jax import lax
from jax.experimental import pallas as pl
from jax.experimental.pallas import tpu as pltpu
from jax.sharding import PartitionSpec as P

WL = 2
WY = 6
WX = 12
SY = 3
SX = 6
HD = 64
NEG = -1000000000.0
AXES = ("lat", "lon", "mp")
MIB = 1024 * 1024

USED = 36
ROWS = 40
KEPT = 4 * ROWS
HALF = 2 * ROWS
PATCH = 4 * WY * WX
WINDOW = WL * WY * WX
FEAT = 32
F_Y = 4
F_X = 10
F_PAD = 22


def pairs(counts, target):
    lats, lons, mps = counts
    result = []
    for a in range(lats):
        for b in range(lons):
            for m in range(mps):
                ta, tb, tm = target(a, b, m)
                dest = ((ta % lats) * lons + tb % lons) * mps + tm
                result.append(((a * lons + b) * mps + m, dest))
    return result


def dot(left, right):
    return jnp.dot(left, right, preferred_element_type=jnp.float32)


def dot_t(left, right):
    return lax.dot_general(left, right, (((1,), (1,)), ((), ())), preferred_element_type=jnp.float32)


def normalize(floats):
    center = floats - jnp.mean(floats, axis=-1, keepdims=True)
    spread = jnp.mean(center * center, axis=-1, keepdims=True)
    return (center * lax.rsqrt(spread + 1e-05)).astype(jnp.bfloat16)


def core_index():
    return lax.rem(lax.axis_index("mp"), 2)


def iota(shape, axis):
    return lax.broadcasted_iota(jnp.int32, shape, axis)


def one_hot(condition):
    return jnp.where(condition, 1.0, 0.0).astype(jnp.bfloat16)


def piece_place(slot):
    level = (slot * 57) >> 10
    rest = slot - level * 18
    row = (rest * 43) >> 8
    return level, row, rest - row * 6


def kept_place(index):
    quad = (index * 205) >> 13
    slot = index - quad * ROWS
    return (quad, slot) + piece_place(slot)


def real_level(level, core):
    return jnp.where(core == 0, 1 + level, 3 - 3 * level)


def patch_place(q, row, col):
    return row + 3 - 3 * (q & 1), col + 6 - 3 * (q & 2)


def bias_rows(table, block, pair):
    shape = (FEAT, 4 * FEAT)
    i, lane = iota(shape, 0), iota(shape, 1)
    j = lane & (FEAT - 1)
    kind = jnp.full(shape, 37, jnp.int32)
    kind = jnp.where((i < WL) & (j < WL), i - j + 1, kind)
    kind = jnp.where((i < WL) & (j == F_PAD), 38, kind)
    in_y = (i >= F_Y) & (i < F_Y + WY) & (j >= F_Y) & (j < F_Y + WY)
    kind = jnp.where(in_y, 3 + i - j + 5, kind)
    in_x = (i >= F_X) & (i < F_X + WX) & (j >= F_X) & (j < F_X + WX)
    kind = jnp.where(in_x, 14 + i - j + 11, kind)
    total = jnp.where(kind == 38, NEG, 0.0)
    for k in range(37):
        value = jnp.where(lane < HD, table[block, 2 * pair + 1, k], table[block, 2 * pair, k])
        total = jnp.where(kind == k, value, total)
    high = total.astype(jnp.bfloat16).astype(jnp.float32)
    return jnp.where((lane & FEAT) != 0, total - high, high).astype(jnp.bfloat16)


def bias_kernel(table, first, second):
    for block, out in enumerate((first, second)):
        for pair in range(2):
            out[:, pair * 128 : pair * 128 + 128] = bias_rows(table, block, pair)


def features(level, row, col, used, count):
    j = iota((count, 128), 1) & (FEAT - 1)
    hit = (j == level) | (j == F_Y + row) | (j == F_X + col)
    return one_hot(jnp.where(used, jnp.where(hit, 1, 0), jnp.where(j == F_PAD, 1, 0)) == 1)


def attend(parts, key_feat):
    low = iota(parts[0][0].shape, 1) < HD
    none = jnp.zeros_like(parts[0][0])
    count = none.shape[0]
    scores = []
    for query, key, _, extra in parts:
        upper = jnp.concatenate([jnp.where(low, query, none), jnp.where(low, none, extra)], axis=1)
        lower = jnp.concatenate([jnp.where(low, none, query), jnp.where(low, extra, none)], axis=1)
        both = jnp.concatenate([upper, lower], axis=0)
        scores.append(dot_t(both, jnp.concatenate([key, key_feat], axis=1)))
    expos, scales = [], []
    for score in scores:
        expo = jnp.exp(score - jnp.max(score, axis=-1, keepdims=True))
        expos.append(expo.astype(jnp.bfloat16))
        scales.append(1.0 / jnp.sum(expo, axis=-1, keepdims=True))
    results = []
    for (_, _, value, _), expo, scale in zip(parts, expos, scales):
        mixed = dot(expo, value) * scale
        results.append(jnp.where(low, mixed[:count], mixed[count:]).astype(jnp.bfloat16))
    return results


def pair_cols(pair):
    return slice(pair * 128, pair * 128 + 128)


def first_kernel(tokens, weight, bias, keep, give, *bases):
    core = core_index()
    floats = tokens[...].astype(jnp.float32).reshape(PATCH, -1)
    xn = normalize(floats)
    q = (dot(xn, weight[0]) * HD**-0.5).astype(jnp.bfloat16)
    k = dot(xn, weight[1]).astype(jnp.bfloat16)
    v = dot(xn, weight[2]).astype(jnp.bfloat16)
    index = iota((PATCH, 1), 0)
    level = (index * 911) >> 16
    order = one_hot(iota((PATCH, PATCH), 1) == (index - 72 * level) * 4 + level)
    q, k, v = (dot(order, part).astype(jnp.bfloat16) for part in (q, k, v))
    index = iota((WINDOW, 1), 0)
    level = (index * 911) >> 16
    rest = index - 72 * level
    row = (rest * 171) >> 11
    feat = features(level, row, rest - 12 * row, index >= 0, WINDOW)
    extra = dot(feat[:, :FEAT], bias[...]).astype(jnp.bfloat16)
    parts = []
    for w in range(2):
        rows = slice(w * WINDOW, (w + 1) * WINDOW)
        for pair in range(2):
            cols = pair_cols(pair)
            parts.append((q[rows, cols], k[rows, cols], v[rows, cols], extra[:, cols]))
    heads = attend(parts, feat)
    windows = [jnp.concatenate(heads[2 * w : 2 * w + 2], axis=1) for w in range(2)]
    mixed = jnp.concatenate(windows, axis=0)
    quad, slot, level, row, col = kept_place(iota((KEPT, 1), 0))
    row, col = patch_place(quad, row, col)
    lanes = iota((KEPT, PATCH), 1)
    for out, chosen in ((keep, core), (give, 1 - core)):
        place = real_level(level, chosen) * 72 + row * 12 + col
        place = jnp.where(slot < USED, place, -1)
        out[...] = dot(one_hot(lanes == place), mixed).astype(jnp.bfloat16)
    place = (row * 12 + col) * 4 + real_level(level, core)
    place = jnp.where(slot < USED, place, -1)
    base = dot(one_hot(lanes == place), floats.astype(jnp.bfloat16)).astype(jnp.bfloat16)
    for h in range(2):
        bases[h][...] = base[h * HALF : (h + 1) * HALF]


def store_halves(total, outs):
    for h in range(2):
        outs[h][...] = total[h * HALF : (h + 1) * HALF].astype(jnp.bfloat16)


def partial_kernel(o0, o1, w0, w1, *outs):
    store_halves(dot(o0[...], w0[...]) + dot(o1[...], w1[...]), outs)


def branch_sum(mine, other):
    total = mine[...].astype(jnp.float32) + other[...].astype(jnp.float32)
    return total.astype(jnp.bfloat16).astype(jnp.float32)


def residual_kernel(mine, other, base, *outs):
    first = base[...].astype(jnp.float32) + branch_sum(mine, other)
    for p in range(2):
        outs[p][...] = first[p * ROWS : (p + 1) * ROWS].astype(jnp.bfloat16)


def joined(pieces):
    return jnp.concatenate([p[...].astype(jnp.float32) for p in pieces], axis=0)


def norm_kernel(p0, p1, out):
    out[...] = normalize(joined((p0, p1)))


def second_kernel(xn_a, p2, p3, w_own, w_sib, o_own, o_sib, b_own, b_sib, *outs):
    xn_b = normalize(joined((p2, p3))).astype(jnp.float32)
    xn = jnp.concatenate([xn_a[...].astype(jnp.float32), xn_b], axis=0).astype(jnp.bfloat16)
    quad, slot, level, row, col = kept_place(iota((KEPT, 1), 0))
    row, col = row + 3 * (quad & 1), col + 3 * (quad & 2)
    feat = features(level, row, col, slot < USED, KEPT)
    lane = iota((KEPT, 128), 1)
    j = lane & (FEAT - 1)
    split_levels = core_index() == 1
    split_rows = lax.axis_index("lat") == 0
    ban_level = (j < WL) & (j != level)
    ban_row = (j >= F_Y) & (j < F_Y + WY) & ((j >= F_Y + SY) != (row >= SY))
    ban = jnp.where(ban_level, split_levels.astype(jnp.int32), jnp.where(ban_row, split_rows.astype(jnp.int32), 0))
    ban = jnp.where((lane & FEAT) == 0, ban, 0) == 1
    parts = []
    for weight, bias in ((w_own, b_own), (w_sib, b_sib)):
        q = (dot(xn, weight[0]) * HD**-0.5).astype(jnp.bfloat16)
        k = dot(xn, weight[1]).astype(jnp.bfloat16)
        v = dot(xn, weight[2]).astype(jnp.bfloat16)
        extra = dot(feat[:, :FEAT], bias[...])
        for pair in range(2):
            cols = pair_cols(pair)
            parts.append((q[:, cols], k[:, cols], v[:, cols], jnp.where(ban, NEG, extra[:, cols]).astype(jnp.bfloat16)))
    heads = attend(parts, feat)
    total = dot(jnp.concatenate(heads[:2], axis=1), o_own[...])
    total = total + dot(jnp.concatenate(heads[2:], axis=1), o_sib[...])
    outs[0][...] = total[ROWS : 3 * ROWS].astype(jnp.bfloat16)
    outs[1][...] = jnp.concatenate([total[:ROWS], total[3 * ROWS :]], axis=0).astype(jnp.bfloat16)


def gelu(x):
    return 0.5 * x * (1.0 + lax.erf(x * np.float32(np.sqrt(0.5))))


def mlp_kernel(mine, other, p0, p1, u0, u1, d0, d1, out):
    second = joined((p0, p1)) + branch_sum(mine, other)
    second = second.astype(jnp.bfloat16).astype(jnp.float32)
    xn = normalize(second)
    h0 = gelu(dot(xn, u0[...])).astype(jnp.bfloat16)
    h1 = gelu(dot(xn, u1[...])).astype(jnp.bfloat16)
    out[...] = (0.5 * second + dot(h0, d0[...]) + dot(h1, d1[...])).astype(jnp.bfloat16)


def sum_kernel(mine, other, *outs):
    total = mine[...].astype(jnp.float32) + other[...].astype(jnp.float32)
    for p in range(2):
        outs[p][...] = total[p * ROWS : (p + 1) * ROWS].astype(jnp.bfloat16)


def join_kernel(p0, p1, out):
    out[...] = joined((p0, p1)).astype(jnp.bfloat16)


def place_kernel(m0, m1, s0, s1, out):
    core = core_index()
    piece, slot, level, row, col = kept_place(iota((1, KEPT), 1))
    quad = jnp.where(piece < 2, piece + 1, jnp.where(piece == 2, 0, piece))
    row, col = patch_place(quad, row, col)
    total = None
    for chosen, parts in ((core, (m0, m1)), (1 - core, (s0, s1))):
        place = (row * 12 + col) * 4 + real_level(level, chosen)
        place = jnp.where(slot < USED, place, -1)
        source = jnp.concatenate([part[...] for part in parts], axis=0)
        term = dot(one_hot(iota((PATCH, KEPT), 0) == place), source)
        total = term if total is None else total + term
    out[...] = total.reshape(out.shape).astype(jnp.bfloat16)


def call(kernel, outs, operands, flops, limit, table=False):
    shapes = [jax.ShapeDtypeStruct(s, jnp.bfloat16) for s in outs]
    moved = sum(o.size * o.dtype.itemsize for o in operands) + sum(2 * s.size for s in shapes)
    result = pl.pallas_call(
        kernel,
        out_shape=shapes,
        in_specs=[pl.BlockSpec(memory_space=pltpu.SMEM if table else pltpu.VMEM)] * len(operands),
        out_specs=[pl.BlockSpec(memory_space=pltpu.VMEM)] * len(shapes),
        compiler_params=pltpu.CompilerParams(vmem_limit_bytes=limit * MIB),
        cost_estimate=pl.CostEstimate(flops=flops, bytes_accessed=moved, transcendentals=0),
    )(*operands)
    return result if len(result) > 1 else result[0]


def tied(*values):
    return lax.optimization_barrier(values)


def body(counts, tokens, qkv_first, qkv_second, out_first, out_second, rel_tables, up_weight, down_weight):
    levels, rows, cols, width = tokens.shape
    turn = counts[1] // 2

    def move(value, target):
        return lax.ppermute(value, AXES, pairs(counts, target))

    def core_swap(value):
        return move(value, lambda a, b, m: (a, b, m ^ 1))

    def chip_swap(value):
        return move(value, lambda a, b, m: (a, b, m ^ 2))

    def out_to(value, dy, dx):
        return move(value, lambda a, b, m: (a + dy, b + dx, m ^ 2 if dx and (b + 1) % turn == 0 else m))

    def home(value, dy, dx):
        return move(value, lambda a, b, m: (a - dy, b - dx, m ^ 2 if dx and b % turn == 0 else m))

    half, piece = [(HALF, width)], [(ROWS, width)]
    heads, features = [(KEPT, 256)], [(FEAT, 256)]

    tok = tokens.transpose(1, 2, 0, 3).reshape(rows * cols, levels, width)
    w_first = qkv_first.transpose(1, 0, 2)
    w_second = qkv_second.transpose(1, 0, 2)

    f1 = core_swap(out_first)
    s1 = core_swap(out_second)
    w_sib = core_swap(w_second)
    bias1, bias2 = call(bias_kernel, features * 2, (rel_tables,), 5 * 10**9, 4, table=True)
    bias2_sib = core_swap(bias2)
    keep, give, base_a, base_b = call(first_kernel, heads * 2 + half * 2, (tok, w_first, bias1), 10**9, 16)
    keep, give, f1, s1, w_sib, bias2_sib = tied(keep, give, f1, s1, w_sib, bias2_sib)
    given, up_late, down_late = tied(core_swap(give), up_weight, down_weight)
    u1 = core_swap(up_late)
    d1 = core_swap(down_late)
    part_a, part_b = call(partial_kernel, half * 2, (keep, given, out_first, f1), 2 * 10**8, 8)
    other_a = chip_swap(part_a)
    other_b = chip_swap(part_b)
    diag, lon = call(residual_kernel, piece * 2, (part_a, other_a, base_a), 10**6, 8)
    diag, lon, part_b = tied(diag, lon, part_b)
    lat, own = call(residual_kernel, piece * 2, (part_b, other_b, base_b), 10**10, 8)
    diag = out_to(diag, 1, 1)
    lon = out_to(lon, 0, 1)
    lat = out_to(lat, 1, 0)

    xn_a = call(norm_kernel, half, (diag, lon), 10**10, 8)
    part_a, part_b = call(
        second_kernel,
        half * 2,
        (xn_a, lat, own, w_second, w_sib, out_second, s1, bias2, bias2_sib),
        10**9,
        16,
    )
    other_a = chip_swap(part_a)
    other_b = chip_swap(part_b)
    mlp = (up_weight, u1, down_weight, d1)
    part_a = call(mlp_kernel, half, (part_a, other_a, lon, lat, *mlp), 10**9, 20)
    part_a, part_b = tied(part_a, part_b)
    other_a = chip_swap(part_a)
    part_b = call(mlp_kernel, half, (part_b, other_b, diag, own, *mlp), 10**9, 20)
    other_b = chip_swap(part_b)
    lon, lat = call(sum_kernel, piece * 2, (part_a, other_a), 10**6, 8)
    lon, lat, part_b = tied(lon, lat, part_b)
    lon = home(lon, 0, 1)
    lat = home(lat, 1, 0)
    diag, own = call(sum_kernel, piece * 2, (part_b, other_b), 10**10, 8)
    diag = home(diag, 1, 1)
    mine_a = call(join_kernel, half, (lon, lat), 10**10, 8)
    mine_a, diag, own = tied(mine_a, diag, own)
    mine_b = call(join_kernel, half, (diag, own), 10**6, 8)
    result = call(
        place_kernel,
        [(rows * cols, levels, width)],
        (mine_a, mine_b, core_swap(mine_a), core_swap(mine_b)),
        2 * 10**8,
        12,
    )
    return result.reshape(rows, cols, levels, width).transpose(2, 0, 1, 3)


def solution(mesh):
    counts = tuple(mesh.shape[name] for name in AXES)
    return jax.shard_map(
        functools.partial(body, counts),
        mesh=mesh,
        in_specs=(
            P(None, "lat", "lon", None),
            P(None, None, "mp"),
            P(None, None, "mp"),
            P("mp", None),
            P("mp", None),
            P(None, "mp", None),
            P(None, "mp"),
            P("mp", None),
        ),
        out_specs=P(None, "lat", "lon", None),
        check_vma=False,
    )
```

```python
import functools

import jax
import jax.numpy as jnp
import numpy as np
from jax import lax
from jax.experimental import pallas as pl
from jax.experimental.pallas import tpu as pltpu
from jax.sharding import PartitionSpec as P

WL = 2
WY = 6
WX = 12
SY = 3
SX = 6
HD = 64
NEG = -1000000000.0
AXES = ("lat", "lon", "mp")
MIB = 1024 * 1024

USED = 36
ROWS = 40
KEPT = 4 * ROWS
HALF = 2 * ROWS
PATCH = 4 * WY * WX
WINDOW = WL * WY * WX
FEAT = 32
F_Y = 4
F_X = 10
F_PAD = 22


def pairs(counts, target):
    lats, lons, mps = counts
    result = []
    for a in range(lats):
        for b in range(lons):
            for m in range(mps):
                ta, tb, tm = target(a, b, m)
                dest = ((ta % lats) * lons + tb % lons) * mps + tm
                result.append(((a * lons + b) * mps + m, dest))
    return result


def dot(left, right):
    return jnp.dot(left, right, preferred_element_type=jnp.float32)


def dot_t(left, right):
    return lax.dot_general(left, right, (((1,), (1,)), ((), ())), preferred_element_type=jnp.float32)


def normalize(floats):
    center = floats - jnp.mean(floats, axis=-1, keepdims=True)
    spread = jnp.mean(center * center, axis=-1, keepdims=True)
    return (center * lax.rsqrt(spread + 1e-05)).astype(jnp.bfloat16)


def core_index():
    return lax.rem(lax.axis_index("mp"), 2)


def iota(shape, axis):
    return lax.broadcasted_iota(jnp.int32, shape, axis)


def one_hot(condition):
    return jnp.where(condition, 1.0, 0.0).astype(jnp.bfloat16)


def piece_place(slot):
    level = (slot * 57) >> 10
    rest = slot - level * 18
    row = (rest * 43) >> 8
    return level, row, rest - row * 6


def kept_place(index):
    quad = (index * 205) >> 13
    slot = index - quad * ROWS
    return (quad, slot) + piece_place(slot)


def real_level(level, core):
    return jnp.where(core == 0, 1 + level, 3 - 3 * level)


def patch_place(q, row, col):
    return row + 3 - 3 * (q & 1), col + 6 - 3 * (q & 2)


def bias_rows(table, block, pair):
    shape = (FEAT, 4 * FEAT)
    i, lane = iota(shape, 0), iota(shape, 1)
    j = lane & (FEAT - 1)
    kind = jnp.full(shape, 37, jnp.int32)
    kind = jnp.where((i < WL) & (j < WL), i - j + 1, kind)
    kind = jnp.where((i < WL) & (j == F_PAD), 38, kind)
    in_y = (i >= F_Y) & (i < F_Y + WY) & (j >= F_Y) & (j < F_Y + WY)
    kind = jnp.where(in_y, 3 + i - j + 5, kind)
    in_x = (i >= F_X) & (i < F_X + WX) & (j >= F_X) & (j < F_X + WX)
    kind = jnp.where(in_x, 14 + i - j + 11, kind)
    total = jnp.where(kind == 38, NEG, 0.0)
    for k in range(37):
        value = jnp.where(lane < HD, table[block, 2 * pair + 1, k], table[block, 2 * pair, k])
        total = jnp.where(kind == k, value, total)
    high = total.astype(jnp.bfloat16).astype(jnp.float32)
    return jnp.where((lane & FEAT) != 0, total - high, high).astype(jnp.bfloat16)


def bias_kernel(block, *refs):
    for table, out in zip(refs[: len(refs) // 2], refs[len(refs) // 2 :]):
        for pair in range(2):
            out[:, pair * 128 : pair * 128 + 128] = bias_rows(table, block, pair)


def features(level, row, col, used, count):
    j = iota((count, 128), 1) & (FEAT - 1)
    hit = (j == level) | (j == F_Y + row) | (j == F_X + col)
    return one_hot(jnp.where(used, jnp.where(hit, 1, 0), jnp.where(j == F_PAD, 1, 0)) == 1)


def attend(parts, key_feat):
    low = iota(parts[0][0].shape, 1) < HD
    none = jnp.zeros_like(parts[0][0])
    count = none.shape[0]
    scores = []
    for query, key, _, extra in parts:
        upper = jnp.concatenate([jnp.where(low, query, none), jnp.where(low, none, extra)], axis=1)
        lower = jnp.concatenate([jnp.where(low, none, query), jnp.where(low, extra, none)], axis=1)
        both = jnp.concatenate([upper, lower], axis=0)
        scores.append(dot_t(both, jnp.concatenate([key, key_feat], axis=1)))
    expos, scales = [], []
    for score in scores:
        expo = jnp.exp(score - jnp.max(score, axis=-1, keepdims=True))
        expos.append(expo.astype(jnp.bfloat16))
        scales.append(1.0 / jnp.sum(expo, axis=-1, keepdims=True))
    results = []
    for (_, _, value, _), expo, scale in zip(parts, expos, scales):
        mixed = dot(expo, value) * scale
        results.append(jnp.where(low, mixed[:count], mixed[count:]).astype(jnp.bfloat16))
    return results


def pair_cols(pair):
    return slice(pair * 128, pair * 128 + 128)


def first_kernel(tokens, weight, bias, keep, give):
    core = core_index()
    floats = tokens[...].astype(jnp.float32).reshape(PATCH, -1)
    xn = normalize(floats)
    q = (dot(xn, weight[0]) * HD**-0.5).astype(jnp.bfloat16)
    k = dot(xn, weight[1]).astype(jnp.bfloat16)
    v = dot(xn, weight[2]).astype(jnp.bfloat16)
    index = iota((PATCH, 1), 0)
    level = (index * 911) >> 16
    order = one_hot(iota((PATCH, PATCH), 1) == (index - 72 * level) * 4 + level)
    q, k, v = (dot(order, part).astype(jnp.bfloat16) for part in (q, k, v))
    index = iota((WINDOW, 1), 0)
    level = (index * 911) >> 16
    rest = index - 72 * level
    row = (rest * 171) >> 11
    feat = features(level, row, rest - 12 * row, index >= 0, WINDOW)
    extra = dot(feat[:, :FEAT], bias[...]).astype(jnp.bfloat16)
    parts = []
    for w in range(2):
        rows = slice(w * WINDOW, (w + 1) * WINDOW)
        for pair in range(2):
            cols = pair_cols(pair)
            parts.append((q[rows, cols], k[rows, cols], v[rows, cols], extra[:, cols]))
    heads = attend(parts, feat)
    windows = [jnp.concatenate(heads[2 * w : 2 * w + 2], axis=1) for w in range(2)]
    mixed = jnp.concatenate(windows, axis=0)
    quad, slot, level, row, col = kept_place(iota((KEPT, 1), 0))
    row, col = patch_place(quad, row, col)
    lanes = iota((KEPT, PATCH), 1)
    for out, chosen in ((keep, core), (give, 1 - core)):
        place = real_level(level, chosen) * 72 + row * 12 + col
        place = jnp.where(slot < USED, place, -1)
        out[...] = dot(one_hot(lanes == place), mixed).astype(jnp.bfloat16)


def base_kernel(tokens, *outs):
    values = tokens[...].astype(jnp.float32).reshape(PATCH, -1).astype(jnp.bfloat16)
    quad, slot, level, row, col = kept_place(iota((KEPT, 1), 0))
    row, col = patch_place(quad, row, col)
    place = (row * 12 + col) * 4 + real_level(level, core_index())
    place = jnp.where(slot < USED, place, -1)
    store_halves(dot(one_hot(iota((KEPT, PATCH), 1) == place), values), outs)


def store_halves(total, outs):
    for h in range(2):
        outs[h][...] = total[h * HALF : (h + 1) * HALF].astype(jnp.bfloat16)


def partial_kernel(o0, o1, w0, w1, *outs):
    store_halves(dot(o0[...], w0[...]) + dot(o1[...], w1[...]), outs)


def branch_sum(mine, other):
    total = mine[...].astype(jnp.float32) + other[...].astype(jnp.float32)
    return total.astype(jnp.bfloat16).astype(jnp.float32)


def residual_kernel(mine, other, base, *outs):
    first = base[...].astype(jnp.float32) + branch_sum(mine, other)
    for p in range(2):
        outs[p][...] = first[p * ROWS : (p + 1) * ROWS].astype(jnp.bfloat16)


def joined(pieces):
    return jnp.concatenate([p[...].astype(jnp.float32) for p in pieces], axis=0)


def norm_kernel(p0, p1, out):
    out[...] = normalize(joined((p0, p1)))


def second_kernel(xn_a, p2, p3, w_own, w_sib, o_own, o_sib, b_own, b_sib, *outs):
    xn_b = normalize(joined((p2, p3))).astype(jnp.float32)
    xn = jnp.concatenate([xn_a[...].astype(jnp.float32), xn_b], axis=0).astype(jnp.bfloat16)
    quad, slot, level, row, col = kept_place(iota((KEPT, 1), 0))
    row, col = row + 3 * (quad & 1), col + 3 * (quad & 2)
    feat = features(level, row, col, slot < USED, KEPT)
    lane = iota((KEPT, 128), 1)
    j = lane & (FEAT - 1)
    split_levels = core_index() == 1
    split_rows = lax.axis_index("lat") == 0
    ban_level = (j < WL) & (j != level)
    ban_row = (j >= F_Y) & (j < F_Y + WY) & ((j >= F_Y + SY) != (row >= SY))
    ban = jnp.where(ban_level, split_levels.astype(jnp.int32), jnp.where(ban_row, split_rows.astype(jnp.int32), 0))
    ban = jnp.where((lane & FEAT) == 0, ban, 0) == 1
    parts = []
    for weight, bias in ((w_own, b_own), (w_sib, b_sib)):
        q = (dot(xn, weight[0]) * HD**-0.5).astype(jnp.bfloat16)
        k = dot(xn, weight[1]).astype(jnp.bfloat16)
        v = dot(xn, weight[2]).astype(jnp.bfloat16)
        extra = dot(feat[:, :FEAT], bias[...])
        for pair in range(2):
            cols = pair_cols(pair)
            parts.append((q[:, cols], k[:, cols], v[:, cols], jnp.where(ban, NEG, extra[:, cols]).astype(jnp.bfloat16)))
    heads = attend(parts, feat)
    total = dot(jnp.concatenate(heads[:2], axis=1), o_own[...])
    total = total + dot(jnp.concatenate(heads[2:], axis=1), o_sib[...])
    outs[0][...] = total[ROWS : 3 * ROWS].astype(jnp.bfloat16)
    outs[1][...] = jnp.concatenate([total[:ROWS], total[3 * ROWS :]], axis=0).astype(jnp.bfloat16)


def gelu(x):
    return 0.5 * x * (1.0 + lax.erf(x * np.float32(np.sqrt(0.5))))


def mlp_kernel(mine, other, p0, p1, u0, u1, d0, d1, out):
    second = joined((p0, p1)) + branch_sum(mine, other)
    second = second.astype(jnp.bfloat16).astype(jnp.float32)
    xn = normalize(second)
    h0 = gelu(dot(xn, u0[...])).astype(jnp.bfloat16)
    h1 = gelu(dot(xn, u1[...])).astype(jnp.bfloat16)
    out[...] = (0.5 * second + dot(h0, d0[...]) + dot(h1, d1[...])).astype(jnp.bfloat16)


def sum_kernel(mine, other, *outs):
    total = mine[...].astype(jnp.float32) + other[...].astype(jnp.float32)
    for p in range(2):
        outs[p][...] = total[p * ROWS : (p + 1) * ROWS].astype(jnp.bfloat16)


def join_kernel(p0, p1, out):
    out[...] = joined((p0, p1)).astype(jnp.bfloat16)


def place_kernel(m0, m1, s0, s1, out):
    core = core_index()
    piece, slot, level, row, col = kept_place(iota((1, KEPT), 1))
    quad = jnp.where(piece < 2, piece + 1, jnp.where(piece == 2, 0, piece))
    row, col = patch_place(quad, row, col)
    total = None
    for chosen, parts in ((core, (m0, m1)), (1 - core, (s0, s1))):
        place = (row * 12 + col) * 4 + real_level(level, chosen)
        place = jnp.where(slot < USED, place, -1)
        source = jnp.concatenate([part[...] for part in parts], axis=0)
        term = dot(one_hot(iota((PATCH, KEPT), 0) == place), source)
        total = term if total is None else total + term
    out[...] = total.reshape(out.shape).astype(jnp.bfloat16)


def call(kernel, outs, operands, flops, limit, table=False):
    shapes = [jax.ShapeDtypeStruct(s, jnp.bfloat16) for s in outs]
    moved = sum(o.size * o.dtype.itemsize for o in operands) + sum(2 * s.size for s in shapes)
    result = pl.pallas_call(
        kernel,
        out_shape=shapes,
        in_specs=[pl.BlockSpec(memory_space=pltpu.SMEM if table else pltpu.VMEM)] * len(operands),
        out_specs=[pl.BlockSpec(memory_space=pltpu.VMEM)] * len(shapes),
        compiler_params=pltpu.CompilerParams(vmem_limit_bytes=limit * MIB),
        cost_estimate=pl.CostEstimate(flops=flops, bytes_accessed=moved, transcendentals=0),
    )(*operands)
    return result if len(result) > 1 else result[0]


def tied(*values):
    return lax.optimization_barrier(values)


def body(counts, tokens, qkv_first, qkv_second, out_first, out_second, rel_tables, up_weight, down_weight):
    levels, rows, cols, width = tokens.shape
    turn = counts[1] // 2

    def move(value, target):
        return lax.ppermute(value, AXES, pairs(counts, target))

    def core_swap(value):
        return move(value, lambda a, b, m: (a, b, m ^ 1))

    def chip_swap(value):
        return move(value, lambda a, b, m: (a, b, m ^ 2))

    def out_to(value, dy, dx):
        return move(value, lambda a, b, m: (a + dy, b + dx, m ^ 2 if dx and (b + 1) % turn == 0 else m))

    def home(value, dy, dx):
        return move(value, lambda a, b, m: (a - dy, b - dx, m ^ 2 if dx and b % turn == 0 else m))

    half, piece = [(HALF, width)], [(ROWS, width)]
    heads, features = [(KEPT, 256)], [(FEAT, 256)]

    tok = tokens.transpose(1, 2, 0, 3).reshape(rows * cols, levels, width)
    w_first = qkv_first.transpose(1, 0, 2)
    w_second = qkv_second.transpose(1, 0, 2)

    f1 = core_swap(out_first)
    s1 = core_swap(out_second)
    w_sib = core_swap(w_second)
    s_table = core_swap(rel_tables)
    bias1 = call(functools.partial(bias_kernel, 0), features, (rel_tables,), 5 * 10**9, 4, table=True)
    keep, give = call(first_kernel, heads * 2, (tok, w_first, bias1), 10**9, 16)
    keep, give, f1, s1, w_sib, s_table = tied(keep, give, f1, s1, w_sib, s_table)
    keep, tok, rel_tables = tied(keep, tok, rel_tables)
    base_a, base_b = call(base_kernel, half * 2, (tok,), 10**9, 8)
    bias2, bias2_sib = call(
        functools.partial(bias_kernel, 1), features * 2, (rel_tables, s_table), 10**9, 4, table=True
    )
    given, up_late, down_late = tied(core_swap(give), up_weight, down_weight)
    u1 = core_swap(up_late)
    d1 = core_swap(down_late)
    part_a, part_b = call(partial_kernel, half * 2, (keep, given, out_first, f1), 2 * 10**8, 8)
    other_a = chip_swap(part_a)
    other_b = chip_swap(part_b)
    diag, lon = call(residual_kernel, piece * 2, (part_a, other_a, base_a), 10**6, 8)
    diag, lon, part_b = tied(diag, lon, part_b)
    lat, own = call(residual_kernel, piece * 2, (part_b, other_b, base_b), 10**10, 8)
    diag = out_to(diag, 1, 1)
    lon = out_to(lon, 0, 1)
    lat = out_to(lat, 1, 0)

    xn_a = call(norm_kernel, half, (diag, lon), 10**10, 8)
    part_a, part_b = call(
        second_kernel,
        half * 2,
        (xn_a, lat, own, w_second, w_sib, out_second, s1, bias2, bias2_sib),
        10**9,
        16,
    )
    other_a = chip_swap(part_a)
    other_b = chip_swap(part_b)
    mlp = (up_weight, u1, down_weight, d1)
    part_a = call(mlp_kernel, half, (part_a, other_a, lon, lat, *mlp), 10**9, 20)
    part_a, part_b = tied(part_a, part_b)
    other_a = chip_swap(part_a)
    part_b = call(mlp_kernel, half, (part_b, other_b, diag, own, *mlp), 10**9, 20)
    other_b = chip_swap(part_b)
    lon, lat = call(sum_kernel, piece * 2, (part_a, other_a), 10**6, 8)
    lon, lat, part_b = tied(lon, lat, part_b)
    lon = home(lon, 0, 1)
    lat = home(lat, 1, 0)
    diag, own = call(sum_kernel, piece * 2, (part_b, other_b), 10**10, 8)
    diag = home(diag, 1, 1)
    mine_a = call(join_kernel, half, (lon, lat), 10**10, 8)
    mine_a, diag, own = tied(mine_a, diag, own)
    mine_b = call(join_kernel, half, (diag, own), 10**6, 8)
    result = call(
        place_kernel,
        [(rows * cols, levels, width)],
        (mine_a, mine_b, core_swap(mine_a), core_swap(mine_b)),
        2 * 10**8,
        12,
    )
    return result.reshape(rows, cols, levels, width).transpose(2, 0, 1, 3)


def solution(mesh):
    counts = tuple(mesh.shape[name] for name in AXES)
    return jax.shard_map(
        functools.partial(body, counts),
        mesh=mesh,
        in_specs=(
            P(None, "lat", "lon", None),
            P(None, None, "mp"),
            P(None, None, "mp"),
            P("mp", None),
            P("mp", None),
            P(None, "mp", None),
            P(None, "mp"),
            P("mp", None),
        ),
        out_specs=P(None, "lat", "lon", None),
        check_vma=False,
    )
```

```python
import functools

import jax
import jax.numpy as jnp
import numpy as np
from jax import lax
from jax.experimental import pallas as pl
from jax.experimental.pallas import tpu as pltpu
from jax.sharding import PartitionSpec as P

WL = 2
WY = 6
WX = 12
SY = 3
SX = 6
HD = 64
NEG = -1000000000.0
AXES = ("lat", "lon", "mp")
MIB = 1024 * 1024

USED = 36
ROWS = 40
KEPT = 4 * ROWS
HALF = 2 * ROWS
PATCH = 4 * WY * WX
WINDOW = WL * WY * WX
FEAT = 32
F_Y = 4
F_X = 10
F_PAD = 22


def pairs(counts, target):
    lats, lons, mps = counts
    result = []
    for a in range(lats):
        for b in range(lons):
            for m in range(mps):
                found = target(a, b, m)
                if found is not None:
                    ta, tb, tm = found
                    dest = ((ta % lats) * lons + tb % lons) * mps + tm
                    result.append(((a * lons + b) * mps + m, dest))
    return result


def dot(left, right):
    return jnp.dot(left, right, preferred_element_type=jnp.float32)


def dot_t(left, right):
    return lax.dot_general(left, right, (((1,), (1,)), ((), ())), preferred_element_type=jnp.float32)


def normalize(floats):
    center = floats - jnp.mean(floats, axis=-1, keepdims=True)
    spread = jnp.mean(center * center, axis=-1, keepdims=True)
    return (center * lax.rsqrt(spread + 1e-05)).astype(jnp.bfloat16)


def core_index():
    return lax.rem(lax.axis_index("mp"), 2)


def iota(shape, axis):
    return lax.broadcasted_iota(jnp.int32, shape, axis)


def one_hot(condition):
    return jnp.where(condition, 1.0, 0.0).astype(jnp.bfloat16)


def piece_place(slot):
    level = (slot * 57) >> 10
    rest = slot - level * 18
    row = (rest * 43) >> 8
    return level, row, rest - row * 6


def kept_place(index):
    quad = (index * 205) >> 13
    slot = index - quad * ROWS
    return (quad, slot) + piece_place(slot)


def real_level(level, core):
    return jnp.where(core == 0, 1 + level, 3 - 3 * level)


def patch_place(q, row, col):
    return row + 3 - 3 * (q & 1), col + 6 - 3 * (q & 2)


def bias_rows(table, block, pair):
    shape = (FEAT, 4 * FEAT)
    i, lane = iota(shape, 0), iota(shape, 1)
    j = lane & (FEAT - 1)
    kind = jnp.full(shape, 37, jnp.int32)
    kind = jnp.where((i < WL) & (j < WL), i - j + 1, kind)
    kind = jnp.where((i < WL) & (j == F_PAD), 38, kind)
    in_y = (i >= F_Y) & (i < F_Y + WY) & (j >= F_Y) & (j < F_Y + WY)
    kind = jnp.where(in_y, 3 + i - j + 5, kind)
    in_x = (i >= F_X) & (i < F_X + WX) & (j >= F_X) & (j < F_X + WX)
    kind = jnp.where(in_x, 14 + i - j + 11, kind)
    total = jnp.where(kind == 38, NEG, 0.0)
    for k in range(37):
        value = jnp.where(lane < HD, table[block, 2 * pair + 1, k], table[block, 2 * pair, k])
        total = jnp.where(kind == k, value, total)
    high = total.astype(jnp.bfloat16).astype(jnp.float32)
    return jnp.where((lane & FEAT) != 0, total - high, high).astype(jnp.bfloat16)


def bias_kernel(block, *refs):
    for table, out in zip(refs[: len(refs) // 2], refs[len(refs) // 2 :]):
        for pair in range(2):
            out[:, pair * 128 : pair * 128 + 128] = bias_rows(table, block, pair)


def features(level, row, col, used, count):
    j = iota((count, 128), 1) & (FEAT - 1)
    hit = (j == level) | (j == F_Y + row) | (j == F_X + col)
    return one_hot(jnp.where(used, jnp.where(hit, 1, 0), jnp.where(j == F_PAD, 1, 0)) == 1)


def attend(parts, key_feat):
    low = iota(parts[0][0].shape, 1) < HD
    none = jnp.zeros_like(parts[0][0])
    count = none.shape[0]
    scores = []
    for query, key, _, extra in parts:
        upper = jnp.concatenate([jnp.where(low, query, none), jnp.where(low, none, extra)], axis=1)
        lower = jnp.concatenate([jnp.where(low, none, query), jnp.where(low, extra, none)], axis=1)
        both = jnp.concatenate([upper, lower], axis=0)
        scores.append(dot_t(both, jnp.concatenate([key, key_feat], axis=1)))
    expos, scales = [], []
    for score in scores:
        expo = jnp.exp(score - jnp.max(score, axis=-1, keepdims=True))
        expos.append(expo.astype(jnp.bfloat16))
        scales.append(1.0 / jnp.sum(expo, axis=-1, keepdims=True))
    results = []
    for (_, _, value, _), expo, scale in zip(parts, expos, scales):
        mixed = dot(expo, value) * scale
        results.append(jnp.where(low, mixed[:count], mixed[count:]).astype(jnp.bfloat16))
    return results


def pair_cols(pair):
    return slice(pair * 128, pair * 128 + 128)


def first_kernel(tokens, weight, bias, keep, give):
    core = core_index()
    floats = tokens[...].astype(jnp.float32).reshape(PATCH, -1)
    xn = normalize(floats)
    q = (dot(xn, weight[0]) * HD**-0.5).astype(jnp.bfloat16)
    k = dot(xn, weight[1]).astype(jnp.bfloat16)
    v = dot(xn, weight[2]).astype(jnp.bfloat16)
    index = iota((PATCH, 1), 0)
    level = (index * 911) >> 16
    order = one_hot(iota((PATCH, PATCH), 1) == (index - 72 * level) * 4 + level)
    q, k, v = (dot(order, part).astype(jnp.bfloat16) for part in (q, k, v))
    index = iota((WINDOW, 1), 0)
    level = (index * 911) >> 16
    rest = index - 72 * level
    row = (rest * 171) >> 11
    feat = features(level, row, rest - 12 * row, index >= 0, WINDOW)
    extra = dot(feat[:, :FEAT], bias[...]).astype(jnp.bfloat16)
    parts = []
    for w in range(2):
        rows = slice(w * WINDOW, (w + 1) * WINDOW)
        for pair in range(2):
            cols = pair_cols(pair)
            parts.append((q[rows, cols], k[rows, cols], v[rows, cols], extra[:, cols]))
    heads = attend(parts, feat)
    windows = [jnp.concatenate(heads[2 * w : 2 * w + 2], axis=1) for w in range(2)]
    mixed = jnp.concatenate(windows, axis=0)
    quad, slot, level, row, col = kept_place(iota((KEPT, 1), 0))
    row, col = patch_place(quad, row, col)
    lanes = iota((KEPT, PATCH), 1)
    for out, chosen in ((keep, core), (give, 1 - core)):
        place = real_level(level, chosen) * 72 + row * 12 + col
        place = jnp.where(slot < USED, place, -1)
        out[...] = dot(one_hot(lanes == place), mixed).astype(jnp.bfloat16)


def base_kernel(tokens, *outs):
    values = tokens[...].astype(jnp.float32).reshape(PATCH, -1).astype(jnp.bfloat16)
    quad, slot, level, row, col = kept_place(iota((KEPT, 1), 0))
    row, col = patch_place(quad, row, col)
    place = (row * 12 + col) * 4 + real_level(level, core_index())
    place = jnp.where(slot < USED, place, -1)
    store_halves(dot(one_hot(iota((KEPT, PATCH), 1) == place), values), outs)


def store_halves(total, outs):
    for h in range(2):
        outs[h][...] = total[h * HALF : (h + 1) * HALF].astype(jnp.bfloat16)


def partial_kernel(o0, o1, w0, w1, *outs):
    store_halves(dot(o0[...], w0[...]) + dot(o1[...], w1[...]), outs)


def branch_sum(mine, other):
    total = mine[...].astype(jnp.float32) + other[...].astype(jnp.float32)
    return total.astype(jnp.bfloat16).astype(jnp.float32)


def residual_kernel(mine, other, base, *outs):
    first = base[...].astype(jnp.float32) + branch_sum(mine, other)
    for p in range(2):
        outs[p][...] = first[p * ROWS : (p + 1) * ROWS].astype(jnp.bfloat16)


def joined(pieces):
    return jnp.concatenate([p[...].astype(jnp.float32) for p in pieces], axis=0)


def norm_kernel(p0, p1, out):
    out[...] = normalize(joined((p0, p1)))


def second_kernel(xn_a, p2, p3, w_own, w_sib, o_own, o_sib, b_own, b_sib, *outs):
    xn_b = normalize(joined((p2, p3))).astype(jnp.float32)
    xn = jnp.concatenate([xn_a[...].astype(jnp.float32), xn_b], axis=0).astype(jnp.bfloat16)
    quad, slot, level, row, col = kept_place(iota((KEPT, 1), 0))
    row, col = row + 3 * (quad & 1), col + 3 * (quad & 2)
    feat = features(level, row, col, slot < USED, KEPT)
    lane = iota((KEPT, 128), 1)
    j = lane & (FEAT - 1)
    split_levels = core_index() == 1
    split_rows = lax.axis_index("lat") == 0
    ban_level = (j < WL) & (j != level)
    ban_row = (j >= F_Y) & (j < F_Y + WY) & ((j >= F_Y + SY) != (row >= SY))
    ban = jnp.where(ban_level, split_levels.astype(jnp.int32), jnp.where(ban_row, split_rows.astype(jnp.int32), 0))
    ban = jnp.where((lane & FEAT) == 0, ban, 0) == 1
    parts = []
    for weight, bias in ((w_own, b_own), (w_sib, b_sib)):
        q = (dot(xn, weight[0]) * HD**-0.5).astype(jnp.bfloat16)
        k = dot(xn, weight[1]).astype(jnp.bfloat16)
        v = dot(xn, weight[2]).astype(jnp.bfloat16)
        extra = dot(feat[:, :FEAT], bias[...])
        for pair in range(2):
            cols = pair_cols(pair)
            parts.append((q[:, cols], k[:, cols], v[:, cols], jnp.where(ban, NEG, extra[:, cols]).astype(jnp.bfloat16)))
    heads = attend(parts, feat)
    total = dot(jnp.concatenate(heads[:2], axis=1), o_own[...])
    total = total + dot(jnp.concatenate(heads[2:], axis=1), o_sib[...])
    outs[0][...] = total[ROWS : 3 * ROWS].astype(jnp.bfloat16)
    outs[1][...] = jnp.concatenate([total[:ROWS], total[3 * ROWS :]], axis=0).astype(jnp.bfloat16)


def gelu(x):
    return 0.5 * x * (1.0 + lax.erf(x * np.float32(np.sqrt(0.5))))


def mlp_kernel(mine, other, p0, p1, u0, u1, d0, d1, out):
    second = joined((p0, p1)) + branch_sum(mine, other)
    second = second.astype(jnp.bfloat16).astype(jnp.float32)
    xn = normalize(second)
    h0 = gelu(dot(xn, u0[...])).astype(jnp.bfloat16)
    h1 = gelu(dot(xn, u1[...])).astype(jnp.bfloat16)
    out[...] = (0.5 * second + dot(h0, d0[...]) + dot(h1, d1[...])).astype(jnp.bfloat16)


def sum_kernel(mine, other, *outs):
    total = mine[...].astype(jnp.float32) + other[...].astype(jnp.float32)
    for p in range(2):
        outs[p][...] = total[p * ROWS : (p + 1) * ROWS].astype(jnp.bfloat16)


def join_kernel(lon, lat, out):
    out[...] = joined((lon, lat)).astype(jnp.bfloat16)


def join_rest_kernel(pair, diag, lon_around, lat_around, diag_around, own, out):
    around = joined((lon_around, lat_around, diag_around))
    total = jnp.concatenate([pair[...].astype(jnp.float32), joined((diag,))], axis=0) + around
    out[...] = jnp.concatenate([total, joined((own,))], axis=0).astype(jnp.bfloat16)


def place_kernel(mine, other, out):
    core = core_index()
    piece, slot, level, row, col = kept_place(iota((1, KEPT), 1))
    quad = jnp.where(piece < 2, piece + 1, jnp.where(piece == 2, 0, piece))
    row, col = patch_place(quad, row, col)
    total = None
    for chosen, rows in ((core, mine), (1 - core, other)):
        place = (row * 12 + col) * 4 + real_level(level, chosen)
        place = jnp.where(slot < USED, place, -1)
        term = dot(one_hot(iota((PATCH, KEPT), 0) == place), rows[...])
        total = term if total is None else total + term
    out[...] = total.reshape(out.shape).astype(jnp.bfloat16)


def call(kernel, outs, operands, flops, limit, table=False):
    shapes = [jax.ShapeDtypeStruct(s, jnp.bfloat16) for s in outs]
    moved = sum(o.size * o.dtype.itemsize for o in operands) + sum(2 * s.size for s in shapes)
    result = pl.pallas_call(
        kernel,
        out_shape=shapes,
        in_specs=[pl.BlockSpec(memory_space=pltpu.SMEM if table else pltpu.VMEM)] * len(operands),
        out_specs=[pl.BlockSpec(memory_space=pltpu.VMEM)] * len(shapes),
        compiler_params=pltpu.CompilerParams(vmem_limit_bytes=limit * MIB),
        cost_estimate=pl.CostEstimate(flops=flops, bytes_accessed=moved, transcendentals=0),
    )(*operands)
    return result if len(result) > 1 else result[0]


def tied(*values):
    return lax.optimization_barrier(values)


def body(counts, tokens, qkv_first, qkv_second, out_first, out_second, rel_tables, up_weight, down_weight):
    levels, rows, cols, width = tokens.shape
    turn = counts[1] // 2

    def move(value, target):
        return lax.ppermute(value, AXES, pairs(counts, target))

    def core_swap(value):
        return move(value, lambda a, b, m: (a, b, m ^ 1))

    def chip_swap(value):
        return move(value, lambda a, b, m: (a, b, m ^ 2))

    def out_to(value, dy, dx):
        return move(value, lambda a, b, m: (a + dy, b + dx, m ^ 2 if dx and (b + 1) % turn == 0 else m))

    def home(value, dy, dx):
        def edges(around):
            def target(a, b, m):
                if ((dy and a == 0) or (dx and b == 0)) != around:
                    return None
                return a - dy, b - dx, m ^ 2 if dx and b % turn == 0 else m

            return move(value, target)

        return edges(False), edges(True)

    half, piece = [(HALF, width)], [(ROWS, width)]
    heads, features = [(KEPT, 256)], [(FEAT, 256)]

    tok = tokens.transpose(1, 2, 0, 3).reshape(rows * cols, levels, width)
    w_first = qkv_first.transpose(1, 0, 2)
    w_second = qkv_second.transpose(1, 0, 2)

    f1 = core_swap(out_first)
    s1 = core_swap(out_second)
    w_sib = core_swap(w_second)
    s_table = core_swap(rel_tables)
    bias1 = call(functools.partial(bias_kernel, 0), features, (rel_tables,), 5 * 10**9, 4, table=True)
    keep, give = call(first_kernel, heads * 2, (tok, w_first, bias1), 10**9, 16)
    keep, give, f1, s1, w_sib = tied(keep, give, f1, s1, w_sib)
    keep, tok, rel_tables = tied(keep, tok, rel_tables)
    base_a, base_b = call(base_kernel, half * 2, (tok,), 10**9, 8)
    bias2, bias2_sib = call(
        functools.partial(bias_kernel, 1), features * 2, (rel_tables, s_table), 10**9, 4, table=True
    )
    given, up_late, down_late = tied(core_swap(give), up_weight, down_weight)
    u1 = core_swap(up_late)
    d1 = core_swap(down_late)
    part_a, part_b = call(partial_kernel, half * 2, (keep, given, out_first, f1), 2 * 10**8, 8)
    other_a = chip_swap(part_a)
    other_b = chip_swap(part_b)
    diag, lon = call(residual_kernel, piece * 2, (part_a, other_a, base_a), 10**6, 8)
    diag, lon, part_b = tied(diag, lon, part_b)
    lat, own = call(residual_kernel, piece * 2, (part_b, other_b, base_b), 10**10, 8)
    diag = out_to(diag, 1, 1)
    lon = out_to(lon, 0, 1)
    lat = out_to(lat, 1, 0)

    xn_a = call(norm_kernel, half, (diag, lon), 10**10, 8)
    part_a, part_b = call(
        second_kernel,
        half * 2,
        (xn_a, lat, own, w_second, w_sib, out_second, s1, bias2, bias2_sib),
        10**9,
        16,
    )
    other_a = chip_swap(part_a)
    other_b = chip_swap(part_b)
    mlp = (up_weight, u1, down_weight, d1)
    part_a = call(mlp_kernel, half, (part_a, other_a, lon, lat, *mlp), 10**9, 20)
    part_a, part_b = tied(part_a, part_b)
    other_a = chip_swap(part_a)
    part_b = call(mlp_kernel, half, (part_b, other_b, diag, own, *mlp), 10**9, 20)
    other_b = chip_swap(part_b)
    lon, lat = call(sum_kernel, piece * 2, (part_a, other_a), 10**6, 8)
    lon, lat, part_b = tied(lon, lat, part_b)
    lon = home(lon, 0, 1)
    lat = home(lat, 1, 0)
    diag, own = call(sum_kernel, piece * 2, (part_b, other_b), 10**10, 8)
    diag = home(diag, 1, 1)
    pair = call(join_kernel, half, (lon[0], lat[0]), 10**10, 8)
    pair, own, diag_in, *around = tied(pair, own, diag[0], lon[1], lat[1], diag[1])
    mine = call(join_rest_kernel, [(KEPT, width)], (pair, diag_in, *around, own), 10**6, 8)
    result = call(
        place_kernel, [(rows * cols, levels, width)], (mine, core_swap(mine)), 2 * 10**8, 12
    )
    return result.reshape(rows, cols, levels, width).transpose(2, 0, 1, 3)


def solution(mesh):
    counts = tuple(mesh.shape[name] for name in AXES)
    return jax.shard_map(
        functools.partial(body, counts),
        mesh=mesh,
        in_specs=(
            P(None, "lat", "lon", None),
            P(None, None, "mp"),
            P(None, None, "mp"),
            P("mp", None),
            P("mp", None),
            P(None, "mp", None),
            P(None, "mp"),
            P("mp", None),
        ),
        out_specs=P(None, "lat", "lon", None),
        check_vma=False,
    )
```

```python
import functools

import jax
import jax.numpy as jnp
import numpy as np
from jax import lax
from jax.experimental import pallas as pl
from jax.experimental.pallas import tpu as pltpu
from jax.sharding import PartitionSpec as P

WL = 2
WY = 6
WX = 12
SY = 3
SX = 6
HD = 64
NEG = -1000000000.0
AXES = ("lat", "lon", "mp")
MIB = 1024 * 1024

USED = 36
ROWS = 40
KEPT = 4 * ROWS
HALF = 2 * ROWS
PATCH = 4 * WY * WX
WINDOW = WL * WY * WX
FEAT = 32
F_Y = 4
F_X = 10
F_PAD = 22


def pairs(counts, target):
    lats, lons, mps = counts
    result = []
    for a in range(lats):
        for b in range(lons):
            for m in range(mps):
                ta, tb, tm = target(a, b, m)
                dest = ((ta % lats) * lons + tb % lons) * mps + tm
                result.append(((a * lons + b) * mps + m, dest))
    return result


def dot(left, right):
    return jnp.dot(left, right, preferred_element_type=jnp.float32)


def dot_t(left, right):
    return lax.dot_general(left, right, (((1,), (1,)), ((), ())), preferred_element_type=jnp.float32)


def normalize(floats):
    center = floats - jnp.mean(floats, axis=-1, keepdims=True)
    spread = jnp.mean(center * center, axis=-1, keepdims=True)
    return (center * lax.rsqrt(spread + 1e-05)).astype(jnp.bfloat16)


def core_index():
    return lax.rem(lax.axis_index("mp"), 2)


def iota(shape, axis):
    return lax.broadcasted_iota(jnp.int32, shape, axis)


def one_hot(condition):
    return jnp.where(condition, 1.0, 0.0).astype(jnp.bfloat16)


def piece_place(slot):
    level = (slot * 57) >> 10
    rest = slot - level * 18
    row = (rest * 43) >> 8
    return level, row, rest - row * 6


def kept_place(index):
    piece = (index * 205) >> 13
    slot = index - piece * ROWS
    return (piece ^ 2, slot) + piece_place(slot)


def real_level(level, core):
    return jnp.where(core == 0, 1 + level, 3 - 3 * level)


def patch_place(q, row, col):
    return row + 3 - 3 * (q & 1), col + 6 - 3 * (q & 2)


def bias_rows(table, block, pair):
    shape = (FEAT, 4 * FEAT)
    i, lane = iota(shape, 0), iota(shape, 1)
    j = lane & (FEAT - 1)
    kind = jnp.full(shape, 37, jnp.int32)
    kind = jnp.where((i < WL) & (j < WL), i - j + 1, kind)
    kind = jnp.where((i < WL) & (j == F_PAD), 38, kind)
    in_y = (i >= F_Y) & (i < F_Y + WY) & (j >= F_Y) & (j < F_Y + WY)
    kind = jnp.where(in_y, 3 + i - j + 5, kind)
    in_x = (i >= F_X) & (i < F_X + WX) & (j >= F_X) & (j < F_X + WX)
    kind = jnp.where(in_x, 14 + i - j + 11, kind)
    total = jnp.where(kind == 38, NEG, 0.0)
    for k in range(37):
        value = jnp.where(lane < HD, table[block, 2 * pair + 1, k], table[block, 2 * pair, k])
        total = jnp.where(kind == k, value, total)
    high = total.astype(jnp.bfloat16).astype(jnp.float32)
    return jnp.where((lane & FEAT) != 0, total - high, high).astype(jnp.bfloat16)


def bias_kernel(block, *refs):
    for table, out in zip(refs[: len(refs) // 2], refs[len(refs) // 2 :]):
        for pair in range(2):
            out[:, pair * 128 : pair * 128 + 128] = bias_rows(table, block, pair)


def features(level, row, col, used, count):
    j = iota((count, 128), 1) & (FEAT - 1)
    hit = (j == level) | (j == F_Y + row) | (j == F_X + col)
    return one_hot(jnp.where(used, jnp.where(hit, 1, 0), jnp.where(j == F_PAD, 1, 0)) == 1)


def attend(parts, key_feat):
    low = iota(parts[0][0].shape, 1) < HD
    none = jnp.zeros_like(parts[0][0])
    count = none.shape[0]
    scores = []
    for query, key, _, extra in parts:
        upper = jnp.concatenate([jnp.where(low, query, none), jnp.where(low, none, extra)], axis=1)
        lower = jnp.concatenate([jnp.where(low, none, query), jnp.where(low, extra, none)], axis=1)
        both = jnp.concatenate([upper, lower], axis=0)
        scores.append(dot_t(both, jnp.concatenate([key, key_feat], axis=1)))
    expos, scales = [], []
    for score in scores:
        expo = jnp.exp(score - jnp.max(score, axis=-1, keepdims=True))
        expos.append(expo.astype(jnp.bfloat16))
        scales.append(1.0 / jnp.sum(expo, axis=-1, keepdims=True))
    results = []
    for (_, _, value, _), expo, scale in zip(parts, expos, scales):
        mixed = dot(expo, value) * scale
        results.append(jnp.where(low, mixed[:count], mixed[count:]).astype(jnp.bfloat16))
    return results


def pair_cols(pair):
    return slice(pair * 128, pair * 128 + 128)


def first_kernel(tokens, weight, bias, keep, give):
    core = core_index()
    floats = tokens[...].astype(jnp.float32).reshape(PATCH, -1)
    xn = normalize(floats)
    q = (dot(xn, weight[0]) * HD**-0.5).astype(jnp.bfloat16)
    k = dot(xn, weight[1]).astype(jnp.bfloat16)
    v = dot(xn, weight[2]).astype(jnp.bfloat16)
    index = iota((PATCH, 1), 0)
    level = (index * 911) >> 16
    order = one_hot(iota((PATCH, PATCH), 1) == (index - 72 * level) * 4 + level)
    q, k, v = (dot(order, part).astype(jnp.bfloat16) for part in (q, k, v))
    index = iota((WINDOW, 1), 0)
    level = (index * 911) >> 16
    rest = index - 72 * level
    row = (rest * 171) >> 11
    feat = features(level, row, rest - 12 * row, index >= 0, WINDOW)
    extra = dot(feat[:, :FEAT], bias[...]).astype(jnp.bfloat16)
    parts = []
    for w in range(2):
        rows = slice(w * WINDOW, (w + 1) * WINDOW)
        for pair in range(2):
            cols = pair_cols(pair)
            parts.append((q[rows, cols], k[rows, cols], v[rows, cols], extra[:, cols]))
    heads = attend(parts, feat)
    windows = [jnp.concatenate(heads[2 * w : 2 * w + 2], axis=1) for w in range(2)]
    mixed = jnp.concatenate(windows, axis=0)
    quad, slot, level, row, col = kept_place(iota((KEPT, 1), 0))
    row, col = patch_place(quad, row, col)
    lanes = iota((KEPT, PATCH), 1)
    for out, chosen in ((keep, core), (give, 1 - core)):
        place = real_level(level, chosen) * 72 + row * 12 + col
        place = jnp.where(slot < USED, place, -1)
        out[...] = dot(one_hot(lanes == place), mixed).astype(jnp.bfloat16)


def base_kernel(tokens, *outs):
    values = tokens[...].astype(jnp.float32).reshape(PATCH, -1).astype(jnp.bfloat16)
    quad, slot, level, row, col = kept_place(iota((KEPT, 1), 0))
    row, col = patch_place(quad, row, col)
    place = (row * 12 + col) * 4 + real_level(level, core_index())
    place = jnp.where(slot < USED, place, -1)
    store_halves(dot(one_hot(iota((KEPT, PATCH), 1) == place), values), outs)


def store_halves(total, outs):
    for h in range(2):
        outs[h][...] = total[h * HALF : (h + 1) * HALF].astype(jnp.bfloat16)


def partial_kernel(o0, o1, w0, w1, *outs):
    store_halves(dot(o0[...], w0[...]) + dot(o1[...], w1[...]), outs)


def branch_sum(mine, other):
    total = mine[...].astype(jnp.float32) + other[...].astype(jnp.float32)
    return total.astype(jnp.bfloat16).astype(jnp.float32)


def residual_kernel(mine, other, base, *outs):
    first = base[...].astype(jnp.float32) + branch_sum(mine, other)
    for p in range(2):
        outs[p][...] = first[p * ROWS : (p + 1) * ROWS].astype(jnp.bfloat16)


def joined(pieces):
    return jnp.concatenate([p[...].astype(jnp.float32) for p in pieces], axis=0)


def norm_kernel(p0, p1, out):
    out[...] = normalize(joined((p0, p1)))


def second_kernel(xn_a, p2, p3, w_own, w_sib, o_own, o_sib, b_own, b_sib, *outs):
    xn_b = normalize(joined((p2, p3))).astype(jnp.float32)
    xn = jnp.concatenate([xn_a[...].astype(jnp.float32), xn_b], axis=0).astype(jnp.bfloat16)
    quad, slot, level, row, col = kept_place(iota((KEPT, 1), 0))
    row, col = row + 3 * (quad & 1), col + 3 * (quad & 2)
    feat = features(level, row, col, slot < USED, KEPT)
    lane = iota((KEPT, 128), 1)
    j = lane & (FEAT - 1)
    split_levels = core_index() == 1
    split_rows = lax.axis_index("lat") == 0
    ban_level = (j < WL) & (j != level)
    ban_row = (j >= F_Y) & (j < F_Y + WY) & ((j >= F_Y + SY) != (row >= SY))
    ban = jnp.where(ban_level, split_levels.astype(jnp.int32), jnp.where(ban_row, split_rows.astype(jnp.int32), 0))
    ban = jnp.where((lane & FEAT) == 0, ban, 0) == 1
    parts = []
    for weight, bias in ((w_own, b_own), (w_sib, b_sib)):
        q = (dot(xn, weight[0]) * HD**-0.5).astype(jnp.bfloat16)
        k = dot(xn, weight[1]).astype(jnp.bfloat16)
        v = dot(xn, weight[2]).astype(jnp.bfloat16)
        extra = dot(feat[:, :FEAT], bias[...])
        for pair in range(2):
            cols = pair_cols(pair)
            parts.append((q[:, cols], k[:, cols], v[:, cols], jnp.where(ban, NEG, extra[:, cols]).astype(jnp.bfloat16)))
    heads = attend(parts, feat)
    total = dot(jnp.concatenate(heads[:2], axis=1), o_own[...])
    total = total + dot(jnp.concatenate(heads[2:], axis=1), o_sib[...])
    outs[0][...] = total[ROWS : 3 * ROWS].astype(jnp.bfloat16)
    outs[1][...] = jnp.concatenate([total[:ROWS], total[3 * ROWS :]], axis=0).astype(jnp.bfloat16)


def gelu(x):
    return 0.5 * x * (1.0 + lax.erf(x * np.float32(np.sqrt(0.5))))


def mlp_kernel(mine, other, p0, p1, u0, u1, d0, d1, out):
    second = joined((p0, p1)) + branch_sum(mine, other)
    second = second.astype(jnp.bfloat16).astype(jnp.float32)
    xn = normalize(second)
    h0 = gelu(dot(xn, u0[...])).astype(jnp.bfloat16)
    h1 = gelu(dot(xn, u1[...])).astype(jnp.bfloat16)
    out[...] = (0.5 * second + dot(h0, d0[...]) + dot(h1, d1[...])).astype(jnp.bfloat16)


def sum_kernel(mine, other, *outs):
    total = mine[...].astype(jnp.float32) + other[...].astype(jnp.float32)
    for p in range(2):
        outs[p][...] = total[p * ROWS : (p + 1) * ROWS].astype(jnp.bfloat16)


def join_kernel(p0, p1, out):
    out[...] = joined((p0, p1)).astype(jnp.bfloat16)


def place_kernel(m0, m1, s0, s1, out):
    core = core_index()
    quad, slot, level, row, col = kept_place(iota((1, KEPT), 1))
    quad = jnp.where(quad == 2, 3, jnp.where(quad == 3, 0, jnp.where(quad == 0, 2, 1)))
    row, col = patch_place(quad, row, col)
    total = None
    for chosen, parts in ((core, (m0, m1)), (1 - core, (s0, s1))):
        place = (row * 12 + col) * 4 + real_level(level, chosen)
        place = jnp.where(slot < USED, place, -1)
        source = jnp.concatenate([part[...] for part in parts], axis=0)
        term = dot(one_hot(iota((PATCH, KEPT), 0) == place), source)
        total = term if total is None else total + term
    out[...] = total.reshape(out.shape).astype(jnp.bfloat16)


def call(kernel, outs, operands, flops, limit, table=False):
    shapes = [jax.ShapeDtypeStruct(s, jnp.bfloat16) for s in outs]
    moved = sum(o.size * o.dtype.itemsize for o in operands) + sum(2 * s.size for s in shapes)
    result = pl.pallas_call(
        kernel,
        out_shape=shapes,
        in_specs=[pl.BlockSpec(memory_space=pltpu.SMEM if table else pltpu.VMEM)] * len(operands),
        out_specs=[pl.BlockSpec(memory_space=pltpu.VMEM)] * len(shapes),
        compiler_params=pltpu.CompilerParams(vmem_limit_bytes=limit * MIB),
        cost_estimate=pl.CostEstimate(flops=flops, bytes_accessed=moved, transcendentals=0),
    )(*operands)
    return result if len(result) > 1 else result[0]


def tied(*values):
    return lax.optimization_barrier(values)


def body(counts, tokens, qkv_first, qkv_second, out_first, out_second, rel_tables, up_weight, down_weight):
    levels, rows, cols, width = tokens.shape
    turn = counts[1] // 2

    def move(value, target):
        return lax.ppermute(value, AXES, pairs(counts, target))

    def core_swap(value):
        return move(value, lambda a, b, m: (a, b, m ^ 1))

    def chip_swap(value):
        return move(value, lambda a, b, m: (a, b, m ^ 2))

    def out_to(value, dy, dx):
        return move(value, lambda a, b, m: (a + dy, b - dx, m ^ 2 if dx and b % turn == 0 else m))

    def home(value, dy, dx):
        return move(value, lambda a, b, m: (a - dy, b + dx, m ^ 2 if dx and (b + 1) % turn == 0 else m))

    half, piece = [(HALF, width)], [(ROWS, width)]
    heads, features = [(KEPT, 256)], [(FEAT, 256)]

    tok = tokens.transpose(1, 2, 0, 3).reshape(rows * cols, levels, width)
    w_first = qkv_first.transpose(1, 0, 2)
    w_second = qkv_second.transpose(1, 0, 2)

    f1 = core_swap(out_first)
    s1 = core_swap(out_second)
    w_sib = core_swap(w_second)
    s_table = core_swap(rel_tables)
    bias1 = call(functools.partial(bias_kernel, 0), features, (rel_tables,), 5 * 10**9, 4, table=True)
    keep, give = call(first_kernel, heads * 2, (tok, w_first, bias1), 10**9, 16)
    keep, give, f1, s1, w_sib = tied(keep, give, f1, s1, w_sib)
    keep, tok, rel_tables = tied(keep, tok, rel_tables)
    base_a, base_b = call(base_kernel, half * 2, (tok,), 10**9, 8)
    bias2, bias2_sib = call(
        functools.partial(bias_kernel, 1), features * 2, (rel_tables, s_table), 10**9, 4, table=True
    )
    given, up_late, down_late = tied(core_swap(give), up_weight, down_weight)
    u1 = core_swap(up_late)
    d1 = core_swap(down_late)
    part_a, part_b = call(partial_kernel, half * 2, (keep, given, out_first, f1), 2 * 10**8, 8)
    other_a = chip_swap(part_a)
    other_b = chip_swap(part_b)
    diag, lon = call(residual_kernel, piece * 2, (part_a, other_a, base_a), 10**6, 8)
    diag, lon, part_b = tied(diag, lon, part_b)
    lat, own = call(residual_kernel, piece * 2, (part_b, other_b, base_b), 10**10, 8)
    diag = out_to(diag, 1, 1)
    lon = out_to(lon, 0, 1)
    lat = out_to(lat, 1, 0)

    xn_a = call(norm_kernel, half, (diag, lon), 10**10, 8)
    part_a, part_b = call(
        second_kernel,
        half * 2,
        (xn_a, lat, own, w_second, w_sib, out_second, s1, bias2, bias2_sib),
        10**9,
        16,
    )
    other_a = chip_swap(part_a)
    other_b = chip_swap(part_b)
    mlp = (up_weight, u1, down_weight, d1)
    part_a = call(mlp_kernel, half, (part_a, other_a, lon, lat, *mlp), 10**9, 20)
    part_a, part_b = tied(part_a, part_b)
    other_a = chip_swap(part_a)
    part_b = call(mlp_kernel, half, (part_b, other_b, diag, own, *mlp), 10**9, 20)
    other_b = chip_swap(part_b)
    lon, lat = call(sum_kernel, piece * 2, (part_a, other_a), 10**6, 8)
    lon, lat, part_b = tied(lon, lat, part_b)
    lon = home(lon, 0, 1)
    lat = home(lat, 1, 0)
    diag, own = call(sum_kernel, piece * 2, (part_b, other_b), 10**10, 8)
    diag = home(diag, 1, 1)
    mine_a = call(join_kernel, half, (lon, lat), 10**10, 8)
    mine_a, diag, own = tied(mine_a, diag, own)
    mine_b = call(join_kernel, half, (diag, own), 10**6, 8)
    result = call(
        place_kernel,
        [(rows * cols, levels, width)],
        (mine_a, mine_b, core_swap(mine_a), core_swap(mine_b)),
        2 * 10**8,
        12,
    )
    return result.reshape(rows, cols, levels, width).transpose(2, 0, 1, 3)


def solution(mesh):
    counts = tuple(mesh.shape[name] for name in AXES)
    return jax.shard_map(
        functools.partial(body, counts),
        mesh=mesh,
        in_specs=(
            P(None, "lat", "lon", None),
            P(None, None, "mp"),
            P(None, None, "mp"),
            P("mp", None),
            P("mp", None),
            P(None, "mp", None),
            P(None, "mp"),
            P("mp", None),
        ),
        out_specs=P(None, "lat", "lon", None),
        check_vma=False,
    )
```

```python
import functools

import jax
import jax.numpy as jnp
import numpy as np
from jax import lax
from jax.experimental import pallas as pl
from jax.experimental.pallas import tpu as pltpu
from jax.sharding import PartitionSpec as P

WL = 2
WY = 6
WX = 12
SY = 3
SX = 6
HD = 64
NEG = -1000000000.0
AXES = ("lat", "lon", "mp")
MIB = 1024 * 1024

USED = 36
ROWS = 40
KEPT = 4 * ROWS
HALF = 2 * ROWS
PATCH = 4 * WY * WX
WINDOW = WL * WY * WX
FEAT = 32
F_Y = 4
F_X = 10
F_PAD = 22


def pairs(counts, target):
    lats, lons, mps = counts
    result = []
    for a in range(lats):
        for b in range(lons):
            for m in range(mps):
                ta, tb, tm = target(a, b, m)
                dest = ((ta % lats) * lons + tb % lons) * mps + tm
                result.append(((a * lons + b) * mps + m, dest))
    return result


def dot(left, right):
    return jnp.dot(left, right, preferred_element_type=jnp.float32)


def dot_t(left, right):
    return lax.dot_general(left, right, (((1,), (1,)), ((), ())), preferred_element_type=jnp.float32)


def normalize(floats):
    center = floats - jnp.mean(floats, axis=-1, keepdims=True)
    spread = jnp.mean(center * center, axis=-1, keepdims=True)
    return (center * lax.rsqrt(spread + 1e-05)).astype(jnp.bfloat16)


def core_index():
    return lax.rem(lax.axis_index("mp"), 2)


def iota(shape, axis):
    return lax.broadcasted_iota(jnp.int32, shape, axis)


def one_hot(condition):
    return jnp.where(condition, 1.0, 0.0).astype(jnp.bfloat16)


def piece_place(slot):
    level = (slot * 57) >> 10
    rest = slot - level * 18
    row = (rest * 43) >> 8
    return level, row, rest - row * 6


def kept_place(index):
    quad = (index * 205) >> 13
    slot = index - quad * ROWS
    return (quad, slot) + piece_place(slot)


def real_level(level, core):
    return jnp.where(core == 0, 1 + level, 3 - 3 * level)


def patch_place(q, row, col):
    return row + 3 - 3 * (q & 1), col + 6 - 3 * (q & 2)


def bias_rows(table, block, pair):
    shape = (FEAT, 4 * FEAT)
    i, lane = iota(shape, 0), iota(shape, 1)
    j = lane & (FEAT - 1)
    kind = jnp.full(shape, 37, jnp.int32)
    kind = jnp.where((i < WL) & (j < WL), i - j + 1, kind)
    kind = jnp.where((i < WL) & (j == F_PAD), 38, kind)
    in_y = (i >= F_Y) & (i < F_Y + WY) & (j >= F_Y) & (j < F_Y + WY)
    kind = jnp.where(in_y, 3 + i - j + 5, kind)
    in_x = (i >= F_X) & (i < F_X + WX) & (j >= F_X) & (j < F_X + WX)
    kind = jnp.where(in_x, 14 + i - j + 11, kind)
    total = jnp.where(kind == 38, NEG, 0.0)
    for k in range(37):
        value = jnp.where(lane < HD, table[block, 2 * pair + 1, k], table[block, 2 * pair, k])
        total = jnp.where(kind == k, value, total)
    high = total.astype(jnp.bfloat16).astype(jnp.float32)
    return jnp.where((lane & FEAT) != 0, total - high, high).astype(jnp.bfloat16)


def bias_kernel(block, table, out):
    for pair in range(2):
        out[:, pair * 128 : pair * 128 + 128] = bias_rows(table, block, pair)


def features(level, row, col, used, count):
    j = iota((count, 128), 1) & (FEAT - 1)
    hit = (j == level) | (j == F_Y + row) | (j == F_X + col)
    return one_hot(jnp.where(used, jnp.where(hit, 1, 0), jnp.where(j == F_PAD, 1, 0)) == 1)


def attend(parts, key_feat):
    low = iota(parts[0][0].shape, 1) < HD
    none = jnp.zeros_like(parts[0][0])
    count = none.shape[0]
    scores = []
    for query, key, _, extra in parts:
        upper = jnp.concatenate([jnp.where(low, query, none), jnp.where(low, none, extra)], axis=1)
        lower = jnp.concatenate([jnp.where(low, none, query), jnp.where(low, extra, none)], axis=1)
        both = jnp.concatenate([upper, lower], axis=0)
        scores.append(dot_t(both, jnp.concatenate([key, key_feat], axis=1)))
    expos, scales = [], []
    for score in scores:
        expo = jnp.exp(score - jnp.max(score, axis=-1, keepdims=True))
        expos.append(expo.astype(jnp.bfloat16))
        scales.append(1.0 / jnp.sum(expo, axis=-1, keepdims=True))
    results = []
    for (_, _, value, _), expo, scale in zip(parts, expos, scales):
        mixed = dot(expo, value) * scale
        results.append(jnp.where(low, mixed[:count], mixed[count:]).astype(jnp.bfloat16))
    return results


def pair_cols(pair):
    return slice(pair * 128, pair * 128 + 128)


def first_kernel(tokens, weight, bias, keep, give):
    core = core_index()
    floats = tokens[...].astype(jnp.float32).reshape(PATCH, -1)
    xn = normalize(floats)
    q = (dot(xn, weight[0]) * HD**-0.5).astype(jnp.bfloat16)
    k = dot(xn, weight[1]).astype(jnp.bfloat16)
    v = dot(xn, weight[2]).astype(jnp.bfloat16)
    index = iota((PATCH, 1), 0)
    level = (index * 911) >> 16
    order = one_hot(iota((PATCH, PATCH), 1) == (index - 72 * level) * 4 + level)
    q, k, v = (dot(order, part).astype(jnp.bfloat16) for part in (q, k, v))
    index = iota((WINDOW, 1), 0)
    level = (index * 911) >> 16
    rest = index - 72 * level
    row = (rest * 171) >> 11
    feat = features(level, row, rest - 12 * row, index >= 0, WINDOW)
    extra = dot(feat[:, :FEAT], bias[...]).astype(jnp.bfloat16)
    parts = []
    for w in range(2):
        rows = slice(w * WINDOW, (w + 1) * WINDOW)
        for pair in range(2):
            cols = pair_cols(pair)
            parts.append((q[rows, cols], k[rows, cols], v[rows, cols], extra[:, cols]))
    heads = attend(parts, feat)
    windows = [jnp.concatenate(heads[2 * w : 2 * w + 2], axis=1) for w in range(2)]
    mixed = jnp.concatenate(windows, axis=0)
    quad, slot, level, row, col = kept_place(iota((KEPT, 1), 0))
    row, col = patch_place(quad, row, col)
    lanes = iota((KEPT, PATCH), 1)
    for out, chosen in ((keep, core), (give, 1 - core)):
        place = real_level(level, chosen) * 72 + row * 12 + col
        place = jnp.where(slot < USED, place, -1)
        out[...] = dot(one_hot(lanes == place), mixed).astype(jnp.bfloat16)


def base_kernel(tokens, *outs):
    values = tokens[...].astype(jnp.float32).reshape(PATCH, -1).astype(jnp.bfloat16)
    quad, slot, level, row, col = kept_place(iota((KEPT, 1), 0))
    row, col = patch_place(quad, row, col)
    place = (row * 12 + col) * 4 + real_level(level, core_index())
    place = jnp.where(slot < USED, place, -1)
    store_halves(dot(one_hot(iota((KEPT, PATCH), 1) == place), values), outs)


def store_halves(total, outs):
    for h in range(2):
        outs[h][...] = total[h * HALF : (h + 1) * HALF].astype(jnp.bfloat16)


def partial_kernel(o0, o1, w0, w1, *outs):
    store_halves(dot(o0[...], w0[...]) + dot(o1[...], w1[...]), outs)


def branch_sum(mine, other):
    total = mine[...].astype(jnp.float32) + other[...].astype(jnp.float32)
    return total.astype(jnp.bfloat16).astype(jnp.float32)


def residual_kernel(mine, other, base, *outs):
    first = base[...].astype(jnp.float32) + branch_sum(mine, other)
    for p in range(2):
        outs[p][...] = first[p * ROWS : (p + 1) * ROWS].astype(jnp.bfloat16)


def joined(pieces):
    return jnp.concatenate([p[...].astype(jnp.float32) for p in pieces], axis=0)


def norm_kernel(p0, p1, out):
    out[...] = normalize(joined((p0, p1)))


def second_kernel(xn_a, p2, p3, w_own, w_sib, o_own, o_sib, b_own, b_sib, *outs):
    xn_b = normalize(joined((p2, p3))).astype(jnp.float32)
    xn = jnp.concatenate([xn_a[...].astype(jnp.float32), xn_b], axis=0).astype(jnp.bfloat16)
    quad, slot, level, row, col = kept_place(iota((KEPT, 1), 0))
    row, col = row + 3 * (quad & 1), col + 3 * (quad & 2)
    feat = features(level, row, col, slot < USED, KEPT)
    lane = iota((KEPT, 128), 1)
    j = lane & (FEAT - 1)
    split_levels = core_index() == 1
    split_rows = lax.axis_index("lat") == 0
    ban_level = (j < WL) & (j != level)
    ban_row = (j >= F_Y) & (j < F_Y + WY) & ((j >= F_Y + SY) != (row >= SY))
    ban = jnp.where(ban_level, split_levels.astype(jnp.int32), jnp.where(ban_row, split_rows.astype(jnp.int32), 0))
    ban = jnp.where((lane & FEAT) == 0, ban, 0) == 1
    parts = []
    for weight, bias in ((w_own, b_own), (w_sib, b_sib)):
        q = (dot(xn, weight[0]) * HD**-0.5).astype(jnp.bfloat16)
        k = dot(xn, weight[1]).astype(jnp.bfloat16)
        v = dot(xn, weight[2]).astype(jnp.bfloat16)
        extra = dot(feat[:, :FEAT], bias[...])
        for pair in range(2):
            cols = pair_cols(pair)
            parts.append((q[:, cols], k[:, cols], v[:, cols], jnp.where(ban, NEG, extra[:, cols]).astype(jnp.bfloat16)))
    heads = attend(parts, feat)
    total = dot(jnp.concatenate(heads[:2], axis=1), o_own[...])
    total = total + dot(jnp.concatenate(heads[2:], axis=1), o_sib[...])
    store_halves(total, outs)


def gelu(x):
    return 0.5 * x * (1.0 + lax.erf(x * np.float32(np.sqrt(0.5))))


def mlp_kernel(mine, other, p0, p1, u0, u1, d0, d1, out):
    second = joined((p0, p1)) + branch_sum(mine, other)
    second = second.astype(jnp.bfloat16).astype(jnp.float32)
    xn = normalize(second)
    h0 = gelu(dot(xn, u0[...])).astype(jnp.bfloat16)
    h1 = gelu(dot(xn, u1[...])).astype(jnp.bfloat16)
    out[...] = (0.5 * second + dot(h0, d0[...]) + dot(h1, d1[...])).astype(jnp.bfloat16)


def sum_kernel(mine, other, *outs):
    total = mine[...].astype(jnp.float32) + other[...].astype(jnp.float32)
    for p in range(2):
        outs[p][...] = total[p * ROWS : (p + 1) * ROWS].astype(jnp.bfloat16)


def join_kernel(p0, p1, out):
    out[...] = joined((p0, p1)).astype(jnp.bfloat16)


def place_kernel(m0, m1, s0, s1, out):
    core = core_index()
    quad, slot, level, row, col = kept_place(iota((1, KEPT), 1))
    row, col = patch_place(quad, row, col)
    total = None
    for chosen, parts in ((core, (m0, m1)), (1 - core, (s0, s1))):
        place = (row * 12 + col) * 4 + real_level(level, chosen)
        place = jnp.where(slot < USED, place, -1)
        source = jnp.concatenate([part[...] for part in parts], axis=0)
        term = dot(one_hot(iota((PATCH, KEPT), 0) == place), source)
        total = term if total is None else total + term
    out[...] = total.reshape(out.shape).astype(jnp.bfloat16)


def call(kernel, outs, operands, flops, limit, table=False):
    shapes = [jax.ShapeDtypeStruct(s, jnp.bfloat16) for s in outs]
    moved = sum(o.size * o.dtype.itemsize for o in operands) + sum(2 * s.size for s in shapes)
    result = pl.pallas_call(
        kernel,
        out_shape=shapes,
        in_specs=[pl.BlockSpec(memory_space=pltpu.SMEM if table else pltpu.VMEM)] * len(operands),
        out_specs=[pl.BlockSpec(memory_space=pltpu.VMEM)] * len(shapes),
        compiler_params=pltpu.CompilerParams(vmem_limit_bytes=limit * MIB),
        cost_estimate=pl.CostEstimate(flops=flops, bytes_accessed=moved, transcendentals=0),
    )(*operands)
    return result if len(result) > 1 else result[0]


def tied(*values):
    return lax.optimization_barrier(values)


def body(counts, tokens, qkv_first, qkv_second, out_first, out_second, rel_tables, up_weight, down_weight):
    levels, rows, cols, width = tokens.shape
    turn = counts[1] // 2

    def move(value, target):
        return lax.ppermute(value, AXES, pairs(counts, target))

    def core_swap(value):
        return move(value, lambda a, b, m: (a, b, m ^ 1))

    def chip_swap(value):
        return move(value, lambda a, b, m: (a, b, m ^ 2))

    def out_to(value, dy, dx):
        return move(value, lambda a, b, m: (a + dy, b + dx, m ^ 2 if dx and (b + 1) % turn == 0 else m))

    def home(value, dy, dx):
        return move(value, lambda a, b, m: (a - dy, b - dx, m ^ 2 if dx and b % turn == 0 else m))

    half, piece = [(HALF, width)], [(ROWS, width)]
    heads, features = [(KEPT, 256)], [(FEAT, 256)]

    tok = tokens.transpose(1, 2, 0, 3).reshape(rows * cols, levels, width)
    w_first = qkv_first.transpose(1, 0, 2)
    w_second = qkv_second.transpose(1, 0, 2)

    f1 = core_swap(out_first)
    s1 = core_swap(out_second)
    w_sib = core_swap(w_second)
    bias1 = call(functools.partial(bias_kernel, 0), features, (rel_tables,), 5 * 10**9, 4, table=True)
    keep, give = call(first_kernel, heads * 2, (tok, w_first, bias1), 10**9, 16)
    keep, give, f1, s1, w_sib = tied(keep, give, f1, s1, w_sib)
    keep, tok, rel_tables = tied(keep, tok, rel_tables)
    base_a, base_b = call(base_kernel, half * 2, (tok,), 10**9, 8)
    bias2 = call(functools.partial(bias_kernel, 1), features, (rel_tables,), 10**9, 4, table=True)
    bias2_sib = core_swap(bias2)
    given, up_late, down_late = tied(core_swap(give), up_weight, down_weight)
    u1 = core_swap(up_late)
    d1 = core_swap(down_late)
    part_a, part_b = call(partial_kernel, half * 2, (keep, given, out_first, f1), 2 * 10**8, 8)
    other_a = chip_swap(part_a)
    other_b = chip_swap(part_b)
    other_a, bias2_sib = tied(other_a, bias2_sib)
    diag, lon = call(residual_kernel, piece * 2, (part_a, other_a, base_a), 10**6, 8)
    diag, lon, part_b = tied(diag, lon, part_b)
    lat, own = call(residual_kernel, piece * 2, (part_b, other_b, base_b), 10**10, 8)
    diag = out_to(diag, 1, 1)
    lon = out_to(lon, 0, 1)
    lat = out_to(lat, 1, 0)

    xn_a = call(norm_kernel, half, (diag, lon), 10**10, 8)
    part_a, part_b = call(
        second_kernel,
        half * 2,
        (xn_a, lat, own, w_second, w_sib, out_second, s1, bias2, bias2_sib),
        10**9,
        16,
    )
    other_a = chip_swap(part_a)
    other_b = chip_swap(part_b)
    mlp = (up_weight, u1, down_weight, d1)
    part_a = call(mlp_kernel, half, (part_a, other_a, diag, lon, *mlp), 10**9, 20)
    part_a, part_b = tied(part_a, part_b)
    other_a = chip_swap(part_a)
    part_b = call(mlp_kernel, half, (part_b, other_b, lat, own, *mlp), 10**9, 20)
    other_b = chip_swap(part_b)
    diag, lon = call(sum_kernel, piece * 2, (part_a, other_a), 10**6, 8)
    diag, lon, part_b = tied(diag, lon, part_b)
    diag = home(diag, 1, 1)
    lon = home(lon, 0, 1)
    lat, own = call(sum_kernel, piece * 2, (part_b, other_b), 10**10, 8)
    lat = home(lat, 1, 0)
    mine_a = call(join_kernel, half, (diag, lon), 10**10, 8)
    mine_a, lat, own = tied(mine_a, lat, own)
    mine_b = call(join_kernel, half, (lat, own), 10**6, 8)
    result = call(
        place_kernel,
        [(rows * cols, levels, width)],
        (mine_a, mine_b, core_swap(mine_a), core_swap(mine_b)),
        2 * 10**8,
        12,
    )
    return result.reshape(rows, cols, levels, width).transpose(2, 0, 1, 3)


def solution(mesh):
    counts = tuple(mesh.shape[name] for name in AXES)
    return jax.shard_map(
        functools.partial(body, counts),
        mesh=mesh,
        in_specs=(
            P(None, "lat", "lon", None),
            P(None, None, "mp"),
            P(None, None, "mp"),
            P("mp", None),
            P("mp", None),
            P(None, "mp", None),
            P(None, "mp"),
            P("mp", None),
        ),
        out_specs=P(None, "lat", "lon", None),
        check_vma=False,
    )
```

```python
import functools

import jax
import jax.numpy as jnp
import numpy as np
from jax import lax
from jax.experimental import pallas as pl
from jax.experimental.pallas import tpu as pltpu
from jax.sharding import PartitionSpec as P

WL = 2
WY = 6
WX = 12
SY = 3
SX = 6
HD = 64
NEG = -1000000000.0
AXES = ("lat", "lon", "mp")
MIB = 1024 * 1024

USED = 36
ROWS = 40
KEPT = 4 * ROWS
HALF = 2 * ROWS
PATCH = 4 * WY * WX
WINDOW = WL * WY * WX
FEAT = 32
F_Y = 4
F_X = 10
F_PAD = 22


def pairs(counts, target):
    lats, lons, mps = counts
    result = []
    for a in range(lats):
        for b in range(lons):
            for m in range(mps):
                ta, tb, tm = target(a, b, m)
                dest = ((ta % lats) * lons + tb % lons) * mps + tm
                result.append(((a * lons + b) * mps + m, dest))
    return result


def dot(left, right):
    return jnp.dot(left, right, preferred_element_type=jnp.float32)


def dot_t(left, right):
    return lax.dot_general(left, right, (((1,), (1,)), ((), ())), preferred_element_type=jnp.float32)


def normalize(floats):
    center = floats - jnp.mean(floats, axis=-1, keepdims=True)
    spread = jnp.mean(center * center, axis=-1, keepdims=True)
    return (center * lax.rsqrt(spread + 1e-05)).astype(jnp.bfloat16)


def core_index():
    return lax.rem(lax.axis_index("mp"), 2)


def iota(shape, axis):
    return lax.broadcasted_iota(jnp.int32, shape, axis)


def one_hot(condition):
    return jnp.where(condition, 1.0, 0.0).astype(jnp.bfloat16)


def piece_place(slot):
    level = (slot * 57) >> 10
    rest = slot - level * 18
    row = (rest * 43) >> 8
    return level, row, rest - row * 6


def kept_place(index):
    quad = (index * 205) >> 13
    slot = index - quad * ROWS
    return (quad, slot) + piece_place(slot)


def real_level(level, core):
    return jnp.where(core == 0, 1 + level, 3 - 3 * level)


def patch_place(q, row, col):
    return row + 3 - 3 * (q & 1), col + 6 - 3 * (q & 2)


def bias_rows(table, block, pair):
    shape = (FEAT, 4 * FEAT)
    i, lane = iota(shape, 0), iota(shape, 1)
    j = lane & (FEAT - 1)
    kind = jnp.full(shape, 37, jnp.int32)
    kind = jnp.where((i < WL) & (j < WL), i - j + 1, kind)
    kind = jnp.where((i < WL) & (j == F_PAD), 38, kind)
    in_y = (i >= F_Y) & (i < F_Y + WY) & (j >= F_Y) & (j < F_Y + WY)
    kind = jnp.where(in_y, 3 + i - j + 5, kind)
    in_x = (i >= F_X) & (i < F_X + WX) & (j >= F_X) & (j < F_X + WX)
    kind = jnp.where(in_x, 14 + i - j + 11, kind)
    total = jnp.where(kind == 38, NEG, 0.0)
    for k in range(37):
        value = jnp.where(lane < HD, table[block, 2 * pair + 1, k], table[block, 2 * pair, k])
        total = jnp.where(kind == k, value, total)
    high = total.astype(jnp.bfloat16).astype(jnp.float32)
    return jnp.where((lane & FEAT) != 0, total - high, high).astype(jnp.bfloat16)


def bias_kernel(block, table, out):
    for pair in range(2):
        out[:, pair * 128 : pair * 128 + 128] = bias_rows(table, block, pair)


def features(level, row, col, used, count):
    j = iota((count, 128), 1) & (FEAT - 1)
    hit = (j == level) | (j == F_Y + row) | (j == F_X + col)
    return one_hot(jnp.where(used, jnp.where(hit, 1, 0), jnp.where(j == F_PAD, 1, 0)) == 1)


def attend(parts, key_feat):
    low = iota(parts[0][0].shape, 1) < HD
    none = jnp.zeros_like(parts[0][0])
    count = none.shape[0]
    scores = []
    for query, key, _, extra in parts:
        upper = jnp.concatenate([jnp.where(low, query, none), jnp.where(low, none, extra)], axis=1)
        lower = jnp.concatenate([jnp.where(low, none, query), jnp.where(low, extra, none)], axis=1)
        both = jnp.concatenate([upper, lower], axis=0)
        scores.append(dot_t(both, jnp.concatenate([key, key_feat], axis=1)))
    expos, scales = [], []
    for score in scores:
        expo = jnp.exp(score - jnp.max(score, axis=-1, keepdims=True))
        expos.append(expo.astype(jnp.bfloat16))
        scales.append(1.0 / jnp.sum(expo, axis=-1, keepdims=True))
    results = []
    for (_, _, value, _), expo, scale in zip(parts, expos, scales):
        mixed = dot(expo, value) * scale
        results.append(jnp.where(low, mixed[:count], mixed[count:]).astype(jnp.bfloat16))
    return results


def pair_cols(pair):
    return slice(pair * 128, pair * 128 + 128)


def first_kernel(tokens, weight, bias, keep, give):
    core = core_index()
    floats = tokens[...].astype(jnp.float32).reshape(PATCH, -1)
    xn = normalize(floats)
    q = (dot(xn, weight[0]) * HD**-0.5).astype(jnp.bfloat16)
    k = dot(xn, weight[1]).astype(jnp.bfloat16)
    v = dot(xn, weight[2]).astype(jnp.bfloat16)
    index = iota((PATCH, 1), 0)
    level = (index * 911) >> 16
    order = one_hot(iota((PATCH, PATCH), 1) == (index - 72 * level) * 4 + level)
    q, k, v = (dot(order, part).astype(jnp.bfloat16) for part in (q, k, v))
    index = iota((WINDOW, 1), 0)
    level = (index * 911) >> 16
    rest = index - 72 * level
    row = (rest * 171) >> 11
    feat = features(level, row, rest - 12 * row, index >= 0, WINDOW)
    extra = dot(feat[:, :FEAT], bias[...]).astype(jnp.bfloat16)
    parts = []
    for w in range(2):
        rows = slice(w * WINDOW, (w + 1) * WINDOW)
        for pair in range(2):
            cols = pair_cols(pair)
            parts.append((q[rows, cols], k[rows, cols], v[rows, cols], extra[:, cols]))
    heads = attend(parts, feat)
    windows = [jnp.concatenate(heads[2 * w : 2 * w + 2], axis=1) for w in range(2)]
    mixed = jnp.concatenate(windows, axis=0)
    quad, slot, level, row, col = kept_place(iota((KEPT, 1), 0))
    row, col = patch_place(quad, row, col)
    lanes = iota((KEPT, PATCH), 1)
    for out, chosen in ((keep, core), (give, 1 - core)):
        place = real_level(level, chosen) * 72 + row * 12 + col
        place = jnp.where(slot < USED, place, -1)
        out[...] = dot(one_hot(lanes == place), mixed).astype(jnp.bfloat16)


def base_kernel(tokens, *outs):
    values = tokens[...].astype(jnp.float32).reshape(PATCH, -1).astype(jnp.bfloat16)
    quad, slot, level, row, col = kept_place(iota((KEPT, 1), 0))
    row, col = patch_place(quad, row, col)
    place = (row * 12 + col) * 4 + real_level(level, core_index())
    place = jnp.where(slot < USED, place, -1)
    store_halves(dot(one_hot(iota((KEPT, PATCH), 1) == place), values), outs)


def store_halves(total, outs):
    for h in range(2):
        outs[h][...] = total[h * HALF : (h + 1) * HALF].astype(jnp.bfloat16)


def partial_kernel(o0, o1, w0, w1, *outs):
    store_halves(dot(o0[...], w0[...]) + dot(o1[...], w1[...]), outs)


def branch_sum(mine, other):
    total = mine[...].astype(jnp.float32) + other[...].astype(jnp.float32)
    return total.astype(jnp.bfloat16).astype(jnp.float32)


def residual_kernel(mine, other, base, *outs):
    first = base[...].astype(jnp.float32) + branch_sum(mine, other)
    for p in range(2):
        outs[p][...] = first[p * ROWS : (p + 1) * ROWS].astype(jnp.bfloat16)


def joined(pieces):
    return jnp.concatenate([p[...].astype(jnp.float32) for p in pieces], axis=0)


def norm_kernel(p0, p1, out):
    out[...] = normalize(joined((p0, p1)))


def second_kernel(xn_a, p2, p3, w_own, w_sib, o_own, o_sib, b_own, b_sib, *outs):
    xn_b = normalize(joined((p2, p3))).astype(jnp.float32)
    xn = jnp.concatenate([xn_a[...].astype(jnp.float32), xn_b], axis=0).astype(jnp.bfloat16)
    quad, slot, level, row, col = kept_place(iota((KEPT, 1), 0))
    row, col = row + 3 * (quad & 1), col + 3 * (quad & 2)
    feat = features(level, row, col, slot < USED, KEPT)
    lane = iota((KEPT, 128), 1)
    j = lane & (FEAT - 1)
    split_levels = core_index() == 1
    split_rows = lax.axis_index("lat") == 0
    ban_level = (j < WL) & (j != level)
    ban_row = (j >= F_Y) & (j < F_Y + WY) & ((j >= F_Y + SY) != (row >= SY))
    ban = jnp.where(ban_level, split_levels.astype(jnp.int32), jnp.where(ban_row, split_rows.astype(jnp.int32), 0))
    ban = jnp.where((lane & FEAT) == 0, ban, 0) == 1
    parts = []
    for weight, bias in ((w_own, b_own), (w_sib, b_sib)):
        q = (dot(xn, weight[0]) * HD**-0.5).astype(jnp.bfloat16)
        k = dot(xn, weight[1]).astype(jnp.bfloat16)
        v = dot(xn, weight[2]).astype(jnp.bfloat16)
        extra = dot(feat[:, :FEAT], bias[...])
        for pair in range(2):
            cols = pair_cols(pair)
            parts.append((q[:, cols], k[:, cols], v[:, cols], jnp.where(ban, NEG, extra[:, cols]).astype(jnp.bfloat16)))
    heads = attend(parts, feat)
    total = dot(jnp.concatenate(heads[:2], axis=1), o_own[...])
    total = total + dot(jnp.concatenate(heads[2:], axis=1), o_sib[...])
    store_halves(total, outs)


def gelu(x):
    return 0.5 * x * (1.0 + lax.erf(x * np.float32(np.sqrt(0.5))))


def mlp_kernel(mine, other, p0, p1, u0, u1, d0, d1, out):
    second = joined((p0, p1)) + branch_sum(mine, other)
    second = second.astype(jnp.bfloat16).astype(jnp.float32)
    xn = normalize(second)
    h0 = gelu(dot(xn, u0[...])).astype(jnp.bfloat16)
    h1 = gelu(dot(xn, u1[...])).astype(jnp.bfloat16)
    out[...] = (0.5 * second + dot(h0, d0[...]) + dot(h1, d1[...])).astype(jnp.bfloat16)


def sum_kernel(mine, other, *outs):
    total = mine[...].astype(jnp.float32) + other[...].astype(jnp.float32)
    for p in range(2):
        outs[p][...] = total[p * ROWS : (p + 1) * ROWS].astype(jnp.bfloat16)


def join_kernel(p0, p1, out):
    out[...] = joined((p0, p1)).astype(jnp.bfloat16)


def place_kernel(m0, m1, s0, s1, out, held, sems):
    core = core_index()
    quad, slot, level, row, col = kept_place(iota((1, KEPT), 1))
    row, col = patch_place(quad, row, col)
    places, sources = [], []
    for chosen, parts in ((core, (m0, m1)), (1 - core, (s0, s1))):
        place = (row * 12 + col) * 4 + real_level(level, chosen)
        places.append(jnp.where(slot < USED, place, -1))
        sources.append(jnp.concatenate([part[...] for part in parts], axis=0))
    count = PATCH // 2
    copies = []
    for h in range(2):
        index = iota((count, KEPT), 0) + h * count
        total = dot(one_hot(index == places[0]), sources[0]) + dot(one_hot(index == places[1]), sources[1])
        rows = pl.ds(h * count // 4, count // 4)
        held[rows] = total.reshape(count // 4, 4, -1).astype(jnp.bfloat16)
        copies.append(pltpu.make_async_copy(held.at[rows], out.at[rows], sems.at[h]))
        copies[h].start()
    for copy in copies:
        copy.wait()


def place_rows(shape, operands):
    return pl.pallas_call(
        place_kernel,
        out_shape=jax.ShapeDtypeStruct(shape, jnp.bfloat16),
        in_specs=[pl.BlockSpec(memory_space=pltpu.VMEM)] * 4,
        out_specs=pl.BlockSpec(memory_space=pl.ANY),
        scratch_shapes=[pltpu.VMEM(shape, jnp.bfloat16), pltpu.SemaphoreType.DMA((2,))],
        compiler_params=pltpu.CompilerParams(vmem_limit_bytes=12 * MIB),
        cost_estimate=pl.CostEstimate(flops=2 * 10**8, bytes_accessed=2 * 10**6, transcendentals=0),
    )(*operands)


def call(kernel, outs, operands, flops, limit, table=False):
    shapes = [jax.ShapeDtypeStruct(s, jnp.bfloat16) for s in outs]
    moved = sum(o.size * o.dtype.itemsize for o in operands) + sum(2 * s.size for s in shapes)
    result = pl.pallas_call(
        kernel,
        out_shape=shapes,
        in_specs=[pl.BlockSpec(memory_space=pltpu.SMEM if table else pltpu.VMEM)] * len(operands),
        out_specs=[pl.BlockSpec(memory_space=pltpu.VMEM)] * len(shapes),
        compiler_params=pltpu.CompilerParams(vmem_limit_bytes=limit * MIB),
        cost_estimate=pl.CostEstimate(flops=flops, bytes_accessed=moved, transcendentals=0),
    )(*operands)
    return result if len(result) > 1 else result[0]


def tied(*values):
    return lax.optimization_barrier(values)


def body(counts, tokens, qkv_first, qkv_second, out_first, out_second, rel_tables, up_weight, down_weight):
    levels, rows, cols, width = tokens.shape
    turn = counts[1] // 2

    def move(value, target):
        return lax.ppermute(value, AXES, pairs(counts, target))

    def core_swap(value):
        return move(value, lambda a, b, m: (a, b, m ^ 1))

    def chip_swap(value):
        return move(value, lambda a, b, m: (a, b, m ^ 2))

    def out_to(value, dy, dx):
        return move(value, lambda a, b, m: (a + dy, b + dx, m ^ 2 if dx and (b + 1) % turn == 0 else m))

    def home(value, dy, dx):
        return move(value, lambda a, b, m: (a - dy, b - dx, m ^ 2 if dx and b % turn == 0 else m))

    half, piece = [(HALF, width)], [(ROWS, width)]
    heads, features = [(KEPT, 256)], [(FEAT, 256)]

    tok = tokens.transpose(1, 2, 0, 3).reshape(rows * cols, levels, width)
    w_first = qkv_first.transpose(1, 0, 2)
    w_second = qkv_second.transpose(1, 0, 2)

    f1 = core_swap(out_first)
    s1 = core_swap(out_second)
    w_sib = core_swap(w_second)
    bias1 = call(functools.partial(bias_kernel, 0), features, (rel_tables,), 5 * 10**9, 4, table=True)
    keep, give = call(first_kernel, heads * 2, (tok, w_first, bias1), 10**9, 16)
    keep, give, f1 = tied(keep, give, f1)
    keep, tok, rel_tables = tied(keep, tok, rel_tables)
    base_a, base_b = call(base_kernel, half * 2, (tok,), 10**9, 8)
    bias2 = call(functools.partial(bias_kernel, 1), features, (rel_tables,), 10**9, 4, table=True)
    bias2_sib = core_swap(bias2)
    given, up_late, down_late, s1, w_sib = tied(core_swap(give), up_weight, down_weight, s1, w_sib)
    u1 = core_swap(up_late)
    d1 = core_swap(down_late)
    part_a, part_b = call(partial_kernel, half * 2, (keep, given, out_first, f1), 2 * 10**8, 8)
    other_a = chip_swap(part_a)
    other_b = chip_swap(part_b)
    other_a, bias2_sib = tied(other_a, bias2_sib)
    diag, lon = call(residual_kernel, piece * 2, (part_a, other_a, base_a), 10**6, 8)
    diag, lon, part_b = tied(diag, lon, part_b)
    lat, own = call(residual_kernel, piece * 2, (part_b, other_b, base_b), 10**10, 8)
    diag = out_to(diag, 1, 1)
    lon = out_to(lon, 0, 1)
    lat = out_to(lat, 1, 0)

    xn_a = call(norm_kernel, half, (diag, lon), 10**10, 8)
    part_a, part_b = call(
        second_kernel,
        half * 2,
        (xn_a, lat, own, w_second, w_sib, out_second, s1, bias2, bias2_sib),
        10**9,
        16,
    )
    other_a = chip_swap(part_a)
    other_b = chip_swap(part_b)
    mlp = (up_weight, u1, down_weight, d1)
    part_a = call(mlp_kernel, half, (part_a, other_a, diag, lon, *mlp), 10**9, 20)
    part_a, part_b = tied(part_a, part_b)
    other_a = chip_swap(part_a)
    part_b = call(mlp_kernel, half, (part_b, other_b, lat, own, *mlp), 10**9, 20)
    other_b = chip_swap(part_b)
    diag, lon = call(sum_kernel, piece * 2, (part_a, other_a), 10**6, 8)
    diag, lon, part_b = tied(diag, lon, part_b)
    diag = home(diag, 1, 1)
    lon = home(lon, 0, 1)
    lat, own = call(sum_kernel, piece * 2, (part_b, other_b), 10**10, 8)
    lat = home(lat, 1, 0)
    mine_a = call(join_kernel, half, (diag, lon), 10**10, 8)
    mine_a, lat, own = tied(mine_a, lat, own)
    mine_b = call(join_kernel, half, (lat, own), 10**6, 8)
    operands = (mine_a, mine_b, core_swap(mine_a), core_swap(mine_b))
    result = place_rows((rows * cols, levels, width), operands)
    return result.reshape(rows, cols, levels, width).transpose(2, 0, 1, 3)


def solution(mesh):
    counts = tuple(mesh.shape[name] for name in AXES)
    return jax.shard_map(
        functools.partial(body, counts),
        mesh=mesh,
        in_specs=(
            P(None, "lat", "lon", None),
            P(None, None, "mp"),
            P(None, None, "mp"),
            P("mp", None),
            P("mp", None),
            P(None, "mp", None),
            P(None, "mp"),
            P("mp", None),
        ),
        out_specs=P(None, "lat", "lon", None),
        check_vma=False,
    )
```

```python
import functools

import jax
import jax.numpy as jnp
import numpy as np
from jax import lax
from jax.experimental import pallas as pl
from jax.experimental.pallas import tpu as pltpu
from jax.sharding import PartitionSpec as P

WL = 2
WY = 6
WX = 12
SY = 3
SX = 6
HD = 64
NEG = -1000000000.0
AXES = ("lat", "lon", "mp")
MIB = 1024 * 1024

USED = 36
ROWS = 40
KEPT = 4 * ROWS
HALF = 2 * ROWS
PATCH = 4 * WY * WX
WINDOW = WL * WY * WX
FEAT = 32
F_Y = 4
F_X = 10
F_PAD = 22


def pairs(counts, target):
    lats, lons, mps = counts
    result = []
    for a in range(lats):
        for b in range(lons):
            for m in range(mps):
                ta, tb, tm = target(a, b, m)
                dest = ((ta % lats) * lons + tb % lons) * mps + tm
                result.append(((a * lons + b) * mps + m, dest))
    return result


def dot(left, right):
    return jnp.dot(left, right, preferred_element_type=jnp.float32)


def dot_t(left, right):
    return lax.dot_general(left, right, (((1,), (1,)), ((), ())), preferred_element_type=jnp.float32)


def normalize(floats):
    center = floats - jnp.mean(floats, axis=-1, keepdims=True)
    spread = jnp.mean(center * center, axis=-1, keepdims=True)
    return (center * lax.rsqrt(spread + 1e-05)).astype(jnp.bfloat16)


def core_index():
    return lax.rem(lax.axis_index("mp"), 2)


def iota(shape, axis):
    return lax.broadcasted_iota(jnp.int32, shape, axis)


def one_hot(condition):
    return jnp.where(condition, 1.0, 0.0).astype(jnp.bfloat16)


def piece_place(slot):
    level = (slot * 57) >> 10
    rest = slot - level * 18
    row = (rest * 43) >> 8
    return level, row, rest - row * 6


def kept_place(index):
    quad = (index * 205) >> 13
    slot = index - quad * ROWS
    return (quad, slot) + piece_place(slot)


def real_level(level, core):
    return jnp.where(core == 0, 1 + level, 3 - 3 * level)


def patch_place(q, row, col):
    return row + 3 - 3 * (q & 1), col + 6 - 3 * (q & 2)


def bias_rows(table, block, pair):
    shape = (FEAT, 4 * FEAT)
    i, lane = iota(shape, 0), iota(shape, 1)
    j = lane & (FEAT - 1)
    kind = jnp.full(shape, 37, jnp.int32)
    kind = jnp.where((i < WL) & (j < WL), i - j + 1, kind)
    kind = jnp.where((i < WL) & (j == F_PAD), 38, kind)
    in_y = (i >= F_Y) & (i < F_Y + WY) & (j >= F_Y) & (j < F_Y + WY)
    kind = jnp.where(in_y, 3 + i - j + 5, kind)
    in_x = (i >= F_X) & (i < F_X + WX) & (j >= F_X) & (j < F_X + WX)
    kind = jnp.where(in_x, 14 + i - j + 11, kind)
    total = jnp.where(kind == 38, NEG, 0.0)
    for k in range(37):
        value = jnp.where(lane < HD, table[block, 2 * pair + 1, k], table[block, 2 * pair, k])
        total = jnp.where(kind == k, value, total)
    high = total.astype(jnp.bfloat16).astype(jnp.float32)
    return jnp.where((lane & FEAT) != 0, total - high, high).astype(jnp.bfloat16)


def bias_kernel(block, table, out):
    for pair in range(2):
        out[:, pair * 128 : pair * 128 + 128] = bias_rows(table, block, pair)


def features(level, row, col, used, count):
    j = iota((count, 128), 1) & (FEAT - 1)
    hit = (j == level) | (j == F_Y + row) | (j == F_X + col)
    return one_hot(jnp.where(used, jnp.where(hit, 1, 0), jnp.where(j == F_PAD, 1, 0)) == 1)


def attend(parts, key_feat):
    low = iota(parts[0][0].shape, 1) < HD
    none = jnp.zeros_like(parts[0][0])
    count = none.shape[0]
    scores = []
    for query, key, _, extra in parts:
        upper = jnp.concatenate([jnp.where(low, query, none), jnp.where(low, none, extra)], axis=1)
        lower = jnp.concatenate([jnp.where(low, none, query), jnp.where(low, extra, none)], axis=1)
        both = jnp.concatenate([upper, lower], axis=0)
        scores.append(dot_t(both, jnp.concatenate([key, key_feat], axis=1)))
    expos, scales = [], []
    for score in scores:
        expo = jnp.exp(score - jnp.max(score, axis=-1, keepdims=True))
        expos.append(expo.astype(jnp.bfloat16))
        scales.append(1.0 / jnp.sum(expo, axis=-1, keepdims=True))
    results = []
    for (_, _, value, _), expo, scale in zip(parts, expos, scales):
        mixed = dot(expo, value) * scale
        results.append(jnp.where(low, mixed[:count], mixed[count:]).astype(jnp.bfloat16))
    return results


def pair_cols(pair):
    return slice(pair * 128, pair * 128 + 128)


def first_kernel(tokens, weight, bias, keep, give):
    core = core_index()
    floats = tokens[...].astype(jnp.float32).reshape(PATCH, -1)
    xn = normalize(floats)
    q = (dot(xn, weight[0]) * HD**-0.5).astype(jnp.bfloat16)
    k = dot(xn, weight[1]).astype(jnp.bfloat16)
    v = dot(xn, weight[2]).astype(jnp.bfloat16)
    index = iota((PATCH, 1), 0)
    level = (index * 911) >> 16
    order = one_hot(iota((PATCH, PATCH), 1) == (index - 72 * level) * 4 + level)
    q, k, v = (dot(order, part).astype(jnp.bfloat16) for part in (q, k, v))
    index = iota((WINDOW, 1), 0)
    level = (index * 911) >> 16
    rest = index - 72 * level
    row = (rest * 171) >> 11
    feat = features(level, row, rest - 12 * row, index >= 0, WINDOW)
    extra = dot(feat[:, :FEAT], bias[...]).astype(jnp.bfloat16)
    parts = []
    for w in range(2):
        rows = slice(w * WINDOW, (w + 1) * WINDOW)
        for pair in range(2):
            cols = pair_cols(pair)
            parts.append((q[rows, cols], k[rows, cols], v[rows, cols], extra[:, cols]))
    heads = attend(parts, feat)
    windows = [jnp.concatenate(heads[2 * w : 2 * w + 2], axis=1) for w in range(2)]
    mixed = jnp.concatenate(windows, axis=0)
    quad, slot, level, row, col = kept_place(iota((KEPT, 1), 0))
    row, col = patch_place(quad, row, col)
    lanes = iota((KEPT, PATCH), 1)
    for out, chosen in ((keep, core), (give, 1 - core)):
        place = real_level(level, chosen) * 72 + row * 12 + col
        place = jnp.where(slot < USED, place, -1)
        out[...] = dot(one_hot(lanes == place), mixed).astype(jnp.bfloat16)


def base_kernel(tokens, *outs):
    values = tokens[...].astype(jnp.float32).reshape(PATCH, -1).astype(jnp.bfloat16)
    quad, slot, level, row, col = kept_place(iota((KEPT, 1), 0))
    row, col = patch_place(quad, row, col)
    place = (row * 12 + col) * 4 + real_level(level, core_index())
    place = jnp.where(slot < USED, place, -1)
    store_halves(dot(one_hot(iota((KEPT, PATCH), 1) == place), values), outs)


def store_halves(total, outs):
    for h in range(2):
        outs[h][...] = total[h * HALF : (h + 1) * HALF].astype(jnp.bfloat16)


def partial_kernel(o0, o1, w0, w1, *outs):
    store_halves(dot(o0[...], w0[...]) + dot(o1[...], w1[...]), outs)


def branch_sum(mine, other):
    total = mine[...].astype(jnp.float32) + other[...].astype(jnp.float32)
    return total.astype(jnp.bfloat16).astype(jnp.float32)


def residual_kernel(mine, other, base, *outs):
    first = base[...].astype(jnp.float32) + branch_sum(mine, other)
    for p in range(2):
        outs[p][...] = first[p * ROWS : (p + 1) * ROWS].astype(jnp.bfloat16)


def joined(pieces):
    return jnp.concatenate([p[...].astype(jnp.float32) for p in pieces], axis=0)


def norm_kernel(p0, p1, out):
    out[...] = normalize(joined((p0, p1)))


def second_kernel(xn_a, p2, p3, w_own, w_sib, o_own, o_sib, b_own, b_sib, *outs):
    xn_b = normalize(joined((p2, p3))).astype(jnp.float32)
    xn = jnp.concatenate([xn_a[...].astype(jnp.float32), xn_b], axis=0).astype(jnp.bfloat16)
    quad, slot, level, row, col = kept_place(iota((KEPT, 1), 0))
    row, col = row + 3 * (quad & 1), col + 3 * (quad & 2)
    feat = features(level, row, col, slot < USED, KEPT)
    lane = iota((KEPT, 128), 1)
    j = lane & (FEAT - 1)
    split_levels = core_index() == 1
    split_rows = lax.axis_index("lat") == 0
    ban_level = (j < WL) & (j != level)
    ban_row = (j >= F_Y) & (j < F_Y + WY) & ((j >= F_Y + SY) != (row >= SY))
    ban = jnp.where(ban_level, split_levels.astype(jnp.int32), jnp.where(ban_row, split_rows.astype(jnp.int32), 0))
    ban = jnp.where((lane & FEAT) == 0, ban, 0) == 1
    parts = []
    for weight, bias in ((w_own, b_own), (w_sib, b_sib)):
        q = (dot(xn, weight[0]) * HD**-0.5).astype(jnp.bfloat16)
        k = dot(xn, weight[1]).astype(jnp.bfloat16)
        v = dot(xn, weight[2]).astype(jnp.bfloat16)
        extra = dot(feat[:, :FEAT], bias[...])
        for pair in range(2):
            cols = pair_cols(pair)
            parts.append((q[:, cols], k[:, cols], v[:, cols], jnp.where(ban, NEG, extra[:, cols]).astype(jnp.bfloat16)))
    heads = attend(parts, feat)
    total = dot(jnp.concatenate(heads[:2], axis=1), o_own[...])
    total = total + dot(jnp.concatenate(heads[2:], axis=1), o_sib[...])
    store_halves(total, outs)


def gelu(x):
    return 0.5 * x * (1.0 + lax.erf(x * np.float32(np.sqrt(0.5))))


def mlp_kernel(mine, other, p0, p1, u0, u1, d0, d1, out):
    second = joined((p0, p1)) + branch_sum(mine, other)
    second = second.astype(jnp.bfloat16).astype(jnp.float32)
    xn = normalize(second)
    h0 = gelu(dot(xn, u0[...])).astype(jnp.bfloat16)
    h1 = gelu(dot(xn, u1[...])).astype(jnp.bfloat16)
    out[...] = (0.5 * second + dot(h0, d0[...]) + dot(h1, d1[...])).astype(jnp.bfloat16)


def sum_kernel(mine, other, *outs):
    total = mine[...].astype(jnp.float32) + other[...].astype(jnp.float32)
    for p in range(2):
        outs[p][...] = total[p * ROWS : (p + 1) * ROWS].astype(jnp.bfloat16)


def join_kernel(second, first, out):
    out[...] = joined((first, second)).astype(jnp.bfloat16)


def place_kernel(m1, m0, s1, s0, out, held, sems):
    core = core_index()
    quad, slot, level, row, col = kept_place(iota((1, KEPT), 1))
    row, col = patch_place(quad, row, col)
    places, sources = [], []
    for chosen, parts in ((core, (m0, m1)), (1 - core, (s0, s1))):
        place = (row * 12 + col) * 4 + real_level(level, chosen)
        places.append(jnp.where(slot < USED, place, -1))
        sources.append(jnp.concatenate([part[...] for part in parts], axis=0))
    count = PATCH // 2
    copies = []
    for h in range(2):
        index = iota((count, KEPT), 0) + h * count
        total = dot(one_hot(index == places[0]), sources[0]) + dot(one_hot(index == places[1]), sources[1])
        rows = pl.ds(h * count // 4, count // 4)
        held[rows] = total.reshape(count // 4, 4, -1).astype(jnp.bfloat16)
        copies.append(pltpu.make_async_copy(held.at[rows], out.at[rows], sems.at[h]))
        copies[h].start()
    for copy in copies:
        copy.wait()


def place_rows(shape, operands):
    return pl.pallas_call(
        place_kernel,
        out_shape=jax.ShapeDtypeStruct(shape, jnp.bfloat16),
        in_specs=[pl.BlockSpec(memory_space=pltpu.VMEM)] * 4,
        out_specs=pl.BlockSpec(memory_space=pl.ANY),
        scratch_shapes=[pltpu.VMEM(shape, jnp.bfloat16), pltpu.SemaphoreType.DMA((2,))],
        compiler_params=pltpu.CompilerParams(vmem_limit_bytes=12 * MIB),
        cost_estimate=pl.CostEstimate(flops=2 * 10**8, bytes_accessed=2 * 10**6, transcendentals=0),
    )(*operands)


def call(kernel, outs, operands, flops, limit, table=False):
    shapes = [jax.ShapeDtypeStruct(s, jnp.bfloat16) for s in outs]
    moved = sum(o.size * o.dtype.itemsize for o in operands) + sum(2 * s.size for s in shapes)
    result = pl.pallas_call(
        kernel,
        out_shape=shapes,
        in_specs=[pl.BlockSpec(memory_space=pltpu.SMEM if table else pltpu.VMEM)] * len(operands),
        out_specs=[pl.BlockSpec(memory_space=pltpu.VMEM)] * len(shapes),
        compiler_params=pltpu.CompilerParams(vmem_limit_bytes=limit * MIB),
        cost_estimate=pl.CostEstimate(flops=flops, bytes_accessed=moved, transcendentals=0),
    )(*operands)
    return result if len(result) > 1 else result[0]


def tied(*values):
    return lax.optimization_barrier(values)


def body(counts, tokens, qkv_first, qkv_second, out_first, out_second, rel_tables, up_weight, down_weight):
    levels, rows, cols, width = tokens.shape
    turn = counts[1] // 2

    def move(value, target):
        return lax.ppermute(value, AXES, pairs(counts, target))

    def core_swap(value):
        return move(value, lambda a, b, m: (a, b, m ^ 1))

    def chip_swap(value):
        return move(value, lambda a, b, m: (a, b, m ^ 2))

    def out_to(value, dy, dx):
        return move(value, lambda a, b, m: (a + dy, b + dx, m ^ 2 if dx and (b + 1) % turn == 0 else m))

    def home(value, dy, dx):
        return move(value, lambda a, b, m: (a - dy, b - dx, m ^ 2 if dx and b % turn == 0 else m))

    half, piece = [(HALF, width)], [(ROWS, width)]
    heads, features = [(KEPT, 256)], [(FEAT, 256)]

    tok = tokens.transpose(1, 2, 0, 3).reshape(rows * cols, levels, width)
    w_first = qkv_first.transpose(1, 0, 2)
    w_second = qkv_second.transpose(1, 0, 2)

    f1 = core_swap(out_first)
    s1 = core_swap(out_second)
    w_sib = core_swap(w_second)
    bias1 = call(functools.partial(bias_kernel, 0), features, (rel_tables,), 5 * 10**9, 4, table=True)
    keep, give = call(first_kernel, heads * 2, (tok, w_first, bias1), 10**9, 16)
    keep, give, f1 = tied(keep, give, f1)
    keep, tok, rel_tables = tied(keep, tok, rel_tables)
    base_a, base_b = call(base_kernel, half * 2, (tok,), 10**9, 8)
    bias2 = call(functools.partial(bias_kernel, 1), features, (rel_tables,), 10**9, 4, table=True)
    bias2_sib = core_swap(bias2)
    given, up_late, down_late, s1, w_sib = tied(core_swap(give), up_weight, down_weight, s1, w_sib)
    u1 = core_swap(up_late)
    d1 = core_swap(down_late)
    part_a, part_b = call(partial_kernel, half * 2, (keep, given, out_first, f1), 2 * 10**8, 8)
    other_a = chip_swap(part_a)
    other_b = chip_swap(part_b)
    other_a, bias2_sib = tied(other_a, bias2_sib)
    diag, lon = call(residual_kernel, piece * 2, (part_a, other_a, base_a), 10**6, 8)
    diag, lon, part_b = tied(diag, lon, part_b)
    lat, own = call(residual_kernel, piece * 2, (part_b, other_b, base_b), 10**10, 8)
    diag = out_to(diag, 1, 1)
    lon = out_to(lon, 0, 1)
    lat = out_to(lat, 1, 0)

    xn_a = call(norm_kernel, half, (diag, lon), 10**10, 8)
    part_a, part_b = call(
        second_kernel,
        half * 2,
        (xn_a, lat, own, w_second, w_sib, out_second, s1, bias2, bias2_sib),
        10**9,
        16,
    )
    other_a = chip_swap(part_a)
    other_b = chip_swap(part_b)
    mlp = (up_weight, u1, down_weight, d1)
    part_a = call(mlp_kernel, half, (part_a, other_a, diag, lon, *mlp), 10**9, 20)
    part_a, part_b = tied(part_a, part_b)
    other_a = chip_swap(part_a)
    part_b = call(mlp_kernel, half, (part_b, other_b, lat, own, *mlp), 10**9, 20)
    other_b = chip_swap(part_b)
    diag, lon = call(sum_kernel, piece * 2, (part_a, other_a), 10**6, 8)
    diag, lon, part_b = tied(diag, lon, part_b)
    diag = home(diag, 1, 1)
    lon = home(lon, 0, 1)
    lat, own = call(sum_kernel, piece * 2, (part_b, other_b), 10**10, 8)
    lat = home(lat, 1, 0)
    mine_a = call(join_kernel, half, (lon, diag), 10**10, 8)
    mine_a, lat, own = tied(mine_a, lat, own)
    mine_b = call(join_kernel, half, (own, lat), 10**6, 8)
    sib_b = core_swap(mine_b)
    operands = (mine_b, mine_a, sib_b, core_swap(mine_a))
    result = place_rows((rows * cols, levels, width), operands)
    return result.reshape(rows, cols, levels, width).transpose(2, 0, 1, 3)


def solution(mesh):
    counts = tuple(mesh.shape[name] for name in AXES)
    return jax.shard_map(
        functools.partial(body, counts),
        mesh=mesh,
        in_specs=(
            P(None, "lat", "lon", None),
            P(None, None, "mp"),
            P(None, None, "mp"),
            P("mp", None),
            P("mp", None),
            P(None, "mp", None),
            P(None, "mp"),
            P("mp", None),
        ),
        out_specs=P(None, "lat", "lon", None),
        check_vma=False,
    )
```

```python
import functools

import jax
import jax.numpy as jnp
import numpy as np
from jax import lax
from jax.experimental import pallas as pl
from jax.experimental.pallas import tpu as pltpu
from jax.sharding import PartitionSpec as P

WL = 2
WY = 6
WX = 12
SY = 3
SX = 6
HD = 64
NEG = -1000000000.0
AXES = ("lat", "lon", "mp")
MIB = 1024 * 1024

USED = 36
ROWS = 40
KEPT = 4 * ROWS
HALF = 2 * ROWS
PATCH = 4 * WY * WX
WINDOW = WL * WY * WX
FEAT = 32
F_Y = 4
F_X = 10
F_PAD = 22


def pairs(counts, target):
    lats, lons, mps = counts
    result = []
    for a in range(lats):
        for b in range(lons):
            for m in range(mps):
                ta, tb, tm = target(a, b, m)
                dest = ((ta % lats) * lons + tb % lons) * mps + tm
                result.append(((a * lons + b) * mps + m, dest))
    return result


def dot(left, right):
    return jnp.dot(left, right, preferred_element_type=jnp.float32)


def dot_t(left, right):
    return lax.dot_general(left, right, (((1,), (1,)), ((), ())), preferred_element_type=jnp.float32)


def normalize(floats):
    center = floats - jnp.mean(floats, axis=-1, keepdims=True)
    spread = jnp.mean(center * center, axis=-1, keepdims=True)
    return (center * lax.rsqrt(spread + 1e-05)).astype(jnp.bfloat16)


def core_index():
    return lax.rem(lax.axis_index("mp"), 2)


def iota(shape, axis):
    return lax.broadcasted_iota(jnp.int32, shape, axis)


def one_hot(condition):
    return jnp.where(condition, 1.0, 0.0).astype(jnp.bfloat16)


def piece_place(slot):
    level = (slot * 57) >> 10
    rest = slot - level * 18
    row = (rest * 43) >> 8
    return level, row, rest - row * 6


def kept_place(index):
    quad = (index * 205) >> 13
    slot = index - quad * ROWS
    return (quad, slot) + piece_place(slot)


def real_level(level, core):
    return jnp.where(core == 0, 1 + level, 3 - 3 * level)


def patch_place(q, row, col):
    return row + 3 - 3 * (q & 1), col + 6 - 3 * (q & 2)


def bias_rows(table, block, pair):
    shape = (FEAT, 4 * FEAT)
    i, lane = iota(shape, 0), iota(shape, 1)
    j = lane & (FEAT - 1)
    kind = jnp.full(shape, 37, jnp.int32)
    kind = jnp.where((i < WL) & (j < WL), i - j + 1, kind)
    kind = jnp.where((i < WL) & (j == F_PAD), 38, kind)
    in_y = (i >= F_Y) & (i < F_Y + WY) & (j >= F_Y) & (j < F_Y + WY)
    kind = jnp.where(in_y, 3 + i - j + 5, kind)
    in_x = (i >= F_X) & (i < F_X + WX) & (j >= F_X) & (j < F_X + WX)
    kind = jnp.where(in_x, 14 + i - j + 11, kind)
    total = jnp.where(kind == 38, NEG, 0.0)
    for k in range(37):
        value = jnp.where(lane < HD, table[block, 2 * pair + 1, k], table[block, 2 * pair, k])
        total = jnp.where(kind == k, value, total)
    high = total.astype(jnp.bfloat16).astype(jnp.float32)
    return jnp.where((lane & FEAT) != 0, total - high, high).astype(jnp.bfloat16)


def bias_kernel(block, table, out):
    for pair in range(2):
        out[:, pair * 128 : pair * 128 + 128] = bias_rows(table, block, pair)


def features(level, row, col, used, count):
    j = iota((count, 128), 1) & (FEAT - 1)
    hit = (j == level) | (j == F_Y + row) | (j == F_X + col)
    return one_hot(jnp.where(used, jnp.where(hit, 1, 0), jnp.where(j == F_PAD, 1, 0)) == 1)


def attend(parts, key_feat):
    low = iota(parts[0][0].shape, 1) < HD
    none = jnp.zeros_like(parts[0][0])
    count = none.shape[0]
    scores = []
    for query, key, _, extra in parts:
        upper = jnp.concatenate([jnp.where(low, query, none), jnp.where(low, none, extra)], axis=1)
        lower = jnp.concatenate([jnp.where(low, none, query), jnp.where(low, extra, none)], axis=1)
        both = jnp.concatenate([upper, lower], axis=0)
        scores.append(dot_t(both, jnp.concatenate([key, key_feat], axis=1)))
    expos, scales = [], []
    for score in scores:
        expo = jnp.exp(score - jnp.max(score, axis=-1, keepdims=True))
        expos.append(expo.astype(jnp.bfloat16))
        scales.append(1.0 / jnp.sum(expo, axis=-1, keepdims=True))
    results = []
    for (_, _, value, _), expo, scale in zip(parts, expos, scales):
        mixed = dot(expo, value) * scale
        results.append(jnp.where(low, mixed[:count], mixed[count:]).astype(jnp.bfloat16))
    return results


def pair_cols(pair):
    return slice(pair * 128, pair * 128 + 128)


def first_kernel(tokens, weight, bias, keep, give):
    core = core_index()
    floats = tokens[...].astype(jnp.float32).reshape(PATCH, -1)
    xn = normalize(floats)
    q = (dot(xn, weight[0]) * HD**-0.5).astype(jnp.bfloat16)
    k = dot(xn, weight[1]).astype(jnp.bfloat16)
    v = dot(xn, weight[2]).astype(jnp.bfloat16)
    index = iota((PATCH, 1), 0)
    level = (index * 911) >> 16
    order = one_hot(iota((PATCH, PATCH), 1) == (index - 72 * level) * 4 + level)
    q, k, v = (dot(order, part).astype(jnp.bfloat16) for part in (q, k, v))
    index = iota((WINDOW, 1), 0)
    level = (index * 911) >> 16
    rest = index - 72 * level
    row = (rest * 171) >> 11
    feat = features(level, row, rest - 12 * row, index >= 0, WINDOW)
    extra = dot(feat[:, :FEAT], bias[...]).astype(jnp.bfloat16)
    parts = []
    for w in range(2):
        rows = slice(w * WINDOW, (w + 1) * WINDOW)
        for pair in range(2):
            cols = pair_cols(pair)
            parts.append((q[rows, cols], k[rows, cols], v[rows, cols], extra[:, cols]))
    heads = attend(parts, feat)
    windows = [jnp.concatenate(heads[2 * w : 2 * w + 2], axis=1) for w in range(2)]
    mixed = jnp.concatenate(windows, axis=0)
    quad, slot, level, row, col = kept_place(iota((KEPT, 1), 0))
    row, col = patch_place(quad, row, col)
    lanes = iota((KEPT, PATCH), 1)
    for out, chosen in ((keep, core), (give, 1 - core)):
        place = real_level(level, chosen) * 72 + row * 12 + col
        place = jnp.where(slot < USED, place, -1)
        out[...] = dot(one_hot(lanes == place), mixed).astype(jnp.bfloat16)


def base_kernel(tokens, *outs):
    values = tokens[...].astype(jnp.float32).reshape(PATCH, -1).astype(jnp.bfloat16)
    quad, slot, level, row, col = kept_place(iota((KEPT, 1), 0))
    row, col = patch_place(quad, row, col)
    place = (row * 12 + col) * 4 + real_level(level, core_index())
    place = jnp.where(slot < USED, place, -1)
    store_three(dot(one_hot(iota((KEPT, PATCH), 1) == place), values), outs)


def store_halves(total, outs):
    for h in range(2):
        outs[h][...] = total[h * HALF : (h + 1) * HALF].astype(jnp.bfloat16)


def store_three(total, outs):
    for out, start, stop in zip(outs, (0, 2 * ROWS, 3 * ROWS), (2 * ROWS, 3 * ROWS, KEPT)):
        out[...] = total[start:stop].astype(jnp.bfloat16)


def partial_kernel(o0, o1, w0, w1, *outs):
    store_three(dot(o0[...], w0[...]) + dot(o1[...], w1[...]), outs)


def branch_sum(mine, other):
    total = mine[...].astype(jnp.float32) + other[...].astype(jnp.float32)
    return total.astype(jnp.bfloat16).astype(jnp.float32)


def residual_kernel(mine, other, base, *outs):
    first = base[...].astype(jnp.float32) + branch_sum(mine, other)
    for p, out in enumerate(outs):
        out[...] = first[p * ROWS : (p + 1) * ROWS].astype(jnp.bfloat16)


def joined(pieces):
    return jnp.concatenate([p[...].astype(jnp.float32) for p in pieces], axis=0)


def norm_kernel(p0, p1, out):
    out[...] = normalize(joined((p0, p1)))


def second_kernel(xn_a, p2, p3, w_own, w_sib, o_own, o_sib, b_own, b_sib, *outs):
    xn_b = normalize(joined((p2, p3))).astype(jnp.float32)
    xn = jnp.concatenate([xn_a[...].astype(jnp.float32), xn_b], axis=0).astype(jnp.bfloat16)
    quad, slot, level, row, col = kept_place(iota((KEPT, 1), 0))
    row, col = row + 3 * (quad & 1), col + 3 * (quad & 2)
    feat = features(level, row, col, slot < USED, KEPT)
    lane = iota((KEPT, 128), 1)
    j = lane & (FEAT - 1)
    split_levels = core_index() == 1
    split_rows = lax.axis_index("lat") == 0
    ban_level = (j < WL) & (j != level)
    ban_row = (j >= F_Y) & (j < F_Y + WY) & ((j >= F_Y + SY) != (row >= SY))
    ban = jnp.where(ban_level, split_levels.astype(jnp.int32), jnp.where(ban_row, split_rows.astype(jnp.int32), 0))
    ban = jnp.where((lane & FEAT) == 0, ban, 0) == 1
    parts = []
    for weight, bias in ((w_own, b_own), (w_sib, b_sib)):
        q = (dot(xn, weight[0]) * HD**-0.5).astype(jnp.bfloat16)
        k = dot(xn, weight[1]).astype(jnp.bfloat16)
        v = dot(xn, weight[2]).astype(jnp.bfloat16)
        extra = dot(feat[:, :FEAT], bias[...])
        for pair in range(2):
            cols = pair_cols(pair)
            parts.append((q[:, cols], k[:, cols], v[:, cols], jnp.where(ban, NEG, extra[:, cols]).astype(jnp.bfloat16)))
    heads = attend(parts, feat)
    total = dot(jnp.concatenate(heads[:2], axis=1), o_own[...])
    total = total + dot(jnp.concatenate(heads[2:], axis=1), o_sib[...])
    store_halves(total, outs)


def gelu(x):
    return 0.5 * x * (1.0 + lax.erf(x * np.float32(np.sqrt(0.5))))


def mlp_kernel(mine, other, p0, p1, u0, u1, d0, d1, out):
    second = joined((p0, p1)) + branch_sum(mine, other)
    second = second.astype(jnp.bfloat16).astype(jnp.float32)
    xn = normalize(second)
    h0 = gelu(dot(xn, u0[...])).astype(jnp.bfloat16)
    h1 = gelu(dot(xn, u1[...])).astype(jnp.bfloat16)
    out[...] = (0.5 * second + dot(h0, d0[...]) + dot(h1, d1[...])).astype(jnp.bfloat16)


def sum_kernel(mine, other, *outs):
    total = mine[...].astype(jnp.float32) + other[...].astype(jnp.float32)
    for p in range(2):
        outs[p][...] = total[p * ROWS : (p + 1) * ROWS].astype(jnp.bfloat16)


def join_kernel(p0, p1, out):
    out[...] = joined((p0, p1)).astype(jnp.bfloat16)


def place_kernel(m0, m1, s0, s1, out, held, sems):
    core = core_index()
    quad, slot, level, row, col = kept_place(iota((1, KEPT), 1))
    row, col = patch_place(quad, row, col)
    places, sources = [], []
    for chosen, parts in ((core, (m0, m1)), (1 - core, (s0, s1))):
        place = (row * 12 + col) * 4 + real_level(level, chosen)
        places.append(jnp.where(slot < USED, place, -1))
        sources.append(jnp.concatenate([part[...] for part in parts], axis=0))
    count = PATCH // 2
    copies = []
    for h in range(2):
        index = iota((count, KEPT), 0) + h * count
        total = dot(one_hot(index == places[0]), sources[0]) + dot(one_hot(index == places[1]), sources[1])
        rows = pl.ds(h * count // 4, count // 4)
        held[rows] = total.reshape(count // 4, 4, -1).astype(jnp.bfloat16)
        copies.append(pltpu.make_async_copy(held.at[rows], out.at[rows], sems.at[h]))
        copies[h].start()
    for copy in copies:
        copy.wait()


def place_rows(shape, operands):
    return pl.pallas_call(
        place_kernel,
        out_shape=jax.ShapeDtypeStruct(shape, jnp.bfloat16),
        in_specs=[pl.BlockSpec(memory_space=pltpu.VMEM)] * 4,
        out_specs=pl.BlockSpec(memory_space=pl.ANY),
        scratch_shapes=[pltpu.VMEM(shape, jnp.bfloat16), pltpu.SemaphoreType.DMA((2,))],
        compiler_params=pltpu.CompilerParams(vmem_limit_bytes=12 * MIB),
        cost_estimate=pl.CostEstimate(flops=2 * 10**8, bytes_accessed=2 * 10**6, transcendentals=0),
    )(*operands)


def call(kernel, outs, operands, flops, limit, table=False):
    shapes = [jax.ShapeDtypeStruct(s, jnp.bfloat16) for s in outs]
    moved = sum(o.size * o.dtype.itemsize for o in operands) + sum(2 * s.size for s in shapes)
    result = pl.pallas_call(
        kernel,
        out_shape=shapes,
        in_specs=[pl.BlockSpec(memory_space=pltpu.SMEM if table else pltpu.VMEM)] * len(operands),
        out_specs=[pl.BlockSpec(memory_space=pltpu.VMEM)] * len(shapes),
        compiler_params=pltpu.CompilerParams(vmem_limit_bytes=limit * MIB),
        cost_estimate=pl.CostEstimate(flops=flops, bytes_accessed=moved, transcendentals=0),
    )(*operands)
    return result if len(result) > 1 else result[0]


def tied(*values):
    return lax.optimization_barrier(values)


def body(counts, tokens, qkv_first, qkv_second, out_first, out_second, rel_tables, up_weight, down_weight):
    levels, rows, cols, width = tokens.shape
    turn = counts[1] // 2

    def move(value, target):
        return lax.ppermute(value, AXES, pairs(counts, target))

    def core_swap(value):
        return move(value, lambda a, b, m: (a, b, m ^ 1))

    def chip_swap(value):
        return move(value, lambda a, b, m: (a, b, m ^ 2))

    def out_to(value, dy, dx):
        return move(value, lambda a, b, m: (a + dy, b + dx, m ^ 2 if dx and (b + 1) % turn == 0 else m))

    def home(value, dy, dx):
        return move(value, lambda a, b, m: (a - dy, b - dx, m ^ 2 if dx and b % turn == 0 else m))

    half, piece = [(HALF, width)], [(ROWS, width)]
    heads, features = [(KEPT, 256)], [(FEAT, 256)]

    tok = tokens.transpose(1, 2, 0, 3).reshape(rows * cols, levels, width)
    w_first = qkv_first.transpose(1, 0, 2)
    w_second = qkv_second.transpose(1, 0, 2)

    f1 = core_swap(out_first)
    s1 = core_swap(out_second)
    w_sib = core_swap(w_second)
    bias1 = call(functools.partial(bias_kernel, 0), features, (rel_tables,), 5 * 10**9, 4, table=True)
    keep, give = call(first_kernel, heads * 2, (tok, w_first, bias1), 10**9, 16)
    keep, give, f1 = tied(keep, give, f1)
    keep, tok, rel_tables = tied(keep, tok, rel_tables)
    base_a, base_lat, base_own = call(base_kernel, half + piece * 2, (tok,), 10**9, 8)
    bias2 = call(functools.partial(bias_kernel, 1), features, (rel_tables,), 10**9, 4, table=True)
    bias2_sib = core_swap(bias2)
    given, up_late, s1, w_sib = tied(core_swap(give), up_weight, s1, w_sib)
    u1 = core_swap(up_late)
    part_a, part_lat, part_own = call(partial_kernel, half + piece * 2, (keep, given, out_first, f1), 2 * 10**8, 8)
    other_a = chip_swap(part_a)
    other_lat = chip_swap(part_lat)
    other_own = chip_swap(part_own)
    other_a, bias2_sib = tied(other_a, bias2_sib)
    diag, lon = call(residual_kernel, piece * 2, (part_a, other_a, base_a), 10**6, 8)
    diag, lon, part_lat = tied(diag, lon, part_lat)
    lat = call(residual_kernel, piece, (part_lat, other_lat, base_lat), 10**10, 8)
    lat, part_own = tied(lat, part_own)
    own = call(residual_kernel, piece, (part_own, other_own, base_own), 10**6, 8)
    diag = out_to(diag, 1, 1)
    lon = out_to(lon, 0, 1)
    lat = out_to(lat, 1, 0)

    xn_a = call(norm_kernel, half, (diag, lon), 10**10, 8)
    part_a, part_b = call(
        second_kernel,
        half * 2,
        (xn_a, lat, own, w_second, w_sib, out_second, s1, bias2, bias2_sib),
        10**9,
        16,
    )
    part_b, down_late = tied(part_b, down_weight)
    other_a = chip_swap(part_a)
    other_b = chip_swap(part_b)
    d1 = core_swap(down_late)
    mlp = (up_weight, u1, down_weight, d1)
    part_a = call(mlp_kernel, half, (part_a, other_a, diag, lon, *mlp), 10**9, 20)
    part_a, part_b = tied(part_a, part_b)
    other_a = chip_swap(part_a)
    part_b = call(mlp_kernel, half, (part_b, other_b, lat, own, *mlp), 10**9, 20)
    other_b = chip_swap(part_b)
    diag, lon = call(sum_kernel, piece * 2, (part_a, other_a), 10**6, 8)
    diag, lon, part_b = tied(diag, lon, part_b)
    diag = home(diag, 1, 1)
    lon = home(lon, 0, 1)
    lat, own = call(sum_kernel, piece * 2, (part_b, other_b), 10**10, 8)
    lat = home(lat, 1, 0)
    mine_a = call(join_kernel, half, (diag, lon), 10**10, 8)
    mine_a, lat, own = tied(mine_a, lat, own)
    mine_b = call(join_kernel, half, (lat, own), 10**6, 8)
    operands = (mine_a, mine_b, core_swap(mine_a), core_swap(mine_b))
    result = place_rows((rows * cols, levels, width), operands)
    return result.reshape(rows, cols, levels, width).transpose(2, 0, 1, 3)


def solution(mesh):
    counts = tuple(mesh.shape[name] for name in AXES)
    return jax.shard_map(
        functools.partial(body, counts),
        mesh=mesh,
        in_specs=(
            P(None, "lat", "lon", None),
            P(None, None, "mp"),
            P(None, None, "mp"),
            P("mp", None),
            P("mp", None),
            P(None, "mp", None),
            P(None, "mp"),
            P("mp", None),
        ),
        out_specs=P(None, "lat", "lon", None),
        check_vma=False,
    )
```

```python
import functools

import jax
import jax.numpy as jnp
import numpy as np
from jax import lax
from jax.experimental import pallas as pl
from jax.experimental.pallas import tpu as pltpu
from jax.sharding import PartitionSpec as P

WL = 2
WY = 6
WX = 12
SY = 3
SX = 6
HD = 64
NEG = -1000000000.0
AXES = ("lat", "lon", "mp")
MIB = 1024 * 1024

USED = 36
ROWS = 40
KEPT = 4 * ROWS
HALF = 2 * ROWS
PATCH = 4 * WY * WX
WINDOW = WL * WY * WX
FEAT = 32
F_Y = 4
F_X = 10
F_PAD = 22


def pairs(counts, target):
    lats, lons, mps = counts
    result = []
    for a in range(lats):
        for b in range(lons):
            for m in range(mps):
                ta, tb, tm = target(a, b, m)
                dest = ((ta % lats) * lons + tb % lons) * mps + tm
                result.append(((a * lons + b) * mps + m, dest))
    return result


def dot(left, right):
    return jnp.dot(left, right, preferred_element_type=jnp.float32)


def dot_t(left, right):
    return lax.dot_general(left, right, (((1,), (1,)), ((), ())), preferred_element_type=jnp.float32)


def normalize(floats):
    center = floats - jnp.mean(floats, axis=-1, keepdims=True)
    spread = jnp.mean(center * center, axis=-1, keepdims=True)
    return (center * lax.rsqrt(spread + 1e-05)).astype(jnp.bfloat16)


def core_index():
    return lax.rem(lax.axis_index("mp"), 2)


def iota(shape, axis):
    return lax.broadcasted_iota(jnp.int32, shape, axis)


def one_hot(condition):
    return jnp.where(condition, 1.0, 0.0).astype(jnp.bfloat16)


def piece_place(slot):
    level = (slot * 57) >> 10
    rest = slot - level * 18
    row = (rest * 43) >> 8
    return level, row, rest - row * 6


def kept_place(index):
    quad = (index * 205) >> 13
    slot = index - quad * ROWS
    return (quad, slot) + piece_place(slot)


def real_level(level, core):
    return jnp.where(core == 0, 1 + level, 3 - 3 * level)


def patch_place(q, row, col):
    return row + 3 - 3 * (q & 1), col + 6 - 3 * (q & 2)


def bias_rows(table, block, pair):
    shape = (FEAT, 4 * FEAT)
    i, lane = iota(shape, 0), iota(shape, 1)
    j = lane & (FEAT - 1)
    kind = jnp.full(shape, 37, jnp.int32)
    kind = jnp.where((i < WL) & (j < WL), i - j + 1, kind)
    kind = jnp.where((i < WL) & (j == F_PAD), 38, kind)
    in_y = (i >= F_Y) & (i < F_Y + WY) & (j >= F_Y) & (j < F_Y + WY)
    kind = jnp.where(in_y, 3 + i - j + 5, kind)
    in_x = (i >= F_X) & (i < F_X + WX) & (j >= F_X) & (j < F_X + WX)
    kind = jnp.where(in_x, 14 + i - j + 11, kind)
    total = jnp.where(kind == 38, NEG, 0.0)
    for k in range(37):
        value = jnp.where(lane < HD, table[block, 2 * pair + 1, k], table[block, 2 * pair, k])
        total = jnp.where(kind == k, value, total)
    high = total.astype(jnp.bfloat16).astype(jnp.float32)
    return jnp.where((lane & FEAT) != 0, total - high, high).astype(jnp.bfloat16)


def bias_kernel(block, table, out):
    for pair in range(2):
        out[:, pair * 128 : pair * 128 + 128] = bias_rows(table, block, pair)


def features(level, row, col, used, count):
    j = iota((count, 128), 1) & (FEAT - 1)
    hit = (j == level) | (j == F_Y + row) | (j == F_X + col)
    return one_hot(jnp.where(used, jnp.where(hit, 1, 0), jnp.where(j == F_PAD, 1, 0)) == 1)


def attend(parts, key_feat):
    low = iota(parts[0][0].shape, 1) < HD
    none = jnp.zeros_like(parts[0][0])
    count = none.shape[0]
    scores = []
    for query, key, _, extra in parts:
        upper = jnp.concatenate([jnp.where(low, query, none), jnp.where(low, none, extra)], axis=1)
        lower = jnp.concatenate([jnp.where(low, none, query), jnp.where(low, extra, none)], axis=1)
        both = jnp.concatenate([upper, lower], axis=0)
        scores.append(dot_t(both, jnp.concatenate([key, key_feat], axis=1)))
    expos, scales = [], []
    for score in scores:
        expo = jnp.exp(score - jnp.max(score, axis=-1, keepdims=True))
        expos.append(expo.astype(jnp.bfloat16))
        scales.append(1.0 / jnp.sum(expo, axis=-1, keepdims=True))
    results = []
    for (_, _, value, _), expo, scale in zip(parts, expos, scales):
        mixed = dot(expo, value) * scale
        results.append(jnp.where(low, mixed[:count], mixed[count:]).astype(jnp.bfloat16))
    return results


def pair_cols(pair):
    return slice(pair * 128, pair * 128 + 128)


def first_kernel(tokens, weight, bias, keep, give):
    core = core_index()
    floats = tokens[...].astype(jnp.float32).reshape(PATCH, -1)
    xn = normalize(floats)
    q = (dot(xn, weight[0]) * HD**-0.5).astype(jnp.bfloat16)
    k = dot(xn, weight[1]).astype(jnp.bfloat16)
    v = dot(xn, weight[2]).astype(jnp.bfloat16)
    index = iota((PATCH, 1), 0)
    level = (index * 911) >> 16
    order = one_hot(iota((PATCH, PATCH), 1) == (index - 72 * level) * 4 + level)
    q, k, v = (dot(order, part).astype(jnp.bfloat16) for part in (q, k, v))
    index = iota((WINDOW, 1), 0)
    level = (index * 911) >> 16
    rest = index - 72 * level
    row = (rest * 171) >> 11
    feat = features(level, row, rest - 12 * row, index >= 0, WINDOW)
    extra = dot(feat[:, :FEAT], bias[...]).astype(jnp.bfloat16)
    parts = []
    for w in range(2):
        rows = slice(w * WINDOW, (w + 1) * WINDOW)
        for pair in range(2):
            cols = pair_cols(pair)
            parts.append((q[rows, cols], k[rows, cols], v[rows, cols], extra[:, cols]))
    heads = attend(parts, feat)
    windows = [jnp.concatenate(heads[2 * w : 2 * w + 2], axis=1) for w in range(2)]
    mixed = jnp.concatenate(windows, axis=0)
    quad, slot, level, row, col = kept_place(iota((KEPT, 1), 0))
    row, col = patch_place(quad, row, col)
    lanes = iota((KEPT, PATCH), 1)
    for out, chosen in ((keep, core), (give, 1 - core)):
        place = real_level(level, chosen) * 72 + row * 12 + col
        place = jnp.where(slot < USED, place, -1)
        out[...] = dot(one_hot(lanes == place), mixed).astype(jnp.bfloat16)


def base_kernel(tokens, *outs):
    values = tokens[...].astype(jnp.float32).reshape(PATCH, -1).astype(jnp.bfloat16)
    quad, slot, level, row, col = kept_place(iota((KEPT, 1), 0))
    row, col = patch_place(quad, row, col)
    place = (row * 12 + col) * 4 + real_level(level, core_index())
    place = jnp.where(slot < USED, place, -1)
    store_three(dot(one_hot(iota((KEPT, PATCH), 1) == place), values), outs)


def store_halves(total, outs):
    for h in range(2):
        outs[h][...] = total[h * HALF : (h + 1) * HALF].astype(jnp.bfloat16)


def store_three(total, outs):
    for out, start, stop in zip(outs, (0, 2 * ROWS, 3 * ROWS), (2 * ROWS, 3 * ROWS, KEPT)):
        out[...] = total[start:stop].astype(jnp.bfloat16)


def partial_kernel(o0, o1, w0, w1, *outs):
    store_three(dot(o0[...], w0[...]) + dot(o1[...], w1[...]), outs)


def branch_sum(mine, other):
    total = mine[...].astype(jnp.float32) + other[...].astype(jnp.float32)
    return total.astype(jnp.bfloat16).astype(jnp.float32)


def residual_kernel(mine, other, base, *outs):
    first = base[...].astype(jnp.float32) + branch_sum(mine, other)
    for p, out in enumerate(outs):
        out[...] = first[p * ROWS : (p + 1) * ROWS].astype(jnp.bfloat16)


def joined(pieces):
    return jnp.concatenate([p[...].astype(jnp.float32) for p in pieces], axis=0)


def norm_kernel(p0, p1, out):
    out[...] = normalize(joined((p0, p1)))


def second_kernel(xn_a, p2, p3, w_own, w_sib, o_own, o_sib, b_own, b_sib, *outs):
    xn_b = normalize(joined((p2, p3))).astype(jnp.float32)
    xn = jnp.concatenate([xn_a[...].astype(jnp.float32), xn_b], axis=0).astype(jnp.bfloat16)
    quad, slot, level, row, col = kept_place(iota((KEPT, 1), 0))
    row, col = row + 3 * (quad & 1), col + 3 * (quad & 2)
    feat = features(level, row, col, slot < USED, KEPT)
    lane = iota((KEPT, 128), 1)
    j = lane & (FEAT - 1)
    split_levels = core_index() == 1
    split_rows = lax.axis_index("lat") == 0
    ban_level = (j < WL) & (j != level)
    ban_row = (j >= F_Y) & (j < F_Y + WY) & ((j >= F_Y + SY) != (row >= SY))
    ban = jnp.where(ban_level, split_levels.astype(jnp.int32), jnp.where(ban_row, split_rows.astype(jnp.int32), 0))
    ban = jnp.where((lane & FEAT) == 0, ban, 0) == 1
    parts = []
    for weight, bias in ((w_own, b_own), (w_sib, b_sib)):
        q = (dot(xn, weight[0]) * HD**-0.5).astype(jnp.bfloat16)
        k = dot(xn, weight[1]).astype(jnp.bfloat16)
        v = dot(xn, weight[2]).astype(jnp.bfloat16)
        extra = dot(feat[:, :FEAT], bias[...])
        for pair in range(2):
            cols = pair_cols(pair)
            parts.append((q[:, cols], k[:, cols], v[:, cols], jnp.where(ban, NEG, extra[:, cols]).astype(jnp.bfloat16)))
    heads = attend(parts, feat)
    total = dot(jnp.concatenate(heads[:2], axis=1), o_own[...])
    total = total + dot(jnp.concatenate(heads[2:], axis=1), o_sib[...])
    store_halves(total, outs)


def gelu(x):
    return 0.5 * x * (1.0 + lax.erf(x * np.float32(np.sqrt(0.5))))


def mlp_kernel(mine, other, p0, p1, u0, u1, d0, d1, out):
    second = joined((p0, p1)) + branch_sum(mine, other)
    second = second.astype(jnp.bfloat16).astype(jnp.float32)
    xn = normalize(second)
    h0 = gelu(dot(xn, u0[...])).astype(jnp.bfloat16)
    h1 = gelu(dot(xn, u1[...])).astype(jnp.bfloat16)
    out[...] = (0.5 * second + dot(h0, d0[...]) + dot(h1, d1[...])).astype(jnp.bfloat16)


def sum_kernel(mine, other, *outs):
    total = mine[...].astype(jnp.float32) + other[...].astype(jnp.float32)
    for p in range(2):
        outs[p][...] = total[p * ROWS : (p + 1) * ROWS].astype(jnp.bfloat16)


def join_kernel(p0, p1, out):
    out[...] = joined((p0, p1)).astype(jnp.bfloat16)


def place_kernel(m0, m1, s0, s1, out, held, sems):
    core = core_index()
    quad, slot, level, row, col = kept_place(iota((1, KEPT), 1))
    row, col = patch_place(quad, row, col)
    places, sources = [], []
    for chosen, parts in ((core, (m0, m1)), (1 - core, (s0, s1))):
        place = (row * 12 + col) * 4 + real_level(level, chosen)
        places.append(jnp.where(slot < USED, place, -1))
        sources.append(jnp.concatenate([part[...] for part in parts], axis=0))
    count = PATCH // 2
    copies = []
    for h in range(2):
        index = iota((count, KEPT), 0) + h * count
        total = dot(one_hot(index == places[0]), sources[0]) + dot(one_hot(index == places[1]), sources[1])
        rows = pl.ds(h * count // 4, count // 4)
        held[rows] = total.reshape(count // 4, 4, -1).astype(jnp.bfloat16)
        copies.append(pltpu.make_async_copy(held.at[rows], out.at[rows], sems.at[h]))
        copies[h].start()
    for copy in copies:
        copy.wait()


def place_rows(shape, operands):
    return pl.pallas_call(
        place_kernel,
        out_shape=jax.ShapeDtypeStruct(shape, jnp.bfloat16),
        in_specs=[pl.BlockSpec(memory_space=pltpu.VMEM)] * 4,
        out_specs=pl.BlockSpec(memory_space=pl.ANY),
        scratch_shapes=[pltpu.VMEM(shape, jnp.bfloat16), pltpu.SemaphoreType.DMA((2,))],
        compiler_params=pltpu.CompilerParams(vmem_limit_bytes=12 * MIB),
        cost_estimate=pl.CostEstimate(flops=2 * 10**8, bytes_accessed=2 * 10**6, transcendentals=0),
    )(*operands)


def call(kernel, outs, operands, flops, limit, table=False):
    shapes = [jax.ShapeDtypeStruct(s, jnp.bfloat16) for s in outs]
    moved = sum(o.size * o.dtype.itemsize for o in operands) + sum(2 * s.size for s in shapes)
    result = pl.pallas_call(
        kernel,
        out_shape=shapes,
        in_specs=[pl.BlockSpec(memory_space=pltpu.SMEM if table else pltpu.VMEM)] * len(operands),
        out_specs=[pl.BlockSpec(memory_space=pltpu.VMEM)] * len(shapes),
        compiler_params=pltpu.CompilerParams(vmem_limit_bytes=limit * MIB),
        cost_estimate=pl.CostEstimate(flops=flops, bytes_accessed=moved, transcendentals=0),
    )(*operands)
    return result if len(result) > 1 else result[0]


def tied(*values):
    return lax.optimization_barrier(values)


def body(counts, tokens, qkv_first, qkv_second, out_first, out_second, rel_tables, up_weight, down_weight):
    levels, rows, cols, width = tokens.shape
    turn = counts[1] // 2

    def move(value, target):
        return lax.ppermute(value, AXES, pairs(counts, target))

    def core_swap(value):
        return move(value, lambda a, b, m: (a, b, m ^ 1))

    def chip_swap(value):
        return move(value, lambda a, b, m: (a, b, m ^ 2))

    def out_to(value, dy, dx):
        return move(value, lambda a, b, m: (a + dy, b + dx, m ^ 2 if dx and (b + 1) % turn == 0 else m))

    def home(value, dy, dx):
        return move(value, lambda a, b, m: (a - dy, b - dx, m ^ 2 if dx and b % turn == 0 else m))

    half, piece = [(HALF, width)], [(ROWS, width)]
    heads, features = [(KEPT, 256)], [(FEAT, 256)]

    tok = tokens.transpose(1, 2, 0, 3).reshape(rows * cols, levels, width)
    w_first = qkv_first.transpose(1, 0, 2)
    w_second = qkv_second.transpose(1, 0, 2)

    f1 = core_swap(out_first)
    s1 = core_swap(out_second)
    w_sib = core_swap(w_second)
    bias1 = call(functools.partial(bias_kernel, 0), features, (rel_tables,), 5 * 10**9, 4, table=True)
    keep, give = call(first_kernel, heads * 2, (tok, w_first, bias1), 10**9, 16)
    keep, give, f1 = tied(keep, give, f1)
    keep, tok, rel_tables = tied(keep, tok, rel_tables)
    base_a, base_lat, base_own = call(base_kernel, half + piece * 2, (tok,), 10**9, 8)
    bias2 = call(functools.partial(bias_kernel, 1), features, (rel_tables,), 10**9, 4, table=True)
    bias2_sib = core_swap(bias2)
    given, up_late, s1, w_sib, down_late = tied(core_swap(give), up_weight, s1, w_sib, down_weight)
    d1 = core_swap(down_late)
    u1 = core_swap(up_late)
    part_a, part_lat, part_own = call(partial_kernel, half + piece * 2, (keep, given, out_first, f1), 2 * 10**8, 8)
    other_a = chip_swap(part_a)
    other_lat = chip_swap(part_lat)
    other_own = chip_swap(part_own)
    other_a, bias2_sib, d1 = tied(other_a, bias2_sib, d1)
    diag, lon = call(residual_kernel, piece * 2, (part_a, other_a, base_a), 10**6, 8)
    diag, lon, part_lat = tied(diag, lon, part_lat)
    lat = call(residual_kernel, piece, (part_lat, other_lat, base_lat), 10**10, 8)
    lat, part_own = tied(lat, part_own)
    own = call(residual_kernel, piece, (part_own, other_own, base_own), 10**6, 8)
    diag = out_to(diag, 1, 1)
    lon = out_to(lon, 0, 1)
    lat = out_to(lat, 1, 0)

    xn_a = call(norm_kernel, half, (diag, lon), 10**10, 8)
    part_a, part_b = call(
        second_kernel,
        half * 2,
        (xn_a, lat, own, w_second, w_sib, out_second, s1, bias2, bias2_sib),
        10**9,
        16,
    )
    other_a = chip_swap(part_a)
    other_b = chip_swap(part_b)
    mlp = (up_weight, u1, down_weight, d1)
    part_a = call(mlp_kernel, half, (part_a, other_a, diag, lon, *mlp), 10**9, 20)
    part_a, part_b = tied(part_a, part_b)
    other_a = chip_swap(part_a)
    part_b = call(mlp_kernel, half, (part_b, other_b, lat, own, *mlp), 10**9, 20)
    other_b = chip_swap(part_b)
    diag, lon = call(sum_kernel, piece * 2, (part_a, other_a), 10**6, 8)
    diag, lon, part_b = tied(diag, lon, part_b)
    diag = home(diag, 1, 1)
    lon = home(lon, 0, 1)
    lat, own = call(sum_kernel, piece * 2, (part_b, other_b), 10**10, 8)
    lat = home(lat, 1, 0)
    mine_a = call(join_kernel, half, (diag, lon), 10**10, 8)
    mine_a, lat, own = tied(mine_a, lat, own)
    mine_b = call(join_kernel, half, (lat, own), 10**6, 8)
    operands = (mine_a, mine_b, core_swap(mine_a), core_swap(mine_b))
    result = place_rows((rows * cols, levels, width), operands)
    return result.reshape(rows, cols, levels, width).transpose(2, 0, 1, 3)


def solution(mesh):
    counts = tuple(mesh.shape[name] for name in AXES)
    return jax.shard_map(
        functools.partial(body, counts),
        mesh=mesh,
        in_specs=(
            P(None, "lat", "lon", None),
            P(None, None, "mp"),
            P(None, None, "mp"),
            P("mp", None),
            P("mp", None),
            P(None, "mp", None),
            P(None, "mp"),
            P("mp", None),
        ),
        out_specs=P(None, "lat", "lon", None),
        check_vma=False,
    )
```

```python
import functools

import jax
import jax.numpy as jnp
import numpy as np
from jax import lax
from jax.experimental import pallas as pl
from jax.experimental.pallas import tpu as pltpu
from jax.sharding import PartitionSpec as P

WL = 2
WY = 6
WX = 12
SY = 3
SX = 6
HD = 64
NEG = -1000000000.0
AXES = ("lat", "lon", "mp")
MIB = 1024 * 1024

USED = 36
ROWS = 40
KEPT = 4 * ROWS
HALF = 2 * ROWS
PATCH = 4 * WY * WX
WINDOW = WL * WY * WX
FEAT = 32
F_Y = 4
F_X = 10
F_PAD = 22


def pairs(counts, target):
    lats, lons, mps = counts
    result = []
    for a in range(lats):
        for b in range(lons):
            for m in range(mps):
                ta, tb, tm = target(a, b, m)
                dest = ((ta % lats) * lons + tb % lons) * mps + tm
                result.append(((a * lons + b) * mps + m, dest))
    return result


def dot(left, right):
    return jnp.dot(left, right, preferred_element_type=jnp.float32)


def dot_t(left, right):
    return lax.dot_general(left, right, (((1,), (1,)), ((), ())), preferred_element_type=jnp.float32)


def normalize(floats):
    center = floats - jnp.mean(floats, axis=-1, keepdims=True)
    spread = jnp.mean(center * center, axis=-1, keepdims=True)
    return (center * lax.rsqrt(spread + 1e-05)).astype(jnp.bfloat16)


def core_index():
    return lax.rem(lax.axis_index("mp"), 2)


def iota(shape, axis):
    return lax.broadcasted_iota(jnp.int32, shape, axis)


def one_hot(condition):
    return jnp.where(condition, 1.0, 0.0).astype(jnp.bfloat16)


def piece_place(slot):
    level = (slot * 57) >> 10
    rest = slot - level * 18
    row = (rest * 43) >> 8
    return level, row, rest - row * 6


def kept_place(index):
    quad = (index * 205) >> 13
    slot = index - quad * ROWS
    return (quad, slot) + piece_place(slot)


def real_level(level, core):
    return jnp.where(core == 0, 1 + level, 3 - 3 * level)


def patch_place(q, row, col):
    return row + 3 - 3 * (q & 1), col + 6 - 3 * (q & 2)


def bias_rows(table, block, pair):
    shape = (FEAT, 4 * FEAT)
    i, lane = iota(shape, 0), iota(shape, 1)
    j = lane & (FEAT - 1)
    kind = jnp.full(shape, 37, jnp.int32)
    kind = jnp.where((i < WL) & (j < WL), i - j + 1, kind)
    kind = jnp.where((i < WL) & (j == F_PAD), 38, kind)
    in_y = (i >= F_Y) & (i < F_Y + WY) & (j >= F_Y) & (j < F_Y + WY)
    kind = jnp.where(in_y, 3 + i - j + 5, kind)
    in_x = (i >= F_X) & (i < F_X + WX) & (j >= F_X) & (j < F_X + WX)
    kind = jnp.where(in_x, 14 + i - j + 11, kind)
    total = jnp.where(kind == 38, NEG, 0.0)
    for k in range(37):
        value = jnp.where(lane < HD, table[block, 2 * pair + 1, k], table[block, 2 * pair, k])
        total = jnp.where(kind == k, value, total)
    high = total.astype(jnp.bfloat16).astype(jnp.float32)
    return jnp.where((lane & FEAT) != 0, total - high, high).astype(jnp.bfloat16)


def bias_kernel(block, table, out):
    for pair in range(2):
        out[:, pair * 128 : pair * 128 + 128] = bias_rows(table, block, pair)


def features(level, row, col, used, count):
    j = iota((count, 128), 1) & (FEAT - 1)
    hit = (j == level) | (j == F_Y + row) | (j == F_X + col)
    return one_hot(jnp.where(used, jnp.where(hit, 1, 0), jnp.where(j == F_PAD, 1, 0)) == 1)


def attend(parts, key_feat):
    low = iota(parts[0][0].shape, 1) < HD
    none = jnp.zeros_like(parts[0][0])
    count = none.shape[0]
    scores = []
    for query, key, _, extra in parts:
        upper = jnp.concatenate([jnp.where(low, query, none), jnp.where(low, none, extra)], axis=1)
        lower = jnp.concatenate([jnp.where(low, none, query), jnp.where(low, extra, none)], axis=1)
        both = jnp.concatenate([upper, lower], axis=0)
        scores.append(dot_t(both, jnp.concatenate([key, key_feat], axis=1)))
    expos, scales = [], []
    for score in scores:
        expo = jnp.exp(score - jnp.max(score, axis=-1, keepdims=True))
        expos.append(expo.astype(jnp.bfloat16))
        scales.append(1.0 / jnp.sum(expo, axis=-1, keepdims=True))
    results = []
    for (_, _, value, _), expo, scale in zip(parts, expos, scales):
        mixed = dot(expo, value) * scale
        results.append(jnp.where(low, mixed[:count], mixed[count:]).astype(jnp.bfloat16))
    return results


def pair_cols(pair):
    return slice(pair * 128, pair * 128 + 128)


def first_kernel(tokens, weight, bias, keep, give):
    core = core_index()
    floats = tokens[...].astype(jnp.float32).reshape(PATCH, -1)
    xn = normalize(floats)
    q = (dot(xn, weight[0]) * HD**-0.5).astype(jnp.bfloat16)
    k = dot(xn, weight[1]).astype(jnp.bfloat16)
    v = dot(xn, weight[2]).astype(jnp.bfloat16)
    index = iota((PATCH, 1), 0)
    level = (index * 911) >> 16
    order = one_hot(iota((PATCH, PATCH), 1) == (index - 72 * level) * 4 + level)
    q, k, v = (dot(order, part).astype(jnp.bfloat16) for part in (q, k, v))
    index = iota((WINDOW, 1), 0)
    level = (index * 911) >> 16
    rest = index - 72 * level
    row = (rest * 171) >> 11
    feat = features(level, row, rest - 12 * row, index >= 0, WINDOW)
    extra = dot(feat[:, :FEAT], bias[...]).astype(jnp.bfloat16)
    parts = []
    for w in range(2):
        rows = slice(w * WINDOW, (w + 1) * WINDOW)
        for pair in range(2):
            cols = pair_cols(pair)
            parts.append((q[rows, cols], k[rows, cols], v[rows, cols], extra[:, cols]))
    heads = attend(parts, feat)
    windows = [jnp.concatenate(heads[2 * w : 2 * w + 2], axis=1) for w in range(2)]
    mixed = jnp.concatenate(windows, axis=0)
    quad, slot, level, row, col = kept_place(iota((KEPT, 1), 0))
    row, col = patch_place(quad, row, col)
    lanes = iota((KEPT, PATCH), 1)
    for out, chosen in ((keep, core), (give, 1 - core)):
        place = real_level(level, chosen) * 72 + row * 12 + col
        place = jnp.where(slot < USED, place, -1)
        out[...] = dot(one_hot(lanes == place), mixed).astype(jnp.bfloat16)


def base_kernel(tokens, *outs):
    values = tokens[...].astype(jnp.float32).reshape(PATCH, -1).astype(jnp.bfloat16)
    quad, slot, level, row, col = kept_place(iota((KEPT, 1), 0))
    row, col = patch_place(quad, row, col)
    place = (row * 12 + col) * 4 + real_level(level, core_index())
    place = jnp.where(slot < USED, place, -1)
    store_three(dot(one_hot(iota((KEPT, PATCH), 1) == place), values), outs)


def store_halves(total, outs):
    for h in range(2):
        outs[h][...] = total[h * HALF : (h + 1) * HALF].astype(jnp.bfloat16)


def store_three(total, outs):
    for out, start, stop in zip(outs, (0, 2 * ROWS, 3 * ROWS), (2 * ROWS, 3 * ROWS, KEPT)):
        out[...] = total[start:stop].astype(jnp.bfloat16)


def partial_kernel(o0, o1, w0, w1, *outs):
    store_three(dot(o0[...], w0[...]) + dot(o1[...], w1[...]), outs)


def branch_sum(mine, other):
    total = mine[...].astype(jnp.float32) + other[...].astype(jnp.float32)
    return total.astype(jnp.bfloat16).astype(jnp.float32)


def residual_kernel(mine, other, base, *outs):
    first = base[...].astype(jnp.float32) + branch_sum(mine, other)
    for p, out in enumerate(outs):
        out[...] = first[p * ROWS : (p + 1) * ROWS].astype(jnp.bfloat16)


def joined(pieces):
    return jnp.concatenate([p[...].astype(jnp.float32) for p in pieces], axis=0)


def norm_kernel(p0, p1, out):
    out[...] = normalize(joined((p0, p1)))


def second_kernel(xn_a, p2, p3, w_own, w_sib, o_own, o_sib, b_own, b_sib, *outs):
    xn_b = normalize(joined((p2, p3))).astype(jnp.float32)
    xn = jnp.concatenate([xn_a[...].astype(jnp.float32), xn_b], axis=0).astype(jnp.bfloat16)
    quad, slot, level, row, col = kept_place(iota((KEPT, 1), 0))
    row, col = row + 3 * (quad & 1), col + 3 * (quad & 2)
    feat = features(level, row, col, slot < USED, KEPT)
    lane = iota((KEPT, 128), 1)
    j = lane & (FEAT - 1)
    split_levels = core_index() == 1
    split_rows = lax.axis_index("lat") == 0
    ban_level = (j < WL) & (j != level)
    ban_row = (j >= F_Y) & (j < F_Y + WY) & ((j >= F_Y + SY) != (row >= SY))
    ban = jnp.where(ban_level, split_levels.astype(jnp.int32), jnp.where(ban_row, split_rows.astype(jnp.int32), 0))
    ban = jnp.where((lane & FEAT) == 0, ban, 0) == 1
    parts = []
    for weight, bias in ((w_own, b_own), (w_sib, b_sib)):
        q = (dot(xn, weight[0]) * HD**-0.5).astype(jnp.bfloat16)
        k = dot(xn, weight[1]).astype(jnp.bfloat16)
        v = dot(xn, weight[2]).astype(jnp.bfloat16)
        extra = dot(feat[:, :FEAT], bias[...])
        for pair in range(2):
            cols = pair_cols(pair)
            parts.append((q[:, cols], k[:, cols], v[:, cols], jnp.where(ban, NEG, extra[:, cols]).astype(jnp.bfloat16)))
    heads = attend(parts, feat)
    mixed = jnp.concatenate(heads, axis=1)
    project_kernel(mixed[:HALF], o_own, o_sib, outs[0])
    outs[1][...] = mixed[HALF:]


def project_kernel(mixed, o_own, o_sib, out):
    total = dot(mixed[:, :256], o_own[...]) + dot(mixed[:, 256:], o_sib[...])
    out[...] = total.astype(jnp.bfloat16)


def gelu(x):
    return 0.5 * x * (1.0 + lax.erf(x * np.float32(np.sqrt(0.5))))


def mlp_kernel(mine, other, p0, p1, u0, u1, d0, d1, out):
    second = joined((p0, p1)) + branch_sum(mine, other)
    second = second.astype(jnp.bfloat16).astype(jnp.float32)
    xn = normalize(second)
    h0 = gelu(dot(xn, u0[...])).astype(jnp.bfloat16)
    h1 = gelu(dot(xn, u1[...])).astype(jnp.bfloat16)
    out[...] = (0.5 * second + dot(h0, d0[...]) + dot(h1, d1[...])).astype(jnp.bfloat16)


def sum_kernel(mine, other, *outs):
    total = mine[...].astype(jnp.float32) + other[...].astype(jnp.float32)
    for p in range(2):
        outs[p][...] = total[p * ROWS : (p + 1) * ROWS].astype(jnp.bfloat16)


def join_kernel(p0, p1, out):
    out[...] = joined((p0, p1)).astype(jnp.bfloat16)


def place_kernel(m0, m1, s0, s1, out, held, sems):
    core = core_index()
    quad, slot, level, row, col = kept_place(iota((1, KEPT), 1))
    row, col = patch_place(quad, row, col)
    places, sources = [], []
    for chosen, parts in ((core, (m0, m1)), (1 - core, (s0, s1))):
        place = (row * 12 + col) * 4 + real_level(level, chosen)
        places.append(jnp.where(slot < USED, place, -1))
        sources.append(jnp.concatenate([part[...] for part in parts], axis=0))
    count = PATCH // 2
    copies = []
    for h in range(2):
        index = iota((count, KEPT), 0) + h * count
        total = dot(one_hot(index == places[0]), sources[0]) + dot(one_hot(index == places[1]), sources[1])
        rows = pl.ds(h * count // 4, count // 4)
        held[rows] = total.reshape(count // 4, 4, -1).astype(jnp.bfloat16)
        copies.append(pltpu.make_async_copy(held.at[rows], out.at[rows], sems.at[h]))
        copies[h].start()
    for copy in copies:
        copy.wait()


def place_rows(shape, operands):
    return pl.pallas_call(
        place_kernel,
        out_shape=jax.ShapeDtypeStruct(shape, jnp.bfloat16),
        in_specs=[pl.BlockSpec(memory_space=pltpu.VMEM)] * 4,
        out_specs=pl.BlockSpec(memory_space=pl.ANY),
        scratch_shapes=[pltpu.VMEM(shape, jnp.bfloat16), pltpu.SemaphoreType.DMA((2,))],
        compiler_params=pltpu.CompilerParams(vmem_limit_bytes=12 * MIB),
        cost_estimate=pl.CostEstimate(flops=2 * 10**8, bytes_accessed=2 * 10**6, transcendentals=0),
    )(*operands)


def call(kernel, outs, operands, flops, limit, table=False):
    shapes = [jax.ShapeDtypeStruct(s, jnp.bfloat16) for s in outs]
    moved = sum(o.size * o.dtype.itemsize for o in operands) + sum(2 * s.size for s in shapes)
    result = pl.pallas_call(
        kernel,
        out_shape=shapes,
        in_specs=[pl.BlockSpec(memory_space=pltpu.SMEM if table else pltpu.VMEM)] * len(operands),
        out_specs=[pl.BlockSpec(memory_space=pltpu.VMEM)] * len(shapes),
        compiler_params=pltpu.CompilerParams(vmem_limit_bytes=limit * MIB),
        cost_estimate=pl.CostEstimate(flops=flops, bytes_accessed=moved, transcendentals=0),
    )(*operands)
    return result if len(result) > 1 else result[0]


def tied(*values):
    return lax.optimization_barrier(values)


def body(counts, tokens, qkv_first, qkv_second, out_first, out_second, rel_tables, up_weight, down_weight):
    levels, rows, cols, width = tokens.shape
    turn = counts[1] // 2

    def move(value, target):
        return lax.ppermute(value, AXES, pairs(counts, target))

    def core_swap(value):
        return move(value, lambda a, b, m: (a, b, m ^ 1))

    def chip_swap(value):
        return move(value, lambda a, b, m: (a, b, m ^ 2))

    def out_to(value, dy, dx):
        return move(value, lambda a, b, m: (a + dy, b + dx, m ^ 2 if dx and (b + 1) % turn == 0 else m))

    def home(value, dy, dx):
        return move(value, lambda a, b, m: (a - dy, b - dx, m ^ 2 if dx and b % turn == 0 else m))

    half, piece = [(HALF, width)], [(ROWS, width)]
    heads, features = [(KEPT, 256)], [(FEAT, 256)]

    tok = tokens.transpose(1, 2, 0, 3).reshape(rows * cols, levels, width)
    w_first = qkv_first.transpose(1, 0, 2)
    w_second = qkv_second.transpose(1, 0, 2)

    f1 = core_swap(out_first)
    s1 = core_swap(out_second)
    w_sib = core_swap(w_second)
    bias1 = call(functools.partial(bias_kernel, 0), features, (rel_tables,), 5 * 10**9, 4, table=True)
    keep, give = call(first_kernel, heads * 2, (tok, w_first, bias1), 10**9, 16)
    keep, give, f1 = tied(keep, give, f1)
    keep, tok, rel_tables = tied(keep, tok, rel_tables)
    base_a, base_lat, base_own = call(base_kernel, half + piece * 2, (tok,), 10**9, 8)
    bias2 = call(functools.partial(bias_kernel, 1), features, (rel_tables,), 10**9, 4, table=True)
    bias2_sib = core_swap(bias2)
    given, up_late, s1, w_sib, down_late = tied(core_swap(give), up_weight, s1, w_sib, down_weight)
    d1 = core_swap(down_late)
    u1 = core_swap(up_late)
    part_a, part_lat, part_own = call(partial_kernel, half + piece * 2, (keep, given, out_first, f1), 2 * 10**8, 8)
    other_a = chip_swap(part_a)
    other_lat = chip_swap(part_lat)
    other_own = chip_swap(part_own)
    other_a, bias2_sib, d1 = tied(other_a, bias2_sib, d1)
    diag, lon = call(residual_kernel, piece * 2, (part_a, other_a, base_a), 10**6, 8)
    diag, lon, part_lat = tied(diag, lon, part_lat)
    lat = call(residual_kernel, piece, (part_lat, other_lat, base_lat), 10**10, 8)
    lat, part_own = tied(lat, part_own)
    own = call(residual_kernel, piece, (part_own, other_own, base_own), 10**6, 8)
    diag = out_to(diag, 1, 1)
    lon = out_to(lon, 0, 1)
    lat = out_to(lat, 1, 0)

    xn_a = call(norm_kernel, half, (diag, lon), 10**10, 8)
    part_a, rest = call(
        second_kernel,
        half + [(HALF, 512)],
        (xn_a, lat, own, w_second, w_sib, out_second, s1, bias2, bias2_sib),
        10**9,
        16,
    )
    other_a = chip_swap(part_a)
    part_b = call(project_kernel, half, (rest, out_second, s1), 10**10, 8)
    other_b = chip_swap(part_b)
    mlp = (up_weight, u1, down_weight, d1)
    part_a = call(mlp_kernel, half, (part_a, other_a, diag, lon, *mlp), 10**9, 20)
    part_a, part_b = tied(part_a, part_b)
    other_a = chip_swap(part_a)
    part_b = call(mlp_kernel, half, (part_b, other_b, lat, own, *mlp), 10**9, 20)
    other_b = chip_swap(part_b)
    diag, lon = call(sum_kernel, piece * 2, (part_a, other_a), 10**6, 8)
    diag, lon, part_b = tied(diag, lon, part_b)
    diag = home(diag, 1, 1)
    lon = home(lon, 0, 1)
    lat, own = call(sum_kernel, piece * 2, (part_b, other_b), 10**10, 8)
    lat = home(lat, 1, 0)
    mine_a = call(join_kernel, half, (diag, lon), 10**10, 8)
    mine_a, lat, own = tied(mine_a, lat, own)
    mine_b = call(join_kernel, half, (lat, own), 10**6, 8)
    operands = (mine_a, mine_b, core_swap(mine_a), core_swap(mine_b))
    result = place_rows((rows * cols, levels, width), operands)
    return result.reshape(rows, cols, levels, width).transpose(2, 0, 1, 3)


def solution(mesh):
    counts = tuple(mesh.shape[name] for name in AXES)
    return jax.shard_map(
        functools.partial(body, counts),
        mesh=mesh,
        in_specs=(
            P(None, "lat", "lon", None),
            P(None, None, "mp"),
            P(None, None, "mp"),
            P("mp", None),
            P("mp", None),
            P(None, "mp", None),
            P(None, "mp"),
            P("mp", None),
        ),
        out_specs=P(None, "lat", "lon", None),
        check_vma=False,
    )
```

```python
import functools

import jax
import jax.numpy as jnp
import numpy as np
from jax import lax
from jax.experimental import pallas as pl
from jax.experimental.pallas import tpu as pltpu
from jax.sharding import PartitionSpec as P

WL = 2
WY = 6
WX = 12
SY = 3
SX = 6
HD = 64
NEG = -1000000000.0
AXES = ("lat", "lon", "mp")
MIB = 1024 * 1024

USED = 36
ROWS = 40
KEPT = 4 * ROWS
HALF = 2 * ROWS
PATCH = 4 * WY * WX
WINDOW = WL * WY * WX
FEAT = 32
F_Y = 4
F_X = 10
F_PAD = 22


def pairs(counts, target):
    lats, lons, mps = counts
    result = []
    for a in range(lats):
        for b in range(lons):
            for m in range(mps):
                ta, tb, tm = target(a, b, m)
                dest = ((ta % lats) * lons + tb % lons) * mps + tm
                result.append(((a * lons + b) * mps + m, dest))
    return result


def dot(left, right):
    return jnp.dot(left, right, preferred_element_type=jnp.float32)


def dot_t(left, right):
    return lax.dot_general(left, right, (((1,), (1,)), ((), ())), preferred_element_type=jnp.float32)


def normalize(floats):
    center = floats - jnp.mean(floats, axis=-1, keepdims=True)
    spread = jnp.mean(center * center, axis=-1, keepdims=True)
    return (center * lax.rsqrt(spread + 1e-05)).astype(jnp.bfloat16)


def core_index():
    return lax.rem(lax.axis_index("mp"), 2)


def iota(shape, axis):
    return lax.broadcasted_iota(jnp.int32, shape, axis)


def one_hot(condition):
    return jnp.where(condition, 1.0, 0.0).astype(jnp.bfloat16)


def piece_place(slot):
    level = (slot * 57) >> 10
    rest = slot - level * 18
    row = (rest * 43) >> 8
    return level, row, rest - row * 6


def kept_place(index):
    quad = (index * 205) >> 13
    slot = index - quad * ROWS
    return (quad, slot) + piece_place(slot)


def real_level(level, core):
    return jnp.where(core == 0, 1 + level, 3 - 3 * level)


def patch_place(q, row, col):
    return row + 3 - 3 * (q & 1), col + 6 - 3 * (q & 2)


def bias_rows(table, block, pair):
    shape = (FEAT, 4 * FEAT)
    i, lane = iota(shape, 0), iota(shape, 1)
    j = lane & (FEAT - 1)
    kind = jnp.full(shape, 37, jnp.int32)
    kind = jnp.where((i < WL) & (j < WL), i - j + 1, kind)
    kind = jnp.where((i < WL) & (j == F_PAD), 38, kind)
    in_y = (i >= F_Y) & (i < F_Y + WY) & (j >= F_Y) & (j < F_Y + WY)
    kind = jnp.where(in_y, 3 + i - j + 5, kind)
    in_x = (i >= F_X) & (i < F_X + WX) & (j >= F_X) & (j < F_X + WX)
    kind = jnp.where(in_x, 14 + i - j + 11, kind)
    total = jnp.where(kind == 38, NEG, 0.0)
    for k in range(37):
        value = jnp.where(lane < HD, table[block, 2 * pair + 1, k], table[block, 2 * pair, k])
        total = jnp.where(kind == k, value, total)
    high = total.astype(jnp.bfloat16).astype(jnp.float32)
    return jnp.where((lane & FEAT) != 0, total - high, high).astype(jnp.bfloat16)


def bias_kernel(block, table, out):
    for pair in range(2):
        out[:, pair * 128 : pair * 128 + 128] = bias_rows(table, block, pair)


def features(level, row, col, used, count):
    j = iota((count, 128), 1) & (FEAT - 1)
    hit = (j == level) | (j == F_Y + row) | (j == F_X + col)
    return one_hot(jnp.where(used, jnp.where(hit, 1, 0), jnp.where(j == F_PAD, 1, 0)) == 1)


def attend(parts, key_feat):
    low = iota(parts[0][0].shape, 1) < HD
    none = jnp.zeros_like(parts[0][0])
    count = none.shape[0]
    scores = []
    for query, key, _, extra in parts:
        upper = jnp.concatenate([jnp.where(low, query, none), jnp.where(low, none, extra)], axis=1)
        lower = jnp.concatenate([jnp.where(low, none, query), jnp.where(low, extra, none)], axis=1)
        both = jnp.concatenate([upper, lower], axis=0)
        scores.append(dot_t(both, jnp.concatenate([key, key_feat], axis=1)))
    expos, scales = [], []
    for score in scores:
        expo = jnp.exp(score - jnp.max(score, axis=-1, keepdims=True))
        expos.append(expo.astype(jnp.bfloat16))
        scales.append(1.0 / jnp.sum(expo, axis=-1, keepdims=True))
    results = []
    for (_, _, value, _), expo, scale in zip(parts, expos, scales):
        mixed = dot(expo, value) * scale
        results.append(jnp.where(low, mixed[:count], mixed[count:]).astype(jnp.bfloat16))
    return results


def pair_cols(pair):
    return slice(pair * 128, pair * 128 + 128)


def first_kernel(tokens, weight, bias, keep, give):
    core = core_index()
    floats = tokens[...].astype(jnp.float32).reshape(PATCH, -1)
    xn = normalize(floats)
    q = (dot(xn, weight[0]) * HD**-0.5).astype(jnp.bfloat16)
    k = dot(xn, weight[1]).astype(jnp.bfloat16)
    v = dot(xn, weight[2]).astype(jnp.bfloat16)
    index = iota((PATCH, 1), 0)
    level = (index * 911) >> 16
    order = one_hot(iota((PATCH, PATCH), 1) == (index - 72 * level) * 4 + level)
    q, k, v = (dot(order, part).astype(jnp.bfloat16) for part in (q, k, v))
    index = iota((WINDOW, 1), 0)
    level = (index * 911) >> 16
    rest = index - 72 * level
    row = (rest * 171) >> 11
    feat = features(level, row, rest - 12 * row, index >= 0, WINDOW)
    extra = dot(feat[:, :FEAT], bias[...]).astype(jnp.bfloat16)
    parts = []
    for w in range(2):
        rows = slice(w * WINDOW, (w + 1) * WINDOW)
        for pair in range(2):
            cols = pair_cols(pair)
            parts.append((q[rows, cols], k[rows, cols], v[rows, cols], extra[:, cols]))
    heads = attend(parts, feat)
    windows = [jnp.concatenate(heads[2 * w : 2 * w + 2], axis=1) for w in range(2)]
    mixed = jnp.concatenate(windows, axis=0)
    quad, slot, level, row, col = kept_place(iota((KEPT, 1), 0))
    row, col = patch_place(quad, row, col)
    lanes = iota((KEPT, PATCH), 1)
    for out, chosen in ((keep, core), (give, 1 - core)):
        place = real_level(level, chosen) * 72 + row * 12 + col
        place = jnp.where(slot < USED, place, -1)
        out[...] = dot(one_hot(lanes == place), mixed).astype(jnp.bfloat16)


def base_kernel(tokens, *outs):
    values = tokens[...].astype(jnp.float32).reshape(PATCH, -1).astype(jnp.bfloat16)
    quad, slot, level, row, col = kept_place(iota((KEPT, 1), 0))
    row, col = patch_place(quad, row, col)
    place = (row * 12 + col) * 4 + real_level(level, core_index())
    place = jnp.where(slot < USED, place, -1)
    store_three(dot(one_hot(iota((KEPT, PATCH), 1) == place), values), outs)


def store_halves(total, outs):
    for h in range(2):
        outs[h][...] = total[h * HALF : (h + 1) * HALF].astype(jnp.bfloat16)


def store_three(total, outs):
    for out, start, stop in zip(outs, (0, 2 * ROWS, 3 * ROWS), (2 * ROWS, 3 * ROWS, KEPT)):
        out[...] = total[start:stop].astype(jnp.bfloat16)


def partial_kernel(half, o0, o1, w0, w1, *outs):
    rows = slice(half * HALF, (half + 1) * HALF)
    total = dot(o0[rows], w0[...]) + dot(o1[rows], w1[...])
    count = HALF // len(outs)
    for p, out in enumerate(outs):
        out[...] = total[p * count : (p + 1) * count].astype(jnp.bfloat16)


def branch_sum(mine, other):
    total = mine[...].astype(jnp.float32) + other[...].astype(jnp.float32)
    return total.astype(jnp.bfloat16).astype(jnp.float32)


def residual_kernel(mine, other, base, *outs):
    first = base[...].astype(jnp.float32) + branch_sum(mine, other)
    for p, out in enumerate(outs):
        out[...] = first[p * ROWS : (p + 1) * ROWS].astype(jnp.bfloat16)


def joined(pieces):
    return jnp.concatenate([p[...].astype(jnp.float32) for p in pieces], axis=0)


def norm_kernel(p0, p1, out):
    out[...] = normalize(joined((p0, p1)))


def second_kernel(xn_a, p2, p3, w_own, w_sib, o_own, o_sib, b_own, b_sib, *outs):
    xn_b = normalize(joined((p2, p3))).astype(jnp.float32)
    xn = jnp.concatenate([xn_a[...].astype(jnp.float32), xn_b], axis=0).astype(jnp.bfloat16)
    quad, slot, level, row, col = kept_place(iota((KEPT, 1), 0))
    row, col = row + 3 * (quad & 1), col + 3 * (quad & 2)
    feat = features(level, row, col, slot < USED, KEPT)
    lane = iota((KEPT, 128), 1)
    j = lane & (FEAT - 1)
    split_levels = core_index() == 1
    split_rows = lax.axis_index("lat") == 0
    ban_level = (j < WL) & (j != level)
    ban_row = (j >= F_Y) & (j < F_Y + WY) & ((j >= F_Y + SY) != (row >= SY))
    ban = jnp.where(ban_level, split_levels.astype(jnp.int32), jnp.where(ban_row, split_rows.astype(jnp.int32), 0))
    ban = jnp.where((lane & FEAT) == 0, ban, 0) == 1
    parts = []
    for weight, bias in ((w_own, b_own), (w_sib, b_sib)):
        q = (dot(xn, weight[0]) * HD**-0.5).astype(jnp.bfloat16)
        k = dot(xn, weight[1]).astype(jnp.bfloat16)
        v = dot(xn, weight[2]).astype(jnp.bfloat16)
        extra = dot(feat[:, :FEAT], bias[...])
        for pair in range(2):
            cols = pair_cols(pair)
            parts.append((q[:, cols], k[:, cols], v[:, cols], jnp.where(ban, NEG, extra[:, cols]).astype(jnp.bfloat16)))
    heads = attend(parts, feat)
    mixed = jnp.concatenate(heads, axis=1)
    project_kernel(mixed[:HALF], o_own, o_sib, outs[0])
    outs[1][...] = mixed[HALF:]


def project_kernel(mixed, o_own, o_sib, out):
    total = dot(mixed[:, :256], o_own[...]) + dot(mixed[:, 256:], o_sib[...])
    out[...] = total.astype(jnp.bfloat16)


def gelu(x):
    return 0.5 * x * (1.0 + lax.erf(x * np.float32(np.sqrt(0.5))))


def mlp_kernel(mine, other, p0, p1, u0, u1, d0, d1, out):
    second = joined((p0, p1)) + branch_sum(mine, other)
    second = second.astype(jnp.bfloat16).astype(jnp.float32)
    xn = normalize(second)
    h0 = gelu(dot(xn, u0[...])).astype(jnp.bfloat16)
    h1 = gelu(dot(xn, u1[...])).astype(jnp.bfloat16)
    out[...] = (0.5 * second + dot(h0, d0[...]) + dot(h1, d1[...])).astype(jnp.bfloat16)


def sum_kernel(mine, other, *outs):
    total = mine[...].astype(jnp.float32) + other[...].astype(jnp.float32)
    for p in range(2):
        outs[p][...] = total[p * ROWS : (p + 1) * ROWS].astype(jnp.bfloat16)


def join_kernel(p0, p1, out):
    out[...] = joined((p0, p1)).astype(jnp.bfloat16)


def place_kernel(m0, m1, s0, s1, out, held, sems):
    core = core_index()
    quad, slot, level, row, col = kept_place(iota((1, KEPT), 1))
    row, col = patch_place(quad, row, col)
    places, sources = [], []
    for chosen, parts in ((core, (m0, m1)), (1 - core, (s0, s1))):
        place = (row * 12 + col) * 4 + real_level(level, chosen)
        places.append(jnp.where(slot < USED, place, -1))
        sources.append(jnp.concatenate([part[...] for part in parts], axis=0))
    count = PATCH // 2
    copies = []
    for h in range(2):
        index = iota((count, KEPT), 0) + h * count
        total = dot(one_hot(index == places[0]), sources[0]) + dot(one_hot(index == places[1]), sources[1])
        rows = pl.ds(h * count // 4, count // 4)
        held[rows] = total.reshape(count // 4, 4, -1).astype(jnp.bfloat16)
        copies.append(pltpu.make_async_copy(held.at[rows], out.at[rows], sems.at[h]))
        copies[h].start()
    for copy in copies:
        copy.wait()


def place_rows(shape, operands):
    return pl.pallas_call(
        place_kernel,
        out_shape=jax.ShapeDtypeStruct(shape, jnp.bfloat16),
        in_specs=[pl.BlockSpec(memory_space=pltpu.VMEM)] * 4,
        out_specs=pl.BlockSpec(memory_space=pl.ANY),
        scratch_shapes=[pltpu.VMEM(shape, jnp.bfloat16), pltpu.SemaphoreType.DMA((2,))],
        compiler_params=pltpu.CompilerParams(vmem_limit_bytes=12 * MIB),
        cost_estimate=pl.CostEstimate(flops=2 * 10**8, bytes_accessed=2 * 10**6, transcendentals=0),
    )(*operands)


def call(kernel, outs, operands, flops, limit, table=False):
    shapes = [jax.ShapeDtypeStruct(s, jnp.bfloat16) for s in outs]
    moved = sum(o.size * o.dtype.itemsize for o in operands) + sum(2 * s.size for s in shapes)
    result = pl.pallas_call(
        kernel,
        out_shape=shapes,
        in_specs=[pl.BlockSpec(memory_space=pltpu.SMEM if table else pltpu.VMEM)] * len(operands),
        out_specs=[pl.BlockSpec(memory_space=pltpu.VMEM)] * len(shapes),
        compiler_params=pltpu.CompilerParams(vmem_limit_bytes=limit * MIB),
        cost_estimate=pl.CostEstimate(flops=flops, bytes_accessed=moved, transcendentals=0),
    )(*operands)
    return result if len(result) > 1 else result[0]


def tied(*values):
    return lax.optimization_barrier(values)


def body(counts, tokens, qkv_first, qkv_second, out_first, out_second, rel_tables, up_weight, down_weight):
    levels, rows, cols, width = tokens.shape
    turn = counts[1] // 2

    def move(value, target):
        return lax.ppermute(value, AXES, pairs(counts, target))

    def core_swap(value):
        return move(value, lambda a, b, m: (a, b, m ^ 1))

    def chip_swap(value):
        return move(value, lambda a, b, m: (a, b, m ^ 2))

    def out_to(value, dy, dx):
        return move(value, lambda a, b, m: (a + dy, b + dx, m ^ 2 if dx and (b + 1) % turn == 0 else m))

    def home(value, dy, dx):
        return move(value, lambda a, b, m: (a - dy, b - dx, m ^ 2 if dx and b % turn == 0 else m))

    half, piece = [(HALF, width)], [(ROWS, width)]
    heads, features = [(KEPT, 256)], [(FEAT, 256)]

    tok = tokens.transpose(1, 2, 0, 3).reshape(rows * cols, levels, width)
    w_first = qkv_first.transpose(1, 0, 2)
    w_second = qkv_second.transpose(1, 0, 2)

    f1 = core_swap(out_first)
    s1 = core_swap(out_second)
    w_sib = core_swap(w_second)
    bias1 = call(functools.partial(bias_kernel, 0), features, (rel_tables,), 5 * 10**9, 4, table=True)
    keep, give = call(first_kernel, heads * 2, (tok, w_first, bias1), 10**9, 16)
    keep, give, f1 = tied(keep, give, f1)
    keep, tok, rel_tables = tied(keep, tok, rel_tables)
    base_a, base_lat, base_own = call(base_kernel, half + piece * 2, (tok,), 10**9, 8)
    bias2 = call(functools.partial(bias_kernel, 1), features, (rel_tables,), 10**9, 4, table=True)
    bias2_sib = core_swap(bias2)
    given, up_late, s1, w_sib, down_late = tied(core_swap(give), up_weight, s1, w_sib, down_weight)
    d1 = core_swap(down_late)
    u1 = core_swap(up_late)
    heads_out = (keep, given, out_first, f1)
    part_a = call(functools.partial(partial_kernel, 0), half, heads_out, 10**8, 8)
    other_a = chip_swap(part_a)
    part_lat, part_own = call(functools.partial(partial_kernel, 1), piece * 2, heads_out, 10**8, 8)
    other_lat = chip_swap(part_lat)
    other_own = chip_swap(part_own)
    other_a, bias2_sib, d1 = tied(other_a, bias2_sib, d1)
    diag, lon = call(residual_kernel, piece * 2, (part_a, other_a, base_a), 10**6, 8)
    diag, lon, part_lat = tied(diag, lon, part_lat)
    lat = call(residual_kernel, piece, (part_lat, other_lat, base_lat), 10**10, 8)
    lat, part_own = tied(lat, part_own)
    own = call(residual_kernel, piece, (part_own, other_own, base_own), 10**6, 8)
    diag = out_to(diag, 1, 1)
    lon = out_to(lon, 0, 1)
    lat = out_to(lat, 1, 0)

    xn_a = call(norm_kernel, half, (diag, lon), 10**10, 8)
    part_a, rest = call(
        second_kernel,
        half + [(HALF, 512)],
        (xn_a, lat, own, w_second, w_sib, out_second, s1, bias2, bias2_sib),
        10**9,
        16,
    )
    other_a = chip_swap(part_a)
    part_b = call(project_kernel, half, (rest, out_second, s1), 10**10, 8)
    other_b = chip_swap(part_b)
    mlp = (up_weight, u1, down_weight, d1)
    part_a = call(mlp_kernel, half, (part_a, other_a, diag, lon, *mlp), 10**9, 20)
    part_a, part_b = tied(part_a, part_b)
    other_a = chip_swap(part_a)
    part_b = call(mlp_kernel, half, (part_b, other_b, lat, own, *mlp), 10**9, 20)
    other_b = chip_swap(part_b)
    diag, lon = call(sum_kernel, piece * 2, (part_a, other_a), 10**6, 8)
    diag, lon, part_b = tied(diag, lon, part_b)
    diag = home(diag, 1, 1)
    lon = home(lon, 0, 1)
    lat, own = call(sum_kernel, piece * 2, (part_b, other_b), 10**10, 8)
    lat = home(lat, 1, 0)
    mine_a = call(join_kernel, half, (diag, lon), 10**10, 8)
    mine_a, lat, own = tied(mine_a, lat, own)
    mine_b = call(join_kernel, half, (lat, own), 10**6, 8)
    operands = (mine_a, mine_b, core_swap(mine_a), core_swap(mine_b))
    result = place_rows((rows * cols, levels, width), operands)
    return result.reshape(rows, cols, levels, width).transpose(2, 0, 1, 3)


def solution(mesh):
    counts = tuple(mesh.shape[name] for name in AXES)
    return jax.shard_map(
        functools.partial(body, counts),
        mesh=mesh,
        in_specs=(
            P(None, "lat", "lon", None),
            P(None, None, "mp"),
            P(None, None, "mp"),
            P("mp", None),
            P("mp", None),
            P(None, "mp", None),
            P(None, "mp"),
            P("mp", None),
        ),
        out_specs=P(None, "lat", "lon", None),
        check_vma=False,
    )
```

```python
import functools

import jax
import jax.numpy as jnp
import numpy as np
from jax import lax
from jax.experimental import pallas as pl
from jax.experimental.pallas import tpu as pltpu
from jax.sharding import PartitionSpec as P

WL = 2
WY = 6
WX = 12
SY = 3
SX = 6
HD = 64
NEG = -1000000000.0
AXES = ("lat", "lon", "mp")
MIB = 1024 * 1024

USED = 36
ROWS = 40
KEPT = 4 * ROWS
HALF = 2 * ROWS
PATCH = 4 * WY * WX
WINDOW = WL * WY * WX
FEAT = 32
F_Y = 4
F_X = 10
F_PAD = 22


def pairs(counts, target):
    lats, lons, mps = counts
    result = []
    for a in range(lats):
        for b in range(lons):
            for m in range(mps):
                ta, tb, tm = target(a, b, m)
                dest = ((ta % lats) * lons + tb % lons) * mps + tm
                result.append(((a * lons + b) * mps + m, dest))
    return result


def dot(left, right):
    return jnp.dot(left, right, preferred_element_type=jnp.float32)


def dot_t(left, right):
    return lax.dot_general(left, right, (((1,), (1,)), ((), ())), preferred_element_type=jnp.float32)


def normalize(floats):
    center = floats - jnp.mean(floats, axis=-1, keepdims=True)
    spread = jnp.mean(center * center, axis=-1, keepdims=True)
    return (center * lax.rsqrt(spread + 1e-05)).astype(jnp.bfloat16)


def core_index():
    return lax.rem(lax.axis_index("mp"), 2)


def iota(shape, axis):
    return lax.broadcasted_iota(jnp.int32, shape, axis)


def one_hot(condition):
    return jnp.where(condition, 1.0, 0.0).astype(jnp.bfloat16)


def piece_place(slot):
    level = (slot * 57) >> 10
    rest = slot - level * 18
    row = (rest * 43) >> 8
    return level, row, rest - row * 6


def kept_place(index):
    quad = (index * 205) >> 13
    slot = index - quad * ROWS
    return (quad, slot) + piece_place(slot)


def real_level(level, core):
    return jnp.where(core == 0, 1 + level, 3 - 3 * level)


def patch_place(q, row, col):
    return row + 3 - 3 * (q & 1), col + 6 - 3 * (q & 2)


def bias_rows(table, block, pair):
    shape = (FEAT, 4 * FEAT)
    i, lane = iota(shape, 0), iota(shape, 1)
    j = lane & (FEAT - 1)
    kind = jnp.full(shape, 37, jnp.int32)
    kind = jnp.where((i < WL) & (j < WL), i - j + 1, kind)
    kind = jnp.where((i < WL) & (j == F_PAD), 38, kind)
    in_y = (i >= F_Y) & (i < F_Y + WY) & (j >= F_Y) & (j < F_Y + WY)
    kind = jnp.where(in_y, 3 + i - j + 5, kind)
    in_x = (i >= F_X) & (i < F_X + WX) & (j >= F_X) & (j < F_X + WX)
    kind = jnp.where(in_x, 14 + i - j + 11, kind)
    total = jnp.where(kind == 38, NEG, 0.0)
    for k in range(37):
        value = jnp.where(lane < HD, table[block, 2 * pair + 1, k], table[block, 2 * pair, k])
        total = jnp.where(kind == k, value, total)
    high = total.astype(jnp.bfloat16).astype(jnp.float32)
    return jnp.where((lane & FEAT) != 0, total - high, high).astype(jnp.bfloat16)


def bias_kernel(block, table, out):
    for pair in range(2):
        out[:, pair * 128 : pair * 128 + 128] = bias_rows(table, block, pair)


def features(level, row, col, used, count):
    j = iota((count, 128), 1) & (FEAT - 1)
    hit = (j == level) | (j == F_Y + row) | (j == F_X + col)
    return one_hot(jnp.where(used, jnp.where(hit, 1, 0), jnp.where(j == F_PAD, 1, 0)) == 1)


def attend(parts, key_feat):
    low = iota(parts[0][0].shape, 1) < HD
    none = jnp.zeros_like(parts[0][0])
    count = none.shape[0]
    scores = []
    for query, key, _, extra in parts:
        upper = jnp.concatenate([jnp.where(low, query, none), jnp.where(low, none, extra)], axis=1)
        lower = jnp.concatenate([jnp.where(low, none, query), jnp.where(low, extra, none)], axis=1)
        both = jnp.concatenate([upper, lower], axis=0)
        scores.append(dot_t(both, jnp.concatenate([key, key_feat], axis=1)))
    expos, scales = [], []
    for score in scores:
        expo = jnp.exp(score - jnp.max(score, axis=-1, keepdims=True))
        expos.append(expo.astype(jnp.bfloat16))
        scales.append(1.0 / jnp.sum(expo, axis=-1, keepdims=True))
    results = []
    for (_, _, value, _), expo, scale in zip(parts, expos, scales):
        mixed = dot(expo, value) * scale
        results.append(jnp.where(low, mixed[:count], mixed[count:]).astype(jnp.bfloat16))
    return results


def pair_cols(pair):
    return slice(pair * 128, pair * 128 + 128)


def first_kernel(tokens, weight, bias, keep, give):
    core = core_index()
    floats = tokens[...].astype(jnp.float32).reshape(PATCH, -1)
    xn = normalize(floats)
    q = (dot(xn, weight[0]) * HD**-0.5).astype(jnp.bfloat16)
    k = dot(xn, weight[1]).astype(jnp.bfloat16)
    v = dot(xn, weight[2]).astype(jnp.bfloat16)
    index = iota((PATCH, 1), 0)
    level = (index * 911) >> 16
    order = one_hot(iota((PATCH, PATCH), 1) == (index - 72 * level) * 4 + level)
    q, k, v = (dot(order, part).astype(jnp.bfloat16) for part in (q, k, v))
    index = iota((WINDOW, 1), 0)
    level = (index * 911) >> 16
    rest = index - 72 * level
    row = (rest * 171) >> 11
    feat = features(level, row, rest - 12 * row, index >= 0, WINDOW)
    extra = dot(feat[:, :FEAT], bias[...]).astype(jnp.bfloat16)
    parts = []
    for w in range(2):
        rows = slice(w * WINDOW, (w + 1) * WINDOW)
        for pair in range(2):
            cols = pair_cols(pair)
            parts.append((q[rows, cols], k[rows, cols], v[rows, cols], extra[:, cols]))
    heads = attend(parts, feat)
    windows = [jnp.concatenate(heads[2 * w : 2 * w + 2], axis=1) for w in range(2)]
    mixed = jnp.concatenate(windows, axis=0)
    quad, slot, level, row, col = kept_place(iota((KEPT, 1), 0))
    row, col = patch_place(quad, row, col)
    lanes = iota((KEPT, PATCH), 1)
    for out, chosen in ((keep, core), (give, 1 - core)):
        place = real_level(level, chosen) * 72 + row * 12 + col
        place = jnp.where(slot < USED, place, -1)
        out[...] = dot(one_hot(lanes == place), mixed).astype(jnp.bfloat16)


def base_kernel(tokens, *outs):
    values = tokens[...].astype(jnp.float32).reshape(PATCH, -1).astype(jnp.bfloat16)
    quad, slot, level, row, col = kept_place(iota((KEPT, 1), 0))
    row, col = patch_place(quad, row, col)
    place = (row * 12 + col) * 4 + real_level(level, core_index())
    place = jnp.where(slot < USED, place, -1)
    store_three(dot(one_hot(iota((KEPT, PATCH), 1) == place), values), outs)


def store_halves(total, outs):
    for h in range(2):
        outs[h][...] = total[h * HALF : (h + 1) * HALF].astype(jnp.bfloat16)


def store_three(total, outs):
    for out, start, stop in zip(outs, (0, 2 * ROWS, 3 * ROWS), (2 * ROWS, 3 * ROWS, KEPT)):
        out[...] = total[start:stop].astype(jnp.bfloat16)


def partial_kernel(half, o0, o1, w0, w1, *outs):
    rows = slice(half * HALF, (half + 1) * HALF)
    total = dot(o0[rows], w0[...]) + dot(o1[rows], w1[...])
    count = HALF // len(outs)
    for p, out in enumerate(outs):
        out[...] = total[p * count : (p + 1) * count].astype(jnp.bfloat16)


def branch_sum(mine, other):
    total = mine[...].astype(jnp.float32) + other[...].astype(jnp.float32)
    return total.astype(jnp.bfloat16).astype(jnp.float32)


def residual_kernel(mine, other, base, *outs):
    first = base[...].astype(jnp.float32) + branch_sum(mine, other)
    for p, out in enumerate(outs):
        out[...] = first[p * ROWS : (p + 1) * ROWS].astype(jnp.bfloat16)


def joined(pieces):
    return jnp.concatenate([p[...].astype(jnp.float32) for p in pieces], axis=0)


def norm_kernel(p0, p1, out):
    out[...] = normalize(joined((p0, p1)))


def second_kernel(xn_a, p2, p3, w_own, w_sib, o_own, o_sib, b_own, b_sib, *outs):
    xn_b = normalize(joined((p2, p3))).astype(jnp.float32)
    xn = jnp.concatenate([xn_a[...].astype(jnp.float32), xn_b], axis=0).astype(jnp.bfloat16)
    quad, slot, level, row, col = kept_place(iota((KEPT, 1), 0))
    row, col = row + 3 * (quad & 1), col + 3 * (quad & 2)
    feat = features(level, row, col, slot < USED, KEPT)
    lane = iota((KEPT, 128), 1)
    j = lane & (FEAT - 1)
    split_levels = core_index() == 1
    split_rows = lax.axis_index("lat") == 0
    ban_level = (j < WL) & (j != level)
    ban_row = (j >= F_Y) & (j < F_Y + WY) & ((j >= F_Y + SY) != (row >= SY))
    ban = jnp.where(ban_level, split_levels.astype(jnp.int32), jnp.where(ban_row, split_rows.astype(jnp.int32), 0))
    ban = jnp.where((lane & FEAT) == 0, ban, 0) == 1
    parts = []
    for weight, bias in ((w_own, b_own), (w_sib, b_sib)):
        q = (dot(xn, weight[0]) * HD**-0.5).astype(jnp.bfloat16)
        k = dot(xn, weight[1]).astype(jnp.bfloat16)
        v = dot(xn, weight[2]).astype(jnp.bfloat16)
        extra = dot(feat[:, :FEAT], bias[...])
        for pair in range(2):
            cols = pair_cols(pair)
            parts.append((q[:, cols], k[:, cols], v[:, cols], jnp.where(ban, NEG, extra[:, cols]).astype(jnp.bfloat16)))
    heads = attend(parts, feat)
    mixed = jnp.concatenate(heads, axis=1)
    project_kernel(mixed[:HALF], o_own, o_sib, outs[0])
    outs[1][...] = mixed[HALF:]


def project_kernel(mixed, o_own, o_sib, out):
    total = dot(mixed[:, :256], o_own[...]) + dot(mixed[:, 256:], o_sib[...])
    out[...] = total.astype(jnp.bfloat16)


def gelu(x):
    return 0.5 * x * (1.0 + lax.erf(x * np.float32(np.sqrt(0.5))))


def mlp_kernel(mine, other, p0, p1, u0, u1, d0, d1, out):
    second = joined((p0, p1)) + branch_sum(mine, other)
    second = second.astype(jnp.bfloat16).astype(jnp.float32)
    xn = normalize(second)
    h0 = gelu(dot(xn, u0[...])).astype(jnp.bfloat16)
    h1 = gelu(dot(xn, u1[...])).astype(jnp.bfloat16)
    out[...] = (0.5 * second + dot(h0, d0[...]) + dot(h1, d1[...])).astype(jnp.bfloat16)


def sum_kernel(mine, other, *outs):
    total = mine[...].astype(jnp.float32) + other[...].astype(jnp.float32)
    for p in range(2):
        outs[p][...] = total[p * ROWS : (p + 1) * ROWS].astype(jnp.bfloat16)


def join_kernel(second, first, out):
    out[...] = joined((first, second)).astype(jnp.bfloat16)


def place_kernel(m0, m1, s0, s1, out, held, sems):
    core = core_index()
    quad, slot, level, row, col = kept_place(iota((1, KEPT), 1))
    row, col = patch_place(quad, row, col)
    places, sources = [], []
    for chosen, parts in ((core, (m0, m1)), (1 - core, (s0, s1))):
        place = (row * 12 + col) * 4 + real_level(level, chosen)
        places.append(jnp.where(slot < USED, place, -1))
        sources.append(jnp.concatenate([part[...] for part in parts], axis=0))
    count = PATCH // 2
    copies = []
    for h in range(2):
        index = iota((count, KEPT), 0) + h * count
        total = dot(one_hot(index == places[0]), sources[0]) + dot(one_hot(index == places[1]), sources[1])
        rows = pl.ds(h * count // 4, count // 4)
        held[rows] = total.reshape(count // 4, 4, -1).astype(jnp.bfloat16)
        copies.append(pltpu.make_async_copy(held.at[rows], out.at[rows], sems.at[h]))
        copies[h].start()
    for copy in copies:
        copy.wait()


def place_rows(shape, operands):
    return pl.pallas_call(
        place_kernel,
        out_shape=jax.ShapeDtypeStruct(shape, jnp.bfloat16),
        in_specs=[pl.BlockSpec(memory_space=pltpu.VMEM)] * 4,
        out_specs=pl.BlockSpec(memory_space=pl.ANY),
        scratch_shapes=[pltpu.VMEM(shape, jnp.bfloat16), pltpu.SemaphoreType.DMA((2,))],
        compiler_params=pltpu.CompilerParams(vmem_limit_bytes=12 * MIB),
        cost_estimate=pl.CostEstimate(flops=2 * 10**8, bytes_accessed=2 * 10**6, transcendentals=0),
    )(*operands)


def call(kernel, outs, operands, flops, limit, table=False):
    shapes = [jax.ShapeDtypeStruct(s, jnp.bfloat16) for s in outs]
    moved = sum(o.size * o.dtype.itemsize for o in operands) + sum(2 * s.size for s in shapes)
    result = pl.pallas_call(
        kernel,
        out_shape=shapes,
        in_specs=[pl.BlockSpec(memory_space=pltpu.SMEM if table else pltpu.VMEM)] * len(operands),
        out_specs=[pl.BlockSpec(memory_space=pltpu.VMEM)] * len(shapes),
        compiler_params=pltpu.CompilerParams(vmem_limit_bytes=limit * MIB),
        cost_estimate=pl.CostEstimate(flops=flops, bytes_accessed=moved, transcendentals=0),
    )(*operands)
    return result if len(result) > 1 else result[0]


def tied(*values):
    return lax.optimization_barrier(values)


def body(counts, tokens, qkv_first, qkv_second, out_first, out_second, rel_tables, up_weight, down_weight):
    levels, rows, cols, width = tokens.shape
    turn = counts[1] // 2

    def move(value, target):
        return lax.ppermute(value, AXES, pairs(counts, target))

    def core_swap(value):
        return move(value, lambda a, b, m: (a, b, m ^ 1))

    def chip_swap(value):
        return move(value, lambda a, b, m: (a, b, m ^ 2))

    def out_to(value, dy, dx):
        return move(value, lambda a, b, m: (a + dy, b + dx, m ^ 2 if dx and (b + 1) % turn == 0 else m))

    def home(value, dy, dx):
        return move(value, lambda a, b, m: (a - dy, b - dx, m ^ 2 if dx and b % turn == 0 else m))

    half, piece = [(HALF, width)], [(ROWS, width)]
    heads, features = [(KEPT, 256)], [(FEAT, 256)]

    tok = tokens.transpose(1, 2, 0, 3).reshape(rows * cols, levels, width)
    w_first = qkv_first.transpose(1, 0, 2)
    w_second = qkv_second.transpose(1, 0, 2)

    f1 = core_swap(out_first)
    s1 = core_swap(out_second)
    w_sib = core_swap(w_second)
    bias1 = call(functools.partial(bias_kernel, 0), features, (rel_tables,), 5 * 10**9, 4, table=True)
    keep, give = call(first_kernel, heads * 2, (tok, w_first, bias1), 10**9, 16)
    keep, give, f1 = tied(keep, give, f1)
    keep, tok, rel_tables = tied(keep, tok, rel_tables)
    base_a, base_lat, base_own = call(base_kernel, half + piece * 2, (tok,), 10**9, 8)
    bias2 = call(functools.partial(bias_kernel, 1), features, (rel_tables,), 10**9, 4, table=True)
    bias2_sib = core_swap(bias2)
    given, up_late, s1, w_sib, down_late = tied(core_swap(give), up_weight, s1, w_sib, down_weight)
    d1 = core_swap(down_late)
    u1 = core_swap(up_late)
    heads_out = (keep, given, out_first, f1)
    part_a = call(functools.partial(partial_kernel, 0), half, heads_out, 10**8, 8)
    other_a = chip_swap(part_a)
    part_lat, part_own = call(functools.partial(partial_kernel, 1), piece * 2, heads_out, 10**8, 8)
    other_lat = chip_swap(part_lat)
    other_own = chip_swap(part_own)
    other_a, bias2_sib, d1 = tied(other_a, bias2_sib, d1)
    diag, lon = call(residual_kernel, piece * 2, (part_a, other_a, base_a), 10**6, 8)
    diag, lon, part_lat = tied(diag, lon, part_lat)
    lat = call(residual_kernel, piece, (part_lat, other_lat, base_lat), 10**10, 8)
    lat, part_own = tied(lat, part_own)
    own = call(residual_kernel, piece, (part_own, other_own, base_own), 10**6, 8)
    diag = out_to(diag, 1, 1)
    lon = out_to(lon, 0, 1)
    lat = out_to(lat, 1, 0)

    xn_a = call(norm_kernel, half, (diag, lon), 10**10, 8)
    part_a, rest = call(
        second_kernel,
        half + [(HALF, 512)],
        (xn_a, lat, own, w_second, w_sib, out_second, s1, bias2, bias2_sib),
        10**9,
        16,
    )
    other_a = chip_swap(part_a)
    part_b = call(project_kernel, half, (rest, out_second, s1), 10**10, 8)
    other_b = chip_swap(part_b)
    mlp = (up_weight, u1, down_weight, d1)
    part_a = call(mlp_kernel, half, (part_a, other_a, diag, lon, *mlp), 10**9, 20)
    part_a, part_b = tied(part_a, part_b)
    other_a = chip_swap(part_a)
    part_b = call(mlp_kernel, half, (part_b, other_b, lat, own, *mlp), 10**9, 20)
    other_b = chip_swap(part_b)
    diag, lon = call(sum_kernel, piece * 2, (part_a, other_a), 10**6, 8)
    diag, lon, part_b = tied(diag, lon, part_b)
    diag = home(diag, 1, 1)
    lon = home(lon, 0, 1)
    lat, own = call(sum_kernel, piece * 2, (part_b, other_b), 10**10, 8)
    lat = home(lat, 1, 0)
    mine_a = call(join_kernel, half, (lon, diag), 10**10, 8)
    mine_a, lat, own = tied(mine_a, lat, own)
    mine_b = call(join_kernel, half, (own, lat), 10**6, 8)
    operands = (mine_a, mine_b, core_swap(mine_a), core_swap(mine_b))
    result = place_rows((rows * cols, levels, width), operands)
    return result.reshape(rows, cols, levels, width).transpose(2, 0, 1, 3)


def solution(mesh):
    counts = tuple(mesh.shape[name] for name in AXES)
    return jax.shard_map(
        functools.partial(body, counts),
        mesh=mesh,
        in_specs=(
            P(None, "lat", "lon", None),
            P(None, None, "mp"),
            P(None, None, "mp"),
            P("mp", None),
            P("mp", None),
            P(None, "mp", None),
            P(None, "mp"),
            P("mp", None),
        ),
        out_specs=P(None, "lat", "lon", None),
        check_vma=False,
    )
```
